512 devices in a mesh: occ: 16 (over z), aux: 8 (over x, core), pair: 4 (over y).
Axes of the slice: x: 4, y: 4, z: 16, core: 2. Of those that a mesh axis runs over, the one named last changes fastest.
Arguments:
- amp_fit: bfloat16 [256, 288, 288], P('aux', None, 'occ'), may hold values from -6 to 6
- amp_cabs: bfloat16 [96, 288, 288], P('aux', None, 'occ'), may hold values from -6 to 6
- coef: bfloat16 [288, 3072], P('occ'), may hold values from -0.375 to 0.375
- f12_weight: float32 [288], P('occ'), may hold values from 0.3 to 3
- ints_fit: bfloat16 [256, 288, 3072], P('aux', 'occ'), may hold values from -0.01953125 to 0.01953125
- ints_cabs: bfloat16 [96, 288, 3072], P('aux', 'occ'), may hold values from -0.01953125 to 0.01953125
- shell_len: int32 [24], replicated, may hold values from 1 to 128, 2400 in all
- pair_blocks: int32 [160, 2], P('pair'), may hold values from 0 to 23
- pair_count: int32 [4], P('pair'), may hold values from 1 to 40, as said below
Outputs:
- pair_density: float32 [160, 128, 128], P('pair', 'occ')
The draws below stay inside these ranges and needn't reach their ends.
Inputs may be any that keep to these rules, and one draw needn't show every extreme that they name: `pair_count`: some owner has exactly 40 live slots in every draw.
All inputs are finite; a program needn't handle non-finite values.
Results may differ from the reference program's by a relative error of at most 0.0029.
Values may be sent and summed in bfloat16 or wider, within the bound.
No kernel may reach another device: no remote copies, remote signals or barrier semaphores. Data moves between devices by JAX's collectives and lax.ppermute only.
A program may use at most 64 MiB of HBM per device.

```python
import math
import jax
import jax.numpy as jnp
import numpy as np
from jax import lax

OCC = 288
NAO = 2400
BS = 128
NBLK = 24
NPAD = 3072
SLOTS = 40
FIT = 256
CABS = 96
PAIRS = 160
N_PAIR = 4


def draw_pair_count(key, part):
    key = jax.random.fold_in(key, 7)
    counts = jax.random.randint(key, (N_PAIR,), 1, SLOTS + 1)
    chosen = jax.random.randint(jax.random.fold_in(key, 11), (), 0, N_PAIR)
    return jnp.where(jnp.arange(N_PAIR) == chosen, SLOTS, counts).astype(jnp.int32)


def with_ends(values, own_key, smallest, top_value):
    longest = values.shape.index(max(values.shape))
    spots = []
    for shift in (0, 1):
        where = [jax.random.randint(jax.random.fold_in(own_key, axis), (), 0, length) for axis, length in enumerate(values.shape)]
        where[longest] = (where[longest] + shift) % values.shape[longest]
        spots.append(tuple(where))
    return values.at[spots[0]].set(smallest).at[spots[1]].set(top_value)


def block_scale(own_key, extent, pieces, least, top_value):
    gain, own = 1.0, jax.random.fold_in(own_key, 6)
    for dim, shards_of in pieces:
        draws = jnp.exp(jax.random.uniform(jax.random.fold_in(own, dim), (shards_of,), jnp.float32, least / len(pieces), top_value / len(pieces)))
        gain = gain * jnp.repeat(draws, extent[dim] // shards_of).reshape([-1 if axis == dim else 1 for axis in range(len(extent))])
    return gain


def split_up(count, total, reach, slope):
    weights = [(1 << 20) // math.isqrt(standing ** slope) + 1 for standing in range(2, count + 1)]
    rest, given = total - reach - (count - 1), [1] * (count - 1)
    while rest > 0:
        candidates = [i for i in range(count - 1) if given[i] < reach]
        mass, remaining = sum([weights[i] for i in candidates]), rest
        for i in candidates:
            more = min(reach - given[i], max(1, remaining * weights[i] // mass), rest)
            given[i] = given[i] + more
            rest = rest - more
    return np.array([reach] + given)


def ragged(stream_key, count, total, reach, lean):
    if count == 2:
        one = jax.random.randint(stream_key, (), max(1, total - reach), min(reach, total - 1) + 1)
        return jnp.stack([one, total - one])
    tallies = jnp.asarray(split_up(count, total, reach, lean), jnp.int32)
    twos = (count - 1) // 2
    donor, receiver = tallies[1:1 + 2 * twos:2], tallies[2:2 + 2 * twos:2]
    slack = jnp.minimum(donor - 1, reach - receiver)
    moved = jax.random.randint(jax.random.fold_in(stream_key, 1), (twos,), 0, 1 << 20) % (slack + 1)
    tallies = tallies.at[1:1 + 2 * twos:2].set(donor - moved).at[2:2 + 2 * twos:2].set(receiver + moved)
    return tallies[jax.random.permutation(jax.random.fold_in(stream_key, 2), count)]


def bell_draw(stream_key, extent, spread, bound, shards=(), kind=jnp.bfloat16):
    gain = block_scale(stream_key, extent, shards, -0.22, 0.18) if shards else 1.0
    array = jax.random.normal(stream_key, extent, jnp.float32) * spread * gain
    return jnp.minimum(jnp.maximum(array, -bound), bound).astype(kind)


def setup_inputs(seed: int = 0) -> dict:
    streams_of = jax.random.split(jax.random.key(seed), 10)
    amp_fit = bell_draw(streams_of[0], (FIT, OCC, OCC), 1.0, 6.0, ((0, 8), (2, 16)))
    amp_cabs = bell_draw(streams_of[1], (CABS, OCC, OCC), 1.0, 6.0, ((0, 8), (2, 16)))
    coef = bell_draw(streams_of[2], (OCC, NPAD), OCC ** -0.5, 0.375, ((0, 16),))
    f12_weight = jnp.clip(jnp.exp(math.log(3.0) - 2.3025851 * jax.random.uniform(streams_of[3], (OCC,), jnp.float32) ** block_scale(streams_of[3], (OCC,), ((0, 16),), -0.2, 0.2)), 0.3, 3.0)
    ints_fit = bell_draw(streams_of[4], (FIT, OCC, NPAD), ((FIT + CABS) * OCC) ** -0.5, 0.01953125, ((0, 8), (1, 16)))
    ints_cabs = bell_draw(streams_of[5], (CABS, OCC, NPAD), ((FIT + CABS) * OCC) ** -0.5, 0.01953125, ((0, 8), (1, 16)))
    shell_len = ragged(streams_of[6], NBLK, NAO, BS, 1).astype(jnp.int32)
    pair_blocks = with_ends(jax.random.randint(streams_of[7], (PAIRS, 2), 0, NBLK), jax.random.fold_in(streams_of[7], 1), 0, NBLK - 1).astype(jnp.int32)
    pair_count = draw_pair_count(jax.random.fold_in(streams_of[9], 71), 0)
    return {"amp_fit": amp_fit, "amp_cabs": amp_cabs, "coef": coef, "f12_weight": f12_weight, "ints_fit": ints_fit, "ints_cabs": ints_cabs, "shell_len": shell_len, "pair_blocks": pair_blocks, "pair_count": pair_count}


def valid_mask(shell_len):
    inside = jnp.arange(BS, dtype=jnp.int32)[None, :] < shell_len[:, None]
    return inside.astype(jnp.float32)


def reference(amp_fit, amp_cabs, coef, f12_weight, ints_fit, ints_cabs, shell_len, pair_blocks, pair_count):
    valid_blk = valid_mask(shell_len)
    valid = valid_blk.reshape(NPAD)
    coef_m = jnp.where(valid[None, :] > 0, coef, jnp.zeros_like(coef))
    half_fit = jnp.dot(amp_fit.reshape(FIT * OCC, OCC), coef_m, preferred_element_type=jnp.float32).astype(jnp.bfloat16)
    cabs_raw = jnp.dot(amp_cabs.reshape(CABS * OCC, OCC), coef_m, preferred_element_type=jnp.float32)
    half_cabs = (cabs_raw.reshape(CABS, OCC, NPAD) * f12_weight[None, :, None]).reshape(CABS * OCC, NPAD).astype(jnp.bfloat16)
    right_fit = ints_fit.reshape(FIT * OCC, NPAD)
    right_cabs = ints_cabs.reshape(CABS * OCC, NPAD)
    live_all = (jnp.arange(SLOTS, dtype=jnp.int32)[None, :] < pair_count[:, None]).reshape(PAIRS).astype(jnp.float32)

    def one_slot(slot_id):
        row_blk = pair_blocks[slot_id, 0]
        col_blk = pair_blocks[slot_id, 1]
        row_off = (row_blk * BS).astype(jnp.int32)
        col_off = (col_blk * BS).astype(jnp.int32)
        left_fit = lax.dynamic_slice_in_dim(half_fit, row_off, BS, 1)
        left_cabs = lax.dynamic_slice_in_dim(half_cabs, row_off, BS, 1)
        rgt_fit = lax.dynamic_slice_in_dim(right_fit, col_off, BS, 1)
        rgt_cabs = lax.dynamic_slice_in_dim(right_cabs, col_off, BS, 1)
        block = jnp.dot(left_fit.T, rgt_fit, preferred_element_type=jnp.float32)
        block = block + jnp.dot(left_cabs.T, rgt_cabs, preferred_element_type=jnp.float32)
        row_mask = valid_blk[row_blk]
        col_mask = valid_blk[col_blk]
        return block * row_mask[:, None] * col_mask[None, :] * live_all[slot_id]

    return lax.map(one_slot, jnp.arange(PAIRS, dtype=jnp.int32))
```

```python
import functools
import math

import jax
import jax.numpy as jnp
from jax import lax
from jax.experimental import pallas as pl
from jax.experimental.pallas import tpu as pltpu
from jax.sharding import PartitionSpec as P

F32, BF16, F16 = jnp.float32, jnp.bfloat16, jnp.float16
LANES = 128
LN2 = math.log(2.0)
NT = (((1,), (1,)), ((), ()))
TN = (((0,), (0,)), ((), ()))


def iota(shape, dim):
    return lax.broadcasted_iota(jnp.int32, shape, dim)


def dot(a, b, dims=(((1,), (0,)), ((), ()))):
    return lax.dot_general(a, b, dims, preferred_element_type=F32)


def one_hot(cond):
    return jnp.where(cond, 1.0, 0.0).astype(BF16)


def swap_pieces(xs, piece):
    lane = iota(xs[0].shape, 1)
    bit = 1
    while bit < len(xs):
        keep = ((lane // piece) & bit) == 0
        ys = list(xs)
        for k in range(len(xs)):
            if k & bit == 0:
                lo, hi = xs[k], xs[k + bit]
                ys[k] = jnp.where(keep, lo, pltpu.roll(hi, piece * bit, 1))
                ys[k + bit] = jnp.where(keep, pltpu.roll(lo, LANES - piece * bit, 1), hi)
        xs = ys
        bit *= 2
    return xs


def vmem(n):
    return [pl.BlockSpec(memory_space=pltpu.VMEM)] * n


SMEM = pl.BlockSpec(memory_space=pltpu.SMEM)
PARAMS = pltpu.CompilerParams(vmem_limit_bytes=40 * 1024 * 1024)


NO, NI, NA, NP, NF, NC, NJ = 16, 18, 8, 4, 32, 12, 5
ROWS = 40
CQ = 16
TJ = NO * NJ


def pack_amps(info, fit, cabs, coef, out, cab32, x, msg):
    first_j = info[3]
    x[0 : NJ * NF, :] = fit[pl.ds(first_j, NJ)].reshape(NJ * NF, NO * NI)
    for q in range(NC):
        cab32[24 * q : 24 * q + NI, :] = cabs[q].astype(F32)
    zero = jnp.zeros((CQ - NC, NO * NI), F32)
    for jj in range(NJ):
        picked = [cab32[pl.ds(24 * q + first_j + jj, 1), :] for q in range(NC)]
        rows = jnp.concatenate(picked + [zero], axis=0)
        x[NJ * NF + CQ * jj : NJ * NF + CQ * (jj + 1), :] = rows.astype(BF16)
    x[NJ * (NF + CQ) :, :] = jnp.zeros((256 - NJ * (NF + CQ), NO * NI), BF16)
    shape = (NO, ROWS, NO * NI)
    t = iota(shape, 1)
    place = jnp.where((iota(shape, 2) == NI * iota(shape, 0) + t) & (t < NI), 1.0, 0.0)
    place = place.reshape(NO * ROWS, NO * NI).astype(BF16)
    msg[...] = dot(place, x[...], NT).reshape(NO, ROWS, 256)
    tiles = [coef[:, LANES * a : LANES * (a + 1)].astype(F32) for a in range(24)]
    none = jnp.zeros_like(tiles[0])
    left = swap_pieces(tiles[:16], 8)
    right = swap_pieces(tiles[16:] + [none] * 8, 8)
    for o in range(NO):
        msg[o, NI : 2 * NI, 0:LANES] = left[o]
        msg[o, NI : 2 * NI, LANES : 2 * LANES] = right[o]
    out[...] = msg[...].astype(BF16)


def partial_t(got, weight, fit, cabs, out, a_fit, a_cab, padded):
    @pl.when(pl.program_id(0) == 0)
    def _():
        shape = (NI, NO, NO * ROWS)
        pick = jnp.where(iota(shape, 2) == ROWS * iota(shape, 1) + iota(shape, 0), 1.0, 0.0)
        pick = pick.reshape(NI * NO, NO * ROWS).astype(BF16)
        amps = dot(pick, got[...].reshape(NO * ROWS, 256))
        amps = [[amps[NO * t : NO * (t + 1), LANES * h : LANES * (h + 1)] for h in (0, 1)] for t in range(NI)]
        lane = iota((NO, LANES), 1)

        def lay(ref_rows, width, start, store):
            per = LANES // width
            for jj in range(NJ):
                half, off = divmod(start + width * jj, LANES)
                for m in range(-(-NI // per)):
                    tile = jnp.zeros((NO, LANES), F32)
                    for k in range(min(per, NI - m * per)):
                        moved = amps[m * per + k][half]
                        if (width * k - off) % LANES:
                            moved = pltpu.roll(moved, (width * k - off) % LANES, 1)
                        tile = jnp.where((lane >= width * k) & (lane < width * (k + 1)), moved, tile)
                    store[NO * jj : NO * (jj + 1), LANES * m : LANES * (m + 1)] = tile.astype(BF16)

        lay(NO, NF, 0, a_fit)
        lay(NO, CQ, NJ * NF, a_cab)
        shape = (3 * LANES, 32 * NC)
        source = iota(shape, 0)
        target = iota(shape, 1)
        order = one_hot(((target >> 5) == (source & 15)) & ((target & 31) == (source >> 4)))
        weighted = dot(a_cab[...], order) * weight[...]
        a_cab[...] = weighted.astype(BF16)
        padded[...] = jnp.zeros(padded.shape, BF16)

    for q in range(NC):
        padded[32 * q : 32 * q + NI, :] = cabs[q]
    total = dot(a_fit[:, : NI * NF], fit[...].reshape(NI * NF, 1024)) + dot(a_cab[...], padded[...])
    pieces = swap_pieces([total[:, LANES * k : LANES * (k + 1)] for k in range(8)], 16)
    for k in range(8):
        out[k] = pieces[k].astype(BF16)


def sum_aux(got, out, total):
    total[...] = jnp.sum(got[...].astype(F32), axis=0)
    for o in range(NO):
        out[o, 0:15, :] = total[15 * o : 15 * o + 15, :]
        out[o, 15:16, :] = jnp.zeros((1, LANES), F32)


def sum_occ(got, out):
    total = jnp.sum(got[...], axis=0)
    top = jnp.max(jnp.max(jnp.abs(total), axis=1, keepdims=True), axis=0, keepdims=True)
    power = jnp.ceil(jnp.log(jnp.maximum(top, 1e-30)) * (1.0 / LN2))
    scaled = total * (jnp.exp(power * -LN2) * 16384.0)
    out[...] = jnp.where(iota(total.shape, 0) == 15, power, scaled)


def pair_blocks_kernel(info, got, amps, out, tsum, tmat, dmat):
    occ, aux, count = info[0], info[1], info[4]
    values = got[...]
    values = values * (jnp.exp(values[:, 15:16, :] * LN2) * (1.0 / 16384.0))
    for y in range(NP):
        for o in range(NO):
            tsum[y, 15 * o : 15 * o + 15, :] = values[NO * y + o, 0:15, :]
    for y in range(NP):
        for g in range(3):
            tmat[TJ * y : TJ * (y + 1), LANES * g : LANES * (g + 1)] = tsum[y, TJ * g : TJ * (g + 1), :]
    shape = (NP, NJ, NO, NO * ROWS)
    y, jj = iota(shape, 0), iota(shape, 1)
    first_j = jnp.minimum(NJ * y, NI - NJ)
    row = ROWS * iota(shape, 2) + NI + first_j + jj
    pick = (iota(shape, 3) == row) & (first_j + jj >= NJ * y)
    pick = jnp.where(pick, 1.0, 0.0).reshape(NP * TJ, NO * ROWS).astype(BF16)
    coef = dot(pick, amps[...].reshape(NO * ROWS, 256)).astype(BF16)
    high = tmat[...].astype(BF16)
    low = (tmat[...] - high.astype(F32)).astype(BF16)
    blocks = dot(coef, high, TN) + dot(coef, low, TN)
    for g in range(3):
        dmat[g] = blocks[:, LANES * g : LANES * (g + 1)]
    lane, row = iota((8, LANES), 1), iota((8, LANES), 0)
    for q in range(5):
        tile = jnp.zeros((8, LANES), F32)
        for k in range(8):
            slot = 8 * q + k
            a, b = info[32 + 2 * slot], info[33 + 2 * slot]
            block = dmat[b >> 3, pl.ds(pl.multiple_of(8 * a, 8), 8), :]
            block = pltpu.roll(block, (16 * (k + 8 - (b & 7))) & 127, 1)
            rows_kept = jnp.where(slot < count, info[8 + a] - 8 * occ, 0)
            lanes_kept = jnp.clip(info[8 + b] - 16 * aux, 0, 16) + 16 * k
            tile = jnp.where((lane >= 16 * k) & (lane < lanes_kept) & (row < rows_kept), block, tile)
        for p in range(NA):
            out[p, 8 * q : 8 * (q + 1), :] = tile


def unpack(got, out):
    for q in range(5):
        blocks = swap_pieces([got[p, 8 * q : 8 * (q + 1), :] for p in range(NA)], 16)
        for k in range(8):
            out[8 * q + k] = blocks[k]


def exchange(x, axes):
    return lax.all_to_all(x, axes, split_axis=0, concat_axis=0, tiled=True)


def shape_of(shape, dtype):
    return jax.ShapeDtypeStruct(shape, dtype)


def on_device(amp_fit, amp_cabs, coef, f12_weight, ints_fit, ints_cabs, shell_len, pair_blocks, pair_count):
    occ, aux, pair = (lax.axis_index(a).astype(jnp.int32) for a in ("occ", "aux", "pair"))
    first_j = jnp.minimum(NJ * pair, NI - NJ)
    info = jnp.concatenate(
        [
            jnp.stack([occ, aux, pair, first_j, pair_count[0], occ, occ, occ]),
            shell_len,
            pair_blocks.reshape(-1),
        ]
    )
    weight = jnp.tile(jnp.pad(f12_weight, (0, 32 - NI)), NC)[None, :]

    sent = pl.pallas_call(
        pack_amps,
        out_shape=shape_of((NO, ROWS, 256), BF16),
        in_specs=[SMEM] + vmem(3),
        out_specs=vmem(1)[0],
        scratch_shapes=[
            pltpu.VMEM((24 * NC, NO * NI), F32),
            pltpu.VMEM((256, NO * NI), BF16),
            pltpu.VMEM((NO, ROWS, 256), F32),
        ],
        compiler_params=PARAMS,
    )(info, jnp.transpose(amp_fit, (2, 0, 1)), jnp.transpose(amp_cabs, (0, 2, 1)), coef)
    amps = exchange(sent, "occ")

    sent = pl.pallas_call(
        partial_t,
        grid=(3,),
        out_shape=shape_of((NA, 3 * TJ, LANES), BF16),
        in_specs=[
            pl.BlockSpec((NO, ROWS, 256), lambda g: (0, 0, 0)),
            pl.BlockSpec((1, 32 * NC), lambda g: (0, 0)),
            pl.BlockSpec((NI, NF, 1024), lambda g: (0, 0, g)),
            pl.BlockSpec((NC, NI, 1024), lambda g: (0, 0, g)),
        ],
        out_specs=pl.BlockSpec((NA, TJ, LANES), lambda g: (0, g, 0)),
        scratch_shapes=[
            pltpu.VMEM((TJ, 5 * LANES), BF16),
            pltpu.VMEM((TJ, 3 * LANES), BF16),
            pltpu.VMEM((32 * NC, 1024), BF16),
        ],
        compiler_params=PARAMS,
    )(amps, weight, jnp.transpose(ints_fit, (1, 0, 2)), ints_cabs)
    got = exchange(sent, "aux")

    sent = pl.pallas_call(
        sum_aux,
        out_shape=shape_of((NO, 16, LANES), F32),
        in_specs=vmem(1),
        out_specs=vmem(1)[0],
        scratch_shapes=[pltpu.VMEM((3 * TJ, LANES), F32)],
        compiler_params=PARAMS,
    )(got)
    got = exchange(sent, "occ")

    sent = pl.pallas_call(
        sum_occ,
        out_shape=shape_of((16, LANES), F32),
        in_specs=vmem(1),
        out_specs=vmem(1)[0],
        compiler_params=PARAMS,
    )(got)
    sent = jnp.broadcast_to(sent.astype(F16)[None], (NP * NO, 16, LANES))
    got = exchange(sent, ("pair", "occ")).astype(F32)

    sent = pl.pallas_call(
        pair_blocks_kernel,
        out_shape=shape_of((NA, 40, LANES), F32),
        in_specs=[SMEM] + vmem(2),
        out_specs=vmem(1)[0],
        scratch_shapes=[
            pltpu.VMEM((NP, 3 * TJ, LANES), F32),
            pltpu.VMEM((NP * TJ, 3 * LANES), F32),
            pltpu.VMEM((3, 256, LANES), F32),
        ],
        compiler_params=PARAMS,
    )(info, got, amps)
    got = exchange(sent, "aux")

    return pl.pallas_call(
        unpack,
        out_shape=shape_of((40, 8, LANES), F32),
        in_specs=vmem(1),
        out_specs=vmem(1)[0],
        compiler_params=PARAMS,
    )(got)


def solution(mesh):
    placed = (
        P("aux", None, "occ"),
        P("aux", None, "occ"),
        P("occ", None),
        P("occ"),
        P("aux", "occ", None),
        P("aux", "occ", None),
        P(),
        P("pair", None),
        P("pair"),
    )
    return jax.shard_map(
        on_device, mesh=mesh, in_specs=placed, out_specs=P("pair", "occ", None), check_vma=False
    )
```

```python
import functools
import math

import jax
import jax.numpy as jnp
from jax import lax
from jax.experimental import pallas as pl
from jax.experimental.pallas import tpu as pltpu
from jax.sharding import PartitionSpec as P

F32, BF16, F16 = jnp.float32, jnp.bfloat16, jnp.float16
LANES = 128
LN2 = math.log(2.0)
NT = (((1,), (1,)), ((), ()))
TN = (((0,), (0,)), ((), ()))


def iota(shape, dim):
    return lax.broadcasted_iota(jnp.int32, shape, dim)


def dot(a, b, dims=(((1,), (0,)), ((), ()))):
    return lax.dot_general(a, b, dims, preferred_element_type=F32)


def one_hot(cond):
    return jnp.where(cond, 1.0, 0.0).astype(BF16)


def swap_pieces(xs, piece):
    lane = iota(xs[0].shape, 1)
    bit = 1
    while bit < len(xs):
        keep = ((lane // piece) & bit) == 0
        ys = list(xs)
        for k in range(len(xs)):
            if k & bit == 0:
                lo, hi = xs[k], xs[k + bit]
                ys[k] = jnp.where(keep, lo, pltpu.roll(hi, piece * bit, 1))
                ys[k + bit] = jnp.where(keep, pltpu.roll(lo, LANES - piece * bit, 1), hi)
        xs = ys
        bit *= 2
    return xs


def vmem(n):
    return [pl.BlockSpec(memory_space=pltpu.VMEM)] * n


SMEM = pl.BlockSpec(memory_space=pltpu.SMEM)
ANY = pl.BlockSpec(memory_space=pl.ANY)

def room(mib):
    return pltpu.CompilerParams(vmem_limit_bytes=mib * 1024 * 1024)


PARAMS = room(40)


NO, NI, NA, NP, NF, NC, NJ = 16, 18, 8, 4, 32, 12, 5
ROWS = 40
CQ = 16
TJ = NO * NJ


def pack_amps(fit_hbm, cabs_hbm, coef_hbm, out, fit, cabs, coef, cab32, x, msg, sems):
    first_j = jnp.minimum(NJ * lax.axis_index("pair"), NI - NJ)
    copies = [
        pltpu.make_async_copy(cabs_hbm, cabs, sems.at[0]),
        pltpu.make_async_copy(fit_hbm.at[pl.ds(first_j, NJ)], fit, sems.at[1]),
        pltpu.make_async_copy(coef_hbm, coef, sems.at[2]),
    ]
    for c in copies:
        c.start()
    shape = (NO, ROWS, NO * NI)
    t = iota(shape, 1)
    place = jnp.where((iota(shape, 2) == NI * iota(shape, 0) + t) & (t < NI), 1.0, 0.0)
    place = place.reshape(NO * ROWS, NO * NI).astype(BF16)
    for c in copies:
        c.wait()
    x[0 : NJ * NF, :] = fit[...].reshape(NJ * NF, NO * NI)
    for q in range(NC):
        cab32[24 * q : 24 * q + NI, :] = cabs[q].astype(F32)
    zero = jnp.zeros((CQ - NC, NO * NI), F32)
    for jj in range(NJ):
        picked = [cab32[pl.ds(24 * q + first_j + jj, 1), :] for q in range(NC)]
        rows = jnp.concatenate(picked + [zero], axis=0)
        x[NJ * NF + CQ * jj : NJ * NF + CQ * (jj + 1), :] = rows.astype(BF16)
    x[NJ * (NF + CQ) :, :] = jnp.zeros((256 - NJ * (NF + CQ), NO * NI), BF16)
    msg[...] = dot(place, x[...], NT).reshape(NO, ROWS, 256)
    tiles = [coef[:, LANES * a : LANES * (a + 1)].astype(F32) for a in range(24)]
    none = jnp.zeros_like(tiles[0])
    left = swap_pieces(tiles[:16], 8)
    right = swap_pieces(tiles[16:] + [none] * 8, 8)
    for o in range(NO):
        msg[o, NI : 2 * NI, 0:LANES] = left[o]
        msg[o, NI : 2 * NI, LANES : 2 * LANES] = right[o]
    out[...] = msg[...].astype(BF16)


def partial_t(got, weight, fit_hbm, cabs_hbm, out, a_fit, a_cab, fit, cabs, padded, sems):
    spans = [pl.ds(1024 * g, 1024) for g in range(3)]
    copies = [
        (
            pltpu.make_async_copy(cabs_hbm.at[:, :, s], cabs.at[:, :, s], sems.at[0, g]),
            pltpu.make_async_copy(fit_hbm.at[:, s], fit.at[:, s], sems.at[1, g]),
        )
        for g, s in enumerate(spans)
    ]
    for pair in copies:
        for c in pair:
            c.start()
    padded[...] = jnp.zeros(padded.shape, BF16)
    shape = (NI, NO, NO * ROWS)
    pick = jnp.where(iota(shape, 2) == ROWS * iota(shape, 1) + iota(shape, 0), 1.0, 0.0)
    pick = pick.reshape(NI * NO, NO * ROWS).astype(BF16)
    amps = dot(pick, got[...].reshape(NO * ROWS, 256))
    amps = [[amps[NO * t : NO * (t + 1), LANES * h : LANES * (h + 1)] for h in (0, 1)] for t in range(NI)]
    lane = iota((NO, LANES), 1)

    def lay(width, start, store):
        per = LANES // width
        for jj in range(NJ):
            half, off = divmod(start + width * jj, LANES)
            for m in range(-(-NI // per)):
                tile = jnp.zeros((NO, LANES), F32)
                for k in range(min(per, NI - m * per)):
                    moved = amps[m * per + k][half]
                    if (width * k - off) % LANES:
                        moved = pltpu.roll(moved, (width * k - off) % LANES, 1)
                    tile = jnp.where((lane >= width * k) & (lane < width * (k + 1)), moved, tile)
                store[NO * jj : NO * (jj + 1), LANES * m : LANES * (m + 1)] = tile.astype(BF16)

    lay(NF, 0, a_fit)
    lay(CQ, NJ * NF, a_cab)
    shape = (3 * LANES, 32 * NC)
    source = iota(shape, 0)
    target = iota(shape, 1)
    order = one_hot(((target >> 5) == (source & 15)) & ((target & 31) == (source >> 4)))
    a_cab[...] = (dot(a_cab[...], order) * weight[...]).astype(BF16)
    for g in range(3):
        for c in copies[g]:
            c.wait()
        for q in range(NC):
            padded[32 * q : 32 * q + NI, :] = cabs[q, :, spans[g]]
        total = dot(a_fit[:, : NI * NF], fit[:, spans[g]]) + dot(a_cab[...], padded[...])
        pieces = swap_pieces([total[:, LANES * k : LANES * (k + 1)] for k in range(8)], 16)
        for k in range(8):
            out[k, TJ * g : TJ * (g + 1), :] = pieces[k].astype(BF16)


def sum_aux(got, out, total):
    total[...] = jnp.sum(got[...].astype(F32), axis=0)
    for o in range(NO):
        out[o, 0:15, :] = total[15 * o : 15 * o + 15, :]
        out[o, 15:16, :] = jnp.zeros((1, LANES), F32)


def sum_occ(got, out):
    total = jnp.sum(got[...], axis=0)
    top = jnp.max(jnp.max(jnp.abs(total), axis=1, keepdims=True), axis=0, keepdims=True)
    power = jnp.ceil(jnp.log(jnp.maximum(top, 1e-30)) * (1.0 / LN2))
    scaled = total * (jnp.exp(power * -LN2) * 16384.0)
    out[...] = jnp.where(iota(total.shape, 0) == 15, power, scaled)


def pair_blocks_kernel(lens, pairs, counts, got, amps, out, tsum, tmat, dmat):
    occ, aux, count = lax.axis_index("occ"), lax.axis_index("aux"), counts[0]
    values = got[...]
    values = values * (jnp.exp(values[:, 15:16, :] * LN2) * (1.0 / 16384.0))
    for y in range(NP):
        for o in range(NO):
            tsum[y, 15 * o : 15 * o + 15, :] = values[NO * y + o, 0:15, :]
    for y in range(NP):
        for g in range(3):
            tmat[TJ * y : TJ * (y + 1), LANES * g : LANES * (g + 1)] = tsum[y, TJ * g : TJ * (g + 1), :]
    shape = (NP, NJ, NO, NO * ROWS)
    y, jj = iota(shape, 0), iota(shape, 1)
    first_j = jnp.minimum(NJ * y, NI - NJ)
    row = ROWS * iota(shape, 2) + NI + first_j + jj
    pick = (iota(shape, 3) == row) & (first_j + jj >= NJ * y)
    pick = jnp.where(pick, 1.0, 0.0).reshape(NP * TJ, NO * ROWS).astype(BF16)
    coef = dot(pick, amps[...].reshape(NO * ROWS, 256)).astype(BF16)
    high = tmat[...].astype(BF16)
    low = (tmat[...] - high.astype(F32)).astype(BF16)
    blocks = dot(coef, high, TN) + dot(coef, low, TN)
    for g in range(3):
        dmat[g] = blocks[:, LANES * g : LANES * (g + 1)]
    lane, row = iota((8, LANES), 1), iota((8, LANES), 0)
    for q in range(5):
        tile = jnp.zeros((8, LANES), F32)
        for k in range(8):
            slot = 8 * q + k
            a, b = pairs[0, slot], pairs[1, slot]
            block = dmat[b >> 3, pl.ds(pl.multiple_of(8 * a, 8), 8), :]
            block = pltpu.roll(block, (16 * (k + 8 - (b & 7))) & 127, 1)
            rows_kept = jnp.where(slot < count, lens[a] - 8 * occ, 0)
            lanes_kept = jnp.clip(lens[b] - 16 * aux, 0, 16) + 16 * k
            tile = jnp.where((lane >= 16 * k) & (lane < lanes_kept) & (row < rows_kept), block, tile)
        for p in range(NA):
            out[p, 8 * q : 8 * (q + 1), :] = tile


def unpack(got, out):
    for q in range(5):
        blocks = swap_pieces([got[p, 8 * q : 8 * (q + 1), :] for p in range(NA)], 16)
        for k in range(8):
            out[8 * q + k] = blocks[k]


def exchange(x, axes):
    return lax.all_to_all(x, axes, split_axis=0, concat_axis=0, tiled=True)


def shape_of(shape, dtype):
    return jax.ShapeDtypeStruct(shape, dtype)


def on_device(amp_fit, amp_cabs, coef, f12_weight, ints_fit, ints_cabs, shell_len, pair_blocks, pair_count):
    weight = jnp.tile(jnp.pad(f12_weight, (0, 32 - NI)), NC)[None, :]

    sent = pl.pallas_call(
        pack_amps,
        out_shape=shape_of((NO, ROWS, 256), BF16),
        in_specs=[ANY] * 3,
        out_specs=vmem(1)[0],
        scratch_shapes=[
            pltpu.VMEM((NJ, NF, NO * NI), BF16),
            pltpu.VMEM((NC, NI, NO * NI), BF16),
            pltpu.VMEM((NI, 24 * LANES), BF16),
            pltpu.VMEM((24 * NC, NO * NI), F32),
            pltpu.VMEM((256, NO * NI), BF16),
            pltpu.VMEM((NO, ROWS, 256), F32),
            pltpu.SemaphoreType.DMA((3,)),
        ],
        compiler_params=room(60),
    )(jnp.transpose(amp_fit, (2, 0, 1)), jnp.transpose(amp_cabs, (0, 2, 1)), coef)
    amps = exchange(sent, "occ")

    sent = pl.pallas_call(
        partial_t,
        out_shape=shape_of((NA, 3 * TJ, LANES), BF16),
        in_specs=vmem(2) + [ANY] * 2,
        out_specs=vmem(1)[0],
        scratch_shapes=[
            pltpu.VMEM((TJ, 5 * LANES), BF16),
            pltpu.VMEM((TJ, 3 * LANES), BF16),
            pltpu.VMEM((NI * NF, 24 * LANES), BF16),
            pltpu.VMEM((NC, NI, 24 * LANES), BF16),
            pltpu.VMEM((32 * NC, 1024), BF16),
            pltpu.SemaphoreType.DMA((2, 3)),
        ],
        compiler_params=room(52),
    )(amps, weight, jnp.transpose(ints_fit, (1, 0, 2)).reshape(NI * NF, 24 * LANES), ints_cabs)
    got = exchange(sent, "aux")

    sent = pl.pallas_call(
        sum_aux,
        out_shape=shape_of((NO, 16, LANES), F32),
        in_specs=vmem(1),
        out_specs=vmem(1)[0],
        scratch_shapes=[pltpu.VMEM((3 * TJ, LANES), F32)],
        compiler_params=PARAMS,
    )(got)
    got = exchange(sent, "occ")

    sent = pl.pallas_call(
        sum_occ,
        out_shape=shape_of((16, LANES), F32),
        in_specs=vmem(1),
        out_specs=vmem(1)[0],
        compiler_params=PARAMS,
    )(got)
    sent = jnp.broadcast_to(sent.astype(F16)[None], (NP * NO, 16, LANES))
    got = exchange(sent, ("pair", "occ")).astype(F32)

    sent = pl.pallas_call(
        pair_blocks_kernel,
        out_shape=shape_of((NA, 40, LANES), F32),
        in_specs=[SMEM] * 3 + vmem(2),
        out_specs=vmem(1)[0],
        scratch_shapes=[
            pltpu.VMEM((NP, 3 * TJ, LANES), F32),
            pltpu.VMEM((NP * TJ, 3 * LANES), F32),
            pltpu.VMEM((3, 256, LANES), F32),
        ],
        compiler_params=PARAMS,
    )(shell_len, pair_blocks.T, pair_count, got, amps)
    got = exchange(sent, "aux")

    return pl.pallas_call(
        unpack,
        out_shape=shape_of((40, 8, LANES), F32),
        in_specs=vmem(1),
        out_specs=vmem(1)[0],
        compiler_params=PARAMS,
    )(got)


def solution(mesh):
    placed = (
        P("aux", None, "occ"),
        P("aux", None, "occ"),
        P("occ", None),
        P("occ"),
        P("aux", "occ", None),
        P("aux", "occ", None),
        P(),
        P("pair", None),
        P("pair"),
    )
    return jax.shard_map(
        on_device, mesh=mesh, in_specs=placed, out_specs=P("pair", "occ", None), check_vma=False
    )
```

```python
import functools
import math

import jax
import jax.numpy as jnp
from jax import lax
from jax.experimental import pallas as pl
from jax.experimental.pallas import tpu as pltpu
from jax.sharding import PartitionSpec as P

F32, BF16, F16 = jnp.float32, jnp.bfloat16, jnp.float16
LANES = 128
LN2 = math.log(2.0)
NT = (((1,), (1,)), ((), ()))
TN = (((0,), (0,)), ((), ()))


def iota(shape, dim):
    return lax.broadcasted_iota(jnp.int32, shape, dim)


def dot(a, b, dims=(((1,), (0,)), ((), ()))):
    return lax.dot_general(a, b, dims, preferred_element_type=F32)


def one_hot(cond):
    return jnp.where(cond, 1.0, 0.0).astype(BF16)


def swap_pieces(xs, piece):
    lane = iota(xs[0].shape, 1)
    bit = 1
    while bit < len(xs):
        keep = ((lane // piece) & bit) == 0
        ys = list(xs)
        for k in range(len(xs)):
            if k & bit == 0:
                lo, hi = xs[k], xs[k + bit]
                ys[k] = jnp.where(keep, lo, pltpu.roll(hi, piece * bit, 1))
                ys[k + bit] = jnp.where(keep, pltpu.roll(lo, LANES - piece * bit, 1), hi)
        xs = ys
        bit *= 2
    return xs


def vmem(n):
    return [pl.BlockSpec(memory_space=pltpu.VMEM)] * n


SMEM = pl.BlockSpec(memory_space=pltpu.SMEM)
ANY = pl.BlockSpec(memory_space=pl.ANY)

def room(mib):
    return pltpu.CompilerParams(vmem_limit_bytes=mib * 1024 * 1024)


PARAMS = room(40)


NO, NI, NA, NP, NF, NC, NJ = 16, 18, 8, 4, 32, 12, 5
CQ = 16
TJ = NO * NJ
TROWS = 3 * TJ
ROWS = 24
CROWS = 240


def pack_amps(fit_hbm, cabs_hbm, coef_hbm, out, fit, cabs, coef, cab32, x, extra, piece, sems):
    aux, pair = lax.axis_index("aux"), lax.axis_index("pair")
    first_j = jnp.minimum(NJ * pair, NI - NJ)
    columns = pl.ds(pl.multiple_of(3 * LANES * aux, LANES), 3 * LANES)
    copies = [
        pltpu.make_async_copy(cabs_hbm, cabs, sems.at[0]),
        pltpu.make_async_copy(fit_hbm.at[pl.ds(first_j, NJ)], fit, sems.at[1]),
        pltpu.make_async_copy(coef_hbm.at[:, columns], coef, sems.at[2]),
    ]
    for c in copies:
        c.start()
    shape = (NO, ROWS, NO * NI)
    t = iota(shape, 1)
    place = jnp.where((iota(shape, 2) == NI * iota(shape, 0) + t) & (t < NI), 1.0, 0.0)
    place = place.reshape(NO * ROWS, NO * NI).astype(BF16)
    source, target = iota((LANES, LANES), 0), iota((LANES, LANES), 1)
    mine = source == 8 * (target & 15) + 2 * pair + ((target >> 4) & 1)
    for c in copies:
        c.wait()
    x[0 : NJ * NF, :] = fit[...].reshape(NJ * NF, NO * NI)
    for q in range(NC):
        cab32[24 * q : 24 * q + NI, :] = cabs[q].astype(F32)
    zero = jnp.zeros((CQ - NC, NO * NI), F32)
    for jj in range(NJ):
        picked = [cab32[pl.ds(24 * q + first_j + jj, 1), :] for q in range(NC)]
        rows = jnp.concatenate(picked + [zero], axis=0)
        x[NJ * NF + CQ * jj : NJ * NF + CQ * (jj + 1), :] = rows.astype(BF16)
    x[NJ * (NF + CQ) :, :] = jnp.zeros((256 - NJ * (NF + CQ), NO * NI), BF16)
    piece[...] = sum(
        dot(coef[:, LANES * k : LANES * (k + 1)], one_hot(mine & ((target >> 5) == k))) for k in range(3)
    )
    lane = iota((6, LANES), 1)
    third = piece[12:18, :]
    extra[...] = jnp.zeros(extra.shape, F32)
    extra[18:24, 0:LANES] = jnp.where(lane < 96, piece[0:6, :], pltpu.roll(third, 96, 1))
    extra[18:24, LANES:] = jnp.where(lane < 96, piece[6:12, :], pltpu.roll(third, 64, 1))
    extra[0:6, LANES:] = jnp.where(lane >= 112, pltpu.roll(third, 48, 1), 0.0)
    extra[6:12, LANES:] = jnp.where(lane >= 112, pltpu.roll(third, 32, 1), 0.0)
    out[...] = (dot(place, x[...], NT).reshape(NO, ROWS, 256) + extra[...][None]).astype(BF16)


def partial_t(got, weight, fit_hbm, cabs_hbm, out, a_fit, a_cab, fit, cabs, padded, own, sems):
    spans = [pl.ds(1024 * g, 1024) for g in range(3)]
    copies = [
        (
            pltpu.make_async_copy(cabs_hbm.at[:, :, s], cabs.at[:, :, s], sems.at[0, g]),
            pltpu.make_async_copy(fit_hbm.at[:, s], fit.at[:, s], sems.at[1, g]),
        )
        for g, s in enumerate(spans)
    ]
    for pair in copies:
        for c in pair:
            c.start()
    padded[...] = jnp.zeros(padded.shape, BF16)
    messages = got[...].reshape(NO * ROWS, 256)
    shape = (NI, NO, NO * ROWS)
    pick = jnp.where(iota(shape, 2) == ROWS * iota(shape, 1) + iota(shape, 0), 1.0, 0.0)
    pick = pick.reshape(NI * NO, NO * ROWS).astype(BF16)
    amps = dot(pick, messages)
    amps = [[amps[NO * t : NO * (t + 1), LANES * h : LANES * (h + 1)] for h in (0, 1)] for t in range(NI)]
    lane = iota((NO, LANES), 1)

    def lay(width, start, store):
        per = LANES // width
        for jj in range(NJ):
            half, off = divmod(start + width * jj, LANES)
            for m in range(-(-NI // per)):
                tile = jnp.zeros((NO, LANES), F32)
                for k in range(min(per, NI - m * per)):
                    moved = amps[m * per + k][half]
                    if (width * k - off) % LANES:
                        moved = pltpu.roll(moved, (width * k - off) % LANES, 1)
                    tile = jnp.where((lane >= width * k) & (lane < width * (k + 1)), moved, tile)
                store[NO * jj : NO * (jj + 1), LANES * m : LANES * (m + 1)] = tile.astype(BF16)

    lay(NF, 0, a_fit)
    lay(CQ, NJ * NF, a_cab)
    shape = (3 * LANES, 32 * NC)
    source = iota(shape, 0)
    target = iota(shape, 1)
    order = one_hot(((target >> 5) == (source & 15)) & ((target & 31) == (source >> 4)))
    a_cab[...] = (dot(a_cab[...], order) * weight[...]).astype(BF16)

    shape = (NO * NI, NO * ROWS)
    row, source = iota(shape, 0), iota(shape, 1)
    occ = (row * 3641) >> 16
    rest = row - NI * occ
    sixth = rest - jnp.where(rest >= 12, 12, jnp.where(rest >= 6, 6, 0))
    base = source - ROWS * occ - sixth
    main = dot(one_hot(base == 18), messages)
    spare0 = dot(one_hot(base == 0), messages[:, LANES:])
    spare1 = dot(one_hot(base == 6), messages[:, LANES:])
    shape = (NO * NI, LANES)
    lane, row = iota(shape, 1), iota(shape, 0)
    rest = row - NI * ((row * 3641) >> 16)
    third = jnp.where(lane < 32, pltpu.roll(main[:, :LANES], 32, 1), pltpu.roll(main[:, LANES:], 64, 1))
    third = jnp.where(lane < 64, third, pltpu.roll(spare0, 80, 1))
    third = jnp.where(lane < 80, third, pltpu.roll(spare1, 96, 1))
    coef = jnp.where(rest < 6, main[:, :LANES], jnp.where(rest < 12, main[:, LANES:], third))
    last = coef[TROWS:]
    lane = iota((48, LANES), 1)
    for b in range(3):
        own[TJ * b : TJ * (b + 1), :] = coef[TJ * b : TJ * (b + 1)]
        moved = pltpu.roll(last, 96 - 32 * b, 1)
        own[TJ * b : TJ * b + 48, :] = jnp.where(lane < 96, coef[TJ * b : TJ * b + 48], moved)
    packed = own[...].astype(BF16)
    for p in range(NA):
        out[p, TROWS:, :] = packed

    for g in range(3):
        for c in copies[g]:
            c.wait()
        for q in range(NC):
            padded[32 * q : 32 * q + NI, :] = cabs[q, :, spans[g]]
        total = dot(a_fit[:, : NI * NF], fit[:, spans[g]]) + dot(a_cab[...], padded[...])
        pieces = swap_pieces([total[:, LANES * k : LANES * (k + 1)] for k in range(8)], 16)
        for k in range(8):
            out[k, TJ * g : TJ * (g + 1), :] = pieces[k].astype(BF16)


def scale_of(top):
    top = jnp.max(jnp.max(top, axis=1, keepdims=True), axis=0, keepdims=True)
    power = jnp.ceil(jnp.log(jnp.maximum(top, 1e-30)) * (1.0 / LN2))
    return power, jnp.exp(power * -LN2) * 16384.0


def unscale(power):
    return jnp.exp(power * LN2) * (1.0 / 16384.0)


def sum_aux(counts, pairs, got, out):
    total = jnp.sum(got[:, 0:TROWS, :].astype(F32), axis=0)
    power, factor = scale_of(jnp.abs(total))
    out[0:TROWS, :] = total * factor
    out[TROWS:, :] = jnp.zeros((16, LANES), F32)
    out[TROWS : TROWS + 1, :] = jnp.broadcast_to(power, (1, LANES))
    out[TROWS + 1 : TROWS + 3, 0:40] = pairs[...].astype(F32)
    out[TROWS + 3 : TROWS + 4, :] = jnp.broadcast_to(counts[0].astype(F32), (1, LANES))


def all_blocks(lens, got, coefs, out, ints, words, tmat, dmat, msg, sem):
    aux, pair = lax.axis_index("aux"), lax.axis_index("pair")
    for y in range(NP):
        ints[8 * y : 8 * (y + 1), :] = got[y, TROWS : TROWS + 8, :].astype(jnp.int32)
    copy = pltpu.make_async_copy(ints, words, sem)
    copy.start()

    lane = iota((1, LANES), 1)
    for g in range(3):
        limit = jnp.zeros((1, LANES), jnp.int32)
        for k in range(8):
            limit = jnp.where((lane >> 4) == k, lens[8 * g + k], limit)
        kept = (lane & 15) + 16 * aux < limit
        for y in range(NP):
            part = got[y, TJ * g : TJ * (g + 1), :] * unscale(got[y, TROWS : TROWS + 1, :])
            part = jnp.where(kept, part, 0.0)
            high = part.astype(BF16)
            tmat[TJ * y : TJ * (y + 1), LANES * g : LANES * (g + 1)] = high
            low = (part - high.astype(F32)).astype(BF16)
            tmat[TJ * y : TJ * (y + 1), LANES * (g + 3) : LANES * (g + 4)] = low
    shape = (NP, NJ, NO, NO * NI)
    y, jj = iota(shape, 0), iota(shape, 1)
    j = jnp.minimum(NJ * y, NI - NJ) + jj
    pick = (iota(shape, 3) == NI * iota(shape, 2) + j) & (j >= NJ * y)
    pick = jnp.where(pick, 1.0, 0.0).reshape(NP * TJ, NO * NI).astype(BF16)
    ordered = dot(pick, tmat[...], TN).astype(BF16)

    for p in range(NA):
        limit = jnp.zeros((1, LANES), jnp.int32)
        for k in range(3):
            limit = jnp.where((lane >> 5) == k, lens[3 * p + k], limit)
        kept = 8 * (lane & 15) + 2 * pair + ((lane >> 4) & 1) < limit
        rows = [coefs[p, TROWS + TJ * b : TROWS + TJ * (b + 1), :].astype(F32) for b in range(3)]
        last = pltpu.roll(rows[0][:48], 32, 1)
        last = jnp.where(lane >= 32, pltpu.roll(rows[1][:48], 64, 1), last)
        last = jnp.where(lane >= 64, pltpu.roll(rows[2][:48], 96, 1), last)
        coef = jnp.concatenate(rows + [last], axis=0)
        coef = jnp.where(kept, coef, 0.0).astype(BF16)
        blocks = dot(coef, ordered[:, : 3 * LANES], TN) + dot(coef, ordered[:, 3 * LANES :], TN)
        for g in range(3):
            dmat[g, LANES * p : LANES * (p + 1), :] = blocks[:, LANES * g : LANES * (g + 1)]

    copy.wait()
    lane = iota((32, LANES), 1)
    top = jnp.zeros((32, LANES), F32)
    for q in range(20):
        y = q // 5
        count = words[8 * y + 3, 0]
        tile = jnp.zeros((32, LANES), F32)
        for k in range(8):
            slot = 8 * (q % 5) + k
            a, b = words[8 * y + 1, slot], words[8 * y + 2, slot]
            third = (a * 171) >> 9
            start = pl.multiple_of(LANES * third + 32 * (a - 3 * third), 32)
            block = dmat[b >> 3, pl.ds(start, 32), :]
            block = pltpu.roll(block, (16 * (k + 8 - (b & 7))) & 127, 1)
            end = jnp.where(slot < count, 16 * (k + 1), 0)
            tile = jnp.where((lane >= 16 * k) & (lane < end), block, tile)
        top = jnp.maximum(top, jnp.abs(tile))
        for e in range(2):
            msg[pl.ds(2 * q + e, NO, stride=48), :] = tile[NO * e : NO * (e + 1)]
    power, factor = scale_of(top)
    row = iota((48, LANES), 0)
    for o in range(NO):
        scaled = jnp.where(row < 40, msg[48 * o : 48 * (o + 1), :] * factor, 0.0)
        out[o] = jnp.where(row == 40, power, scaled)


def sum_occ(got, out, total):
    total[...] = sum(got[o, 0:40, :] * unscale(got[o, 40:41, :]) for o in range(NO))
    for y in range(NP):
        rows = total[10 * y : 10 * (y + 1), :]
        for p in range(NA):
            out[NA * y + p, 0:10, :] = rows
            out[NA * y + p, 10:16, :] = jnp.zeros((6, LANES), F32)


def unpack(got, out, rows):
    for q in range(5):
        for p in range(NA):
            for y in range(NP):
                rows[p, 2 * y : 2 * y + 2, :] = got[NA * y + p, 2 * q : 2 * q + 2, :]
        blocks = swap_pieces([rows[p] for p in range(NA)], 16)
        for k in range(8):
            out[8 * q + k] = blocks[k]


def exchange(x, axes):
    return lax.all_to_all(x, axes, split_axis=0, concat_axis=0, tiled=True)


def shape_of(shape, dtype):
    return jax.ShapeDtypeStruct(shape, dtype)


def on_device(amp_fit, amp_cabs, coef, f12_weight, ints_fit, ints_cabs, shell_len, pair_blocks, pair_count):
    weight = jnp.tile(jnp.pad(f12_weight, (0, 32 - NI)), NC)[None, :]

    sent = pl.pallas_call(
        pack_amps,
        out_shape=shape_of((NO, ROWS, 256), BF16),
        in_specs=[ANY] * 3,
        out_specs=vmem(1)[0],
        scratch_shapes=[
            pltpu.VMEM((NJ, NF, NO * NI), BF16),
            pltpu.VMEM((NC, NI, NO * NI), BF16),
            pltpu.VMEM((NI, 3 * LANES), BF16),
            pltpu.VMEM((24 * NC, NO * NI), F32),
            pltpu.VMEM((256, NO * NI), BF16),
            pltpu.VMEM((ROWS, 256), F32),
            pltpu.VMEM((NI, LANES), F32),
            pltpu.SemaphoreType.DMA((3,)),
        ],
        compiler_params=room(60),
    )(jnp.transpose(amp_fit, (2, 0, 1)), jnp.transpose(amp_cabs, (0, 2, 1)), coef)
    amps = exchange(sent, "occ")

    sent = pl.pallas_call(
        partial_t,
        out_shape=shape_of((NA, TROWS + CROWS, LANES), BF16),
        in_specs=vmem(2) + [ANY] * 2,
        out_specs=vmem(1)[0],
        scratch_shapes=[
            pltpu.VMEM((TJ, 5 * LANES), BF16),
            pltpu.VMEM((TJ, 3 * LANES), BF16),
            pltpu.VMEM((NI * NF, 24 * LANES), BF16),
            pltpu.VMEM((NC, NI, 24 * LANES), BF16),
            pltpu.VMEM((32 * NC, 1024), BF16),
            pltpu.VMEM((CROWS, LANES), F32),
            pltpu.SemaphoreType.DMA((2, 3)),
        ],
        compiler_params=room(52),
    )(amps, weight, jnp.transpose(ints_fit, (1, 0, 2)).reshape(NI * NF, 24 * LANES), ints_cabs)
    shares = exchange(sent, "aux")

    sent = pl.pallas_call(
        sum_aux,
        out_shape=shape_of((TROWS + 16, LANES), F32),
        in_specs=[SMEM] + vmem(2),
        out_specs=vmem(1)[0],
        compiler_params=PARAMS,
    )(pair_count, pair_blocks.T, shares)
    sent = jnp.broadcast_to(sent.astype(F16)[None], (NP, TROWS + 16, LANES))
    got = exchange(sent, "pair").astype(F32)

    sent = pl.pallas_call(
        all_blocks,
        out_shape=shape_of((NO, 48, LANES), F32),
        in_specs=[SMEM] + vmem(2),
        out_specs=vmem(1)[0],
        scratch_shapes=[
            pltpu.VMEM((8 * NP, LANES), jnp.int32),
            pltpu.SMEM((8 * NP, LANES), jnp.int32),
            pltpu.VMEM((NP * TJ, 6 * LANES), BF16),
            pltpu.VMEM((3, 8 * LANES, LANES), F32),
            pltpu.VMEM((NO * 48, LANES), F32),
            pltpu.SemaphoreType.DMA,
        ],
        compiler_params=PARAMS,
    )(shell_len, got, shares)
    got = exchange(sent.astype(F16), "occ").astype(F32)

    sent = pl.pallas_call(
        sum_occ,
        out_shape=shape_of((NP * NA, 16, LANES), F32),
        in_specs=vmem(1),
        out_specs=vmem(1)[0],
        scratch_shapes=[pltpu.VMEM((40, LANES), F32)],
        compiler_params=PARAMS,
    )(got)
    got = exchange(sent, ("pair", "aux"))

    return pl.pallas_call(
        unpack,
        out_shape=shape_of((40, 8, LANES), F32),
        in_specs=vmem(1),
        out_specs=vmem(1)[0],
        scratch_shapes=[pltpu.VMEM((NA, 8, LANES), F32)],
        compiler_params=PARAMS,
    )(got)


def solution(mesh):
    placed = (
        P("aux", None, "occ"),
        P("aux", None, "occ"),
        P("occ", None),
        P("occ"),
        P("aux", "occ", None),
        P("aux", "occ", None),
        P(),
        P("pair", None),
        P("pair"),
    )
    return jax.shard_map(
        on_device, mesh=mesh, in_specs=placed, out_specs=P("pair", "occ", None), check_vma=False
    )
```

```python
import functools
import math

import jax
import jax.numpy as jnp
from jax import lax
from jax.experimental import pallas as pl
from jax.experimental.pallas import tpu as pltpu
from jax.sharding import PartitionSpec as P

F32, BF16, F16 = jnp.float32, jnp.bfloat16, jnp.float16
LANES = 128
LN2 = math.log(2.0)
NT = (((1,), (1,)), ((), ()))
TN = (((0,), (0,)), ((), ()))


def iota(shape, dim):
    return lax.broadcasted_iota(jnp.int32, shape, dim)


def dot(a, b, dims=(((1,), (0,)), ((), ()))):
    return lax.dot_general(a, b, dims, preferred_element_type=F32)


def one_hot(cond):
    return jnp.where(cond, 1.0, 0.0).astype(BF16)


def swap_pieces(xs, piece):
    lane = iota(xs[0].shape, 1)
    bit = 1
    while bit < len(xs):
        keep = ((lane // piece) & bit) == 0
        ys = list(xs)
        for k in range(len(xs)):
            if k & bit == 0:
                lo, hi = xs[k], xs[k + bit]
                ys[k] = jnp.where(keep, lo, pltpu.roll(hi, piece * bit, 1))
                ys[k + bit] = jnp.where(keep, pltpu.roll(lo, LANES - piece * bit, 1), hi)
        xs = ys
        bit *= 2
    return xs


def vmem(n):
    return [pl.BlockSpec(memory_space=pltpu.VMEM)] * n


SMEM = pl.BlockSpec(memory_space=pltpu.SMEM)
ANY = pl.BlockSpec(memory_space=pl.ANY)

def room(mib):
    return pltpu.CompilerParams(vmem_limit_bytes=mib * 1024 * 1024)


PARAMS = room(40)


NO, NI, NA, NP, NF, NC, NJ = 16, 18, 8, 4, 32, 12, 5
CQ = 16
TJ = NO * NJ
GROUP = 8 * LANES
TROWS = 3 * TJ
ROWS = 24
CROWS = 240


def pack_amps(fit_hbm, cabs_hbm, coef_hbm, out, fit, cabs, coef, cab32, x, extra, piece, sems):
    aux, pair = lax.axis_index("aux"), lax.axis_index("pair")
    first_j = jnp.minimum(NJ * pair, NI - NJ)
    columns = pl.ds(pl.multiple_of(3 * LANES * aux, LANES), 3 * LANES)
    copies = [
        pltpu.make_async_copy(cabs_hbm, cabs, sems.at[0]),
        pltpu.make_async_copy(fit_hbm.at[pl.ds(first_j, NJ)], fit, sems.at[1]),
        pltpu.make_async_copy(coef_hbm.at[:, columns], coef, sems.at[2]),
    ]
    for c in copies:
        c.start()
    shape = (NO, ROWS, NO * NI)
    t = iota(shape, 1)
    place = jnp.where((iota(shape, 2) == NI * iota(shape, 0) + t) & (t < NI), 1.0, 0.0)
    place = place.reshape(NO * ROWS, NO * NI).astype(BF16)
    source, target = iota((LANES, LANES), 0), iota((LANES, LANES), 1)
    mine = source == 8 * (target & 15) + 2 * pair + ((target >> 4) & 1)
    for c in copies:
        c.wait()
    x[0 : NJ * NF, :] = fit[...].reshape(NJ * NF, NO * NI)
    for q in range(NC):
        cab32[24 * q : 24 * q + NI, :] = cabs[q].astype(F32)
    zero = jnp.zeros((CQ - NC, NO * NI), F32)
    for jj in range(NJ):
        picked = [cab32[pl.ds(24 * q + first_j + jj, 1), :] for q in range(NC)]
        rows = jnp.concatenate(picked + [zero], axis=0)
        x[NJ * NF + CQ * jj : NJ * NF + CQ * (jj + 1), :] = rows.astype(BF16)
    x[NJ * (NF + CQ) :, :] = jnp.zeros((256 - NJ * (NF + CQ), NO * NI), BF16)
    piece[...] = sum(
        dot(coef[:, LANES * k : LANES * (k + 1)], one_hot(mine & ((target >> 5) == k))) for k in range(3)
    )
    lane = iota((6, LANES), 1)
    third = piece[12:18, :]
    extra[...] = jnp.zeros(extra.shape, F32)
    extra[18:24, 0:LANES] = jnp.where(lane < 96, piece[0:6, :], pltpu.roll(third, 96, 1))
    extra[18:24, LANES:] = jnp.where(lane < 96, piece[6:12, :], pltpu.roll(third, 64, 1))
    extra[0:6, LANES:] = jnp.where(lane >= 112, pltpu.roll(third, 48, 1), 0.0)
    extra[6:12, LANES:] = jnp.where(lane >= 112, pltpu.roll(third, 32, 1), 0.0)
    out[...] = (dot(place, x[...], NT).reshape(NO, ROWS, 256) + extra[...][None]).astype(BF16)


def join_cabs(cabs_hbm, out, cabs, sem):
    copy = pltpu.make_async_copy(cabs_hbm, cabs, sem)
    copy.start()
    copy.wait()
    for q in range(NC):
        out[NI * q : NI * (q + 1), :] = cabs[q]


def partial_t(got, weight, cabs, fit_hbm, out, a_fit, a_cab, own, fit, sems):
    spans = [pl.ds(GROUP * g, GROUP) for g in range(3)]
    copies = [pltpu.make_async_copy(fit_hbm.at[:, s], fit.at[:, s], sems.at[g]) for g, s in enumerate(spans)]
    for c in copies:
        c.start()
    messages = got[...].reshape(NO * ROWS, 256)
    shape = (NI, NO, NO * ROWS)
    pick = jnp.where(iota(shape, 2) == ROWS * iota(shape, 1) + iota(shape, 0), 1.0, 0.0)
    pick = pick.reshape(NI * NO, NO * ROWS).astype(BF16)
    amps = dot(pick, messages)
    amps = [[amps[NO * t : NO * (t + 1), LANES * h : LANES * (h + 1)] for h in (0, 1)] for t in range(NI)]
    lane = iota((NO, LANES), 1)

    def lay(width, start, store):
        per = LANES // width
        for jj in range(NJ):
            half, off = divmod(start + width * jj, LANES)
            for m in range(-(-NI // per)):
                tile = jnp.zeros((NO, LANES), F32)
                for k in range(min(per, NI - m * per)):
                    moved = amps[m * per + k][half]
                    if (width * k - off) % LANES:
                        moved = pltpu.roll(moved, (width * k - off) % LANES, 1)
                    tile = jnp.where((lane >= width * k) & (lane < width * (k + 1)), moved, tile)
                store[NO * jj : NO * (jj + 1), LANES * m : LANES * (m + 1)] = tile.astype(BF16)

    lay(NF, 0, a_fit)
    lay(CQ, NJ * NF, a_cab)
    shape = (3 * LANES, 2 * LANES)
    source, target = iota(shape, 0), iota(shape, 1)
    q = (target * 3641) >> 16
    order = one_hot((q == (source & 15)) & (target - NI * q == (source >> 4)))
    a_cab[:, : 2 * LANES] = (dot(a_cab[...], order) * weight[...]).astype(BF16)

    shape = (NO * NI, NO * ROWS)
    row, source = iota(shape, 0), iota(shape, 1)
    occ = (row * 3641) >> 16
    rest = row - NI * occ
    sixth = rest - jnp.where(rest >= 12, 12, jnp.where(rest >= 6, 6, 0))
    base = source - ROWS * occ - sixth
    main = dot(one_hot(base == 18), messages)
    spare0 = dot(one_hot(base == 0), messages[:, LANES:])
    spare1 = dot(one_hot(base == 6), messages[:, LANES:])
    shape = (NO * NI, LANES)
    lane, row = iota(shape, 1), iota(shape, 0)
    rest = row - NI * ((row * 3641) >> 16)
    third = jnp.where(lane < 32, pltpu.roll(main[:, :LANES], 32, 1), pltpu.roll(main[:, LANES:], 64, 1))
    third = jnp.where(lane < 64, third, pltpu.roll(spare0, 80, 1))
    third = jnp.where(lane < 80, third, pltpu.roll(spare1, 96, 1))
    coef = jnp.where(rest < 6, main[:, :LANES], jnp.where(rest < 12, main[:, LANES:], third))
    last = coef[TROWS:]
    lane = iota((48, LANES), 1)
    for b in range(3):
        own[TJ * b : TJ * (b + 1), :] = coef[TJ * b : TJ * (b + 1)]
        moved = pltpu.roll(last, 96 - 32 * b, 1)
        own[TJ * b : TJ * b + 48, :] = jnp.where(lane < 96, coef[TJ * b : TJ * b + 48], moved)
    packed = own[...].astype(BF16)
    for p in range(NA):
        out[p, TROWS:, :] = packed

    for g in range(3):
        copies[g].wait()
        total = dot(a_fit[:, : NI * NF], fit[:, spans[g]]) + dot(a_cab[:, : NI * NC], cabs[:, spans[g]])
        pieces = swap_pieces([total[:, LANES * k : LANES * (k + 1)] for k in range(8)], 16)
        for k in range(8):
            out[k, TJ * g : TJ * (g + 1), :] = pieces[k].astype(BF16)


def scale_of(top):
    top = jnp.max(jnp.max(top, axis=1, keepdims=True), axis=0, keepdims=True)
    power = jnp.ceil(jnp.log(jnp.maximum(top, 1e-30)) * (1.0 / LN2))
    return power, jnp.exp(power * -LN2) * 16384.0


def unscale(power):
    return jnp.exp(power * LN2) * (1.0 / 16384.0)


def sum_aux(counts, pairs, got, out):
    total = jnp.sum(got[:, 0:TROWS, :].astype(F32), axis=0)
    power, factor = scale_of(jnp.abs(total))
    out[0:TROWS, :] = total * factor
    out[TROWS:, :] = jnp.zeros((16, LANES), F32)
    out[TROWS : TROWS + 1, :] = jnp.broadcast_to(power, (1, LANES))
    out[TROWS + 1 : TROWS + 3, 0:40] = pairs[...].astype(F32)
    out[TROWS + 3 : TROWS + 4, :] = jnp.broadcast_to(counts[0].astype(F32), (1, LANES))


def all_blocks(lens, got, coefs, out, ints, words, tmat, dmat, msg, sem):
    aux, pair = lax.axis_index("aux"), lax.axis_index("pair")
    for y in range(NP):
        ints[8 * y : 8 * (y + 1), :] = got[y, TROWS : TROWS + 8, :].astype(jnp.int32)
    copy = pltpu.make_async_copy(ints, words, sem)
    copy.start()

    lane = iota((1, LANES), 1)
    for g in range(3):
        limit = jnp.zeros((1, LANES), jnp.int32)
        for k in range(8):
            limit = jnp.where((lane >> 4) == k, lens[8 * g + k], limit)
        kept = (lane & 15) + 16 * aux < limit
        for y in range(NP):
            part = got[y, TJ * g : TJ * (g + 1), :] * unscale(got[y, TROWS : TROWS + 1, :])
            part = jnp.where(kept, part, 0.0)
            high = part.astype(BF16)
            tmat[TJ * y : TJ * (y + 1), LANES * g : LANES * (g + 1)] = high
            low = (part - high.astype(F32)).astype(BF16)
            tmat[TJ * y : TJ * (y + 1), LANES * (g + 3) : LANES * (g + 4)] = low
    shape = (NP, NJ, NO, NO * NI)
    y, jj = iota(shape, 0), iota(shape, 1)
    j = jnp.minimum(NJ * y, NI - NJ) + jj
    pick = (iota(shape, 3) == NI * iota(shape, 2) + j) & (j >= NJ * y)
    pick = jnp.where(pick, 1.0, 0.0).reshape(NP * TJ, NO * NI).astype(BF16)
    ordered = dot(pick, tmat[...], TN).astype(BF16)

    for p in range(NA):
        limit = jnp.zeros((1, LANES), jnp.int32)
        for k in range(3):
            limit = jnp.where((lane >> 5) == k, lens[3 * p + k], limit)
        kept = 8 * (lane & 15) + 2 * pair + ((lane >> 4) & 1) < limit
        rows = [coefs[p, TROWS + TJ * b : TROWS + TJ * (b + 1), :].astype(F32) for b in range(3)]
        last = pltpu.roll(rows[0][:48], 32, 1)
        last = jnp.where(lane >= 32, pltpu.roll(rows[1][:48], 64, 1), last)
        last = jnp.where(lane >= 64, pltpu.roll(rows[2][:48], 96, 1), last)
        coef = jnp.concatenate(rows + [last], axis=0)
        coef = jnp.where(kept, coef, 0.0).astype(BF16)
        blocks = dot(coef, ordered[:, : 3 * LANES], TN) + dot(coef, ordered[:, 3 * LANES :], TN)
        for g in range(3):
            dmat[g, LANES * p : LANES * (p + 1), :] = blocks[:, LANES * g : LANES * (g + 1)]

    copy.wait()
    lane = iota((32, LANES), 1)
    top = jnp.zeros((32, LANES), F32)
    for q in range(20):
        y = q // 5
        count = words[8 * y + 3, 0]
        tile = jnp.zeros((32, LANES), F32)
        for k in range(8):
            slot = 8 * (q % 5) + k
            a, b = words[8 * y + 1, slot], words[8 * y + 2, slot]
            third = (a * 171) >> 9
            start = pl.multiple_of(LANES * third + 32 * (a - 3 * third), 32)
            block = dmat[b >> 3, pl.ds(start, 32), :]
            block = pltpu.roll(block, (16 * (k + 8 - (b & 7))) & 127, 1)
            end = jnp.where(slot < count, 16 * (k + 1), 0)
            tile = jnp.where((lane >= 16 * k) & (lane < end), block, tile)
        top = jnp.maximum(top, jnp.abs(tile))
        for e in range(2):
            msg[pl.ds(2 * q + e, NO, stride=48), :] = tile[NO * e : NO * (e + 1)]
    power, factor = scale_of(top)
    row = iota((48, LANES), 0)
    for o in range(NO):
        scaled = jnp.where(row < 40, msg[48 * o : 48 * (o + 1), :] * factor, 0.0)
        out[o] = jnp.where(row == 40, power, scaled)


def sum_occ(got, out, total):
    blocks = sum(got[o, 0:40, :] * unscale(got[o, 40:41, :]) for o in range(NO))
    power, factor = scale_of(jnp.abs(blocks))
    total[...] = blocks * factor
    rest = jnp.where(iota((6, LANES), 0) == 0, power, 0.0)
    for y in range(NP):
        rows = total[10 * y : 10 * (y + 1), :]
        for p in range(NA):
            out[NA * y + p, 0:10, :] = rows
            out[NA * y + p, 10:16, :] = rest


def unpack(got, out, rows):
    for y in range(NP):
        for p in range(NA):
            part = got[NA * y + p]
            part = part * unscale(part[10:11, :])
            for q in range(5):
                rows[q, p, 2 * y : 2 * y + 2, :] = part[2 * q : 2 * q + 2, :]
    for q in range(5):
        blocks = swap_pieces([rows[q, p] for p in range(NA)], 16)
        for k in range(8):
            out[8 * q + k] = blocks[k]


def exchange(x, axes):
    return lax.all_to_all(x, axes, split_axis=0, concat_axis=0, tiled=True)


def shape_of(shape, dtype):
    return jax.ShapeDtypeStruct(shape, dtype)


def on_device(amp_fit, amp_cabs, coef, f12_weight, ints_fit, ints_cabs, shell_len, pair_blocks, pair_count):
    weight = jnp.pad(jnp.tile(f12_weight, NC), (0, 2 * LANES - NI * NC))[None, :]

    sent = pl.pallas_call(
        pack_amps,
        out_shape=shape_of((NO, ROWS, 256), BF16),
        in_specs=[ANY] * 3,
        out_specs=vmem(1)[0],
        scratch_shapes=[
            pltpu.VMEM((NJ, NF, NO * NI), BF16),
            pltpu.VMEM((NC, NI, NO * NI), BF16),
            pltpu.VMEM((NI, 3 * LANES), BF16),
            pltpu.VMEM((24 * NC, NO * NI), F32),
            pltpu.VMEM((256, NO * NI), BF16),
            pltpu.VMEM((ROWS, 256), F32),
            pltpu.VMEM((NI, LANES), F32),
            pltpu.SemaphoreType.DMA((3,)),
        ],
        compiler_params=room(60),
    )(jnp.transpose(amp_fit, (2, 0, 1)), jnp.transpose(amp_cabs, (0, 2, 1)), coef)
    amps = exchange(sent, "occ")

    cabs = pl.pallas_call(
        join_cabs,
        out_shape=shape_of((NC * NI, 24 * LANES), BF16),
        in_specs=[ANY],
        out_specs=vmem(1)[0],
        scratch_shapes=[pltpu.VMEM((NC, NI, 24 * LANES), BF16), pltpu.SemaphoreType.DMA],
        compiler_params=room(51),
        cost_estimate=pl.CostEstimate(flops=0, bytes_accessed=5_000_000, transcendentals=0),
    )(ints_cabs)
    sent = pl.pallas_call(
        partial_t,
        out_shape=shape_of((NA, TROWS + CROWS, LANES), BF16),
        in_specs=vmem(3) + [ANY],
        out_specs=vmem(1)[0],
        scratch_shapes=[
            pltpu.VMEM((TJ, 5 * LANES), BF16),
            pltpu.VMEM((TJ, 3 * LANES), BF16),
            pltpu.VMEM((CROWS, LANES), F32),
            pltpu.VMEM((NI * NF, 24 * LANES), BF16),
            pltpu.SemaphoreType.DMA((3,)),
        ],
        compiler_params=room(51),
    )(amps, weight, cabs, jnp.transpose(ints_fit, (1, 0, 2)).reshape(NI * NF, 24 * LANES))
    shares = exchange(sent, "aux")

    sent = pl.pallas_call(
        sum_aux,
        out_shape=shape_of((TROWS + 16, LANES), F32),
        in_specs=[SMEM] + vmem(2),
        out_specs=vmem(1)[0],
        compiler_params=PARAMS,
    )(pair_count, pair_blocks.T, shares)
    sent = jnp.broadcast_to(sent.astype(F16)[None], (NP, TROWS + 16, LANES))
    got = exchange(sent, "pair").astype(F32)

    sent = pl.pallas_call(
        all_blocks,
        out_shape=shape_of((NO, 48, LANES), F32),
        in_specs=[SMEM] + vmem(2),
        out_specs=vmem(1)[0],
        scratch_shapes=[
            pltpu.VMEM((8 * NP, LANES), jnp.int32),
            pltpu.SMEM((8 * NP, LANES), jnp.int32),
            pltpu.VMEM((NP * TJ, 6 * LANES), BF16),
            pltpu.VMEM((3, 8 * LANES, LANES), F32),
            pltpu.VMEM((NO * 48, LANES), F32),
            pltpu.SemaphoreType.DMA,
        ],
        compiler_params=PARAMS,
    )(shell_len, got, shares)
    got = exchange(sent.astype(F16), "occ").astype(F32)

    sent = pl.pallas_call(
        sum_occ,
        out_shape=shape_of((NP * NA, 16, LANES), F32),
        in_specs=vmem(1),
        out_specs=vmem(1)[0],
        scratch_shapes=[pltpu.VMEM((40, LANES), F32)],
        compiler_params=PARAMS,
    )(got)
    got = exchange(sent.astype(F16), ("pair", "aux")).astype(F32)

    return pl.pallas_call(
        unpack,
        out_shape=shape_of((40, 8, LANES), F32),
        in_specs=vmem(1),
        out_specs=vmem(1)[0],
        scratch_shapes=[pltpu.VMEM((5, NA, 8, LANES), F32)],
        compiler_params=PARAMS,
    )(got)


def solution(mesh):
    placed = (
        P("aux", None, "occ"),
        P("aux", None, "occ"),
        P("occ", None),
        P("occ"),
        P("aux", "occ", None),
        P("aux", "occ", None),
        P(),
        P("pair", None),
        P("pair"),
    )
    return jax.shard_map(
        on_device, mesh=mesh, in_specs=placed, out_specs=P("pair", "occ", None), check_vma=False
    )
```

```python
import functools
import math

import jax
import jax.numpy as jnp
from jax import lax
from jax.experimental import pallas as pl
from jax.experimental.pallas import tpu as pltpu
from jax.sharding import PartitionSpec as P

F32, BF16, F16 = jnp.float32, jnp.bfloat16, jnp.float16
LANES = 128
LN2 = math.log(2.0)
NT = (((1,), (1,)), ((), ()))
TN = (((0,), (0,)), ((), ()))


def iota(shape, dim):
    return lax.broadcasted_iota(jnp.int32, shape, dim)


def dot(a, b, dims=(((1,), (0,)), ((), ()))):
    return lax.dot_general(a, b, dims, preferred_element_type=F32)


def one_hot(cond):
    return jnp.where(cond, 1.0, 0.0).astype(BF16)


def swap_pieces(xs, piece):
    lane = iota(xs[0].shape, 1)
    bit = 1
    while bit < len(xs):
        keep = ((lane // piece) & bit) == 0
        ys = list(xs)
        for k in range(len(xs)):
            if k & bit == 0:
                lo, hi = xs[k], xs[k + bit]
                ys[k] = jnp.where(keep, lo, pltpu.roll(hi, piece * bit, 1))
                ys[k + bit] = jnp.where(keep, pltpu.roll(lo, LANES - piece * bit, 1), hi)
        xs = ys
        bit *= 2
    return xs


def vmem(n):
    return [pl.BlockSpec(memory_space=pltpu.VMEM)] * n


SMEM = pl.BlockSpec(memory_space=pltpu.SMEM)
ANY = pl.BlockSpec(memory_space=pl.ANY)

def room(mib):
    return pltpu.CompilerParams(vmem_limit_bytes=mib * 1024 * 1024)


PARAMS = room(40)


NO, NI, NA, NP, NF, NC, NJ = 16, 18, 8, 4, 32, 12, 5
CQ = 16
TJ = NO * NJ
GROUP = 8 * LANES
TROWS = 3 * TJ
ROWS = 24
CROWS = 240


def pack_amps(fit_hbm, cabs_hbm, coef_hbm, out, fit, cabs, coef, cab32, x, extra, piece, sems):
    aux, pair = lax.axis_index("aux"), lax.axis_index("pair")
    first_j = jnp.minimum(NJ * pair, NI - NJ)
    columns = pl.ds(pl.multiple_of(3 * LANES * aux, LANES), 3 * LANES)
    copies = [
        pltpu.make_async_copy(cabs_hbm, cabs, sems.at[0]),
        pltpu.make_async_copy(fit_hbm.at[pl.ds(first_j, NJ)], fit, sems.at[1]),
        pltpu.make_async_copy(coef_hbm.at[:, columns], coef, sems.at[2]),
    ]
    for c in copies:
        c.start()
    shape = (NO, ROWS, NO * NI)
    t = iota(shape, 1)
    place = jnp.where((iota(shape, 2) == NI * iota(shape, 0) + t) & (t < NI), 1.0, 0.0)
    place = place.reshape(NO * ROWS, NO * NI).astype(BF16)
    source, target = iota((LANES, LANES), 0), iota((LANES, LANES), 1)
    mine = source == 8 * (target & 15) + 2 * pair + ((target >> 4) & 1)
    for c in copies:
        c.wait()
    x[0 : NJ * NF, :] = fit[...].reshape(NJ * NF, NO * NI)
    for q in range(NC):
        cab32[24 * q : 24 * q + NI, :] = cabs[q].astype(F32)
    zero = jnp.zeros((CQ - NC, NO * NI), F32)
    for jj in range(NJ):
        picked = [cab32[pl.ds(24 * q + first_j + jj, 1), :] for q in range(NC)]
        rows = jnp.concatenate(picked + [zero], axis=0)
        x[NJ * NF + CQ * jj : NJ * NF + CQ * (jj + 1), :] = rows.astype(BF16)
    x[NJ * (NF + CQ) :, :] = jnp.zeros((256 - NJ * (NF + CQ), NO * NI), BF16)
    piece[...] = sum(
        dot(coef[:, LANES * k : LANES * (k + 1)], one_hot(mine & ((target >> 5) == k))) for k in range(3)
    )
    lane = iota((6, LANES), 1)
    third = piece[12:18, :]
    extra[...] = jnp.zeros(extra.shape, F32)
    extra[18:24, 0:LANES] = jnp.where(lane < 96, piece[0:6, :], pltpu.roll(third, 96, 1))
    extra[18:24, LANES:] = jnp.where(lane < 96, piece[6:12, :], pltpu.roll(third, 64, 1))
    extra[0:6, LANES:] = jnp.where(lane >= 112, pltpu.roll(third, 48, 1), 0.0)
    extra[6:12, LANES:] = jnp.where(lane >= 112, pltpu.roll(third, 32, 1), 0.0)
    out[...] = (dot(place, x[...], NT).reshape(NO, ROWS, 256) + extra[...][None]).astype(BF16)


def join_cabs(cabs_hbm, out, cabs, sem):
    copy = pltpu.make_async_copy(cabs_hbm, cabs, sem)
    copy.start()
    copy.wait()
    for q in range(NC):
        out[NI * q : NI * (q + 1), :] = cabs[q]


def partial_t(got, weight, cabs, fit_hbm, out, a_fit, a_cab, own, fit, sems):
    spans = [pl.ds(GROUP * g, GROUP) for g in range(3)]
    copies = [pltpu.make_async_copy(fit_hbm.at[:, s], fit.at[:, s], sems.at[g]) for g, s in enumerate(spans)]
    for c in copies:
        c.start()
    messages = got[...].reshape(NO * ROWS, 256)
    shape = (NI, NO, NO * ROWS)
    pick = jnp.where(iota(shape, 2) == ROWS * iota(shape, 1) + iota(shape, 0), 1.0, 0.0)
    pick = pick.reshape(NI * NO, NO * ROWS).astype(BF16)
    amps = dot(pick, messages)
    amps = [[amps[NO * t : NO * (t + 1), LANES * h : LANES * (h + 1)] for h in (0, 1)] for t in range(NI)]
    lane = iota((NO, LANES), 1)

    def lay(width, start, store):
        per = LANES // width
        for jj in range(NJ):
            half, off = divmod(start + width * jj, LANES)
            for m in range(-(-NI // per)):
                tile = jnp.zeros((NO, LANES), F32)
                for k in range(min(per, NI - m * per)):
                    moved = amps[m * per + k][half]
                    if (width * k - off) % LANES:
                        moved = pltpu.roll(moved, (width * k - off) % LANES, 1)
                    tile = jnp.where((lane >= width * k) & (lane < width * (k + 1)), moved, tile)
                store[NO * jj : NO * (jj + 1), LANES * m : LANES * (m + 1)] = tile.astype(BF16)

    lay(NF, 0, a_fit)
    lay(CQ, NJ * NF, a_cab)
    shape = (3 * LANES, 2 * LANES)
    source, target = iota(shape, 0), iota(shape, 1)
    q = (target * 3641) >> 16
    order = one_hot((q == (source & 15)) & (target - NI * q == (source >> 4)))
    a_cab[:, : 2 * LANES] = (dot(a_cab[...], order) * weight[...]).astype(BF16)

    def pack_coefficients():
        shape = (NO * NI, NO * ROWS)
        row, source = iota(shape, 0), iota(shape, 1)
        occ = (row * 3641) >> 16
        rest = row - NI * occ
        sixth = rest - jnp.where(rest >= 12, 12, jnp.where(rest >= 6, 6, 0))
        base = source - ROWS * occ - sixth
        main = dot(one_hot(base == 18), messages)
        spare0 = dot(one_hot(base == 0), messages[:, LANES:])
        spare1 = dot(one_hot(base == 6), messages[:, LANES:])
        shape = (NO * NI, LANES)
        lane, row = iota(shape, 1), iota(shape, 0)
        rest = row - NI * ((row * 3641) >> 16)
        third = jnp.where(lane < 32, pltpu.roll(main[:, :LANES], 32, 1), pltpu.roll(main[:, LANES:], 64, 1))
        third = jnp.where(lane < 64, third, pltpu.roll(spare0, 80, 1))
        third = jnp.where(lane < 80, third, pltpu.roll(spare1, 96, 1))
        coef = jnp.where(rest < 6, main[:, :LANES], jnp.where(rest < 12, main[:, LANES:], third))
        last = coef[TROWS:]
        lane = iota((48, LANES), 1)
        for b in range(3):
            own[TJ * b : TJ * (b + 1), :] = coef[TJ * b : TJ * (b + 1)]
            moved = pltpu.roll(last, 96 - 32 * b, 1)
            own[TJ * b : TJ * b + 48, :] = jnp.where(lane < 96, coef[TJ * b : TJ * b + 48], moved)
        packed = own[...].astype(BF16)
        for p in range(NA):
            out[p, TROWS:, :] = packed

    for g in range(3):
        copies[g].wait()
        total = dot(a_fit[:, : NI * NF], fit[:, spans[g]]) + dot(a_cab[:, : NI * NC], cabs[:, spans[g]])
        pieces = swap_pieces([total[:, LANES * k : LANES * (k + 1)] for k in range(8)], 16)
        for k in range(8):
            out[k, TJ * g : TJ * (g + 1), :] = pieces[k].astype(BF16)
        if g == 0:
            pack_coefficients()


def scale_of(top):
    top = jnp.max(jnp.max(top, axis=1, keepdims=True), axis=0, keepdims=True)
    power = jnp.ceil(jnp.log(jnp.maximum(top, 1e-30)) * (1.0 / LN2))
    return power, jnp.exp(power * -LN2) * 16384.0


def unscale(power):
    return jnp.exp(power * LN2) * (1.0 / 16384.0)


def sum_aux(counts, pairs, got, out):
    total = jnp.sum(got[:, 0:TROWS, :].astype(F32), axis=0)
    power, factor = scale_of(jnp.abs(total))
    out[0:TROWS, :] = total * factor
    out[TROWS:, :] = jnp.zeros((16, LANES), F32)
    out[TROWS : TROWS + 1, :] = jnp.broadcast_to(power, (1, LANES))
    out[TROWS + 1 : TROWS + 3, 0:40] = pairs[...].astype(F32)
    out[TROWS + 3 : TROWS + 4, :] = jnp.broadcast_to(counts[0].astype(F32), (1, LANES))


def all_blocks(lens, got, coefs, out, ints, words, tmat, dmat, msg, sem):
    aux, pair = lax.axis_index("aux"), lax.axis_index("pair")
    for y in range(NP):
        ints[8 * y : 8 * (y + 1), :] = got[y, TROWS : TROWS + 8, :].astype(jnp.int32)
    copy = pltpu.make_async_copy(ints, words, sem)
    copy.start()

    lane = iota((1, LANES), 1)
    for g in range(3):
        limit = jnp.zeros((1, LANES), jnp.int32)
        for k in range(8):
            limit = jnp.where((lane >> 4) == k, lens[8 * g + k], limit)
        kept = (lane & 15) + 16 * aux < limit
        for y in range(NP):
            part = got[y, TJ * g : TJ * (g + 1), :] * unscale(got[y, TROWS : TROWS + 1, :])
            part = jnp.where(kept, part, 0.0)
            high = part.astype(BF16)
            tmat[TJ * y : TJ * (y + 1), LANES * g : LANES * (g + 1)] = high
            low = (part - high.astype(F32)).astype(BF16)
            tmat[TJ * y : TJ * (y + 1), LANES * (g + 3) : LANES * (g + 4)] = low
    shape = (NP, NJ, NO, NO * NI)
    y, jj = iota(shape, 0), iota(shape, 1)
    j = jnp.minimum(NJ * y, NI - NJ) + jj
    pick = (iota(shape, 3) == NI * iota(shape, 2) + j) & (j >= NJ * y)
    pick = jnp.where(pick, 1.0, 0.0).reshape(NP * TJ, NO * NI).astype(BF16)
    ordered = dot(pick, tmat[...], TN).astype(BF16)

    for p in range(NA):
        limit = jnp.zeros((1, LANES), jnp.int32)
        for k in range(3):
            limit = jnp.where((lane >> 5) == k, lens[3 * p + k], limit)
        kept = 8 * (lane & 15) + 2 * pair + ((lane >> 4) & 1) < limit
        rows = [coefs[p, TROWS + TJ * b : TROWS + TJ * (b + 1), :].astype(F32) for b in range(3)]
        last = pltpu.roll(rows[0][:48], 32, 1)
        last = jnp.where(lane >= 32, pltpu.roll(rows[1][:48], 64, 1), last)
        last = jnp.where(lane >= 64, pltpu.roll(rows[2][:48], 96, 1), last)
        coef = jnp.concatenate(rows + [last], axis=0)
        coef = jnp.where(kept, coef, 0.0).astype(BF16)
        blocks = dot(coef, ordered, TN)
        blocks = blocks[:, : 3 * LANES] + blocks[:, 3 * LANES :]
        for g in range(3):
            dmat[g, LANES * p : LANES * (p + 1), :] = blocks[:, LANES * g : LANES * (g + 1)]

    copy.wait()
    lane = iota((32, LANES), 1)
    top = jnp.zeros((32, LANES), F32)
    for q in range(20):
        y = q // 5
        count = words[8 * y + 3, 0]
        tile = jnp.zeros((32, LANES), F32)
        for k in range(8):
            slot = 8 * (q % 5) + k
            a, b = words[8 * y + 1, slot], words[8 * y + 2, slot]
            third = (a * 171) >> 9
            start = pl.multiple_of(LANES * third + 32 * (a - 3 * third), 32)
            block = dmat[b >> 3, pl.ds(start, 32), :]
            block = pltpu.roll(block, (16 * (k + 8 - (b & 7))) & 127, 1)
            end = jnp.where(slot < count, 16 * (k + 1), 0)
            tile = jnp.where((lane >= 16 * k) & (lane < end), block, tile)
        top = jnp.maximum(top, jnp.abs(tile))
        for e in range(2):
            msg[pl.ds(2 * q + e, NO, stride=48), :] = tile[NO * e : NO * (e + 1)]
    power, factor = scale_of(top)
    row = iota((48, LANES), 0)
    for o in range(NO):
        scaled = jnp.where(row < 40, msg[48 * o : 48 * (o + 1), :] * factor, 0.0)
        out[o] = jnp.where(row == 40, power, scaled)


def sum_occ(got, out, total):
    blocks = sum(got[o, 0:40, :] * unscale(got[o, 40:41, :]) for o in range(NO))
    power, factor = scale_of(jnp.abs(blocks))
    total[...] = blocks * factor
    rest = jnp.where(iota((6, LANES), 0) == 0, power, 0.0)
    for y in range(NP):
        rows = total[10 * y : 10 * (y + 1), :]
        for p in range(NA):
            out[NA * y + p, 0:10, :] = rows
            out[NA * y + p, 10:16, :] = rest


def unpack(got, out, rows):
    for y in range(NP):
        for p in range(NA):
            part = got[NA * y + p]
            part = part * unscale(part[10:11, :])
            for q in range(5):
                rows[q, p, 2 * y : 2 * y + 2, :] = part[2 * q : 2 * q + 2, :]
    for q in range(5):
        blocks = swap_pieces([rows[q, p] for p in range(NA)], 16)
        for k in range(8):
            out[8 * q + k] = blocks[k]


def exchange(x, axes):
    return lax.all_to_all(x, axes, split_axis=0, concat_axis=0, tiled=True)


def shape_of(shape, dtype):
    return jax.ShapeDtypeStruct(shape, dtype)


def on_device(amp_fit, amp_cabs, coef, f12_weight, ints_fit, ints_cabs, shell_len, pair_blocks, pair_count):
    weight = jnp.pad(jnp.tile(f12_weight, NC), (0, 2 * LANES - NI * NC))[None, :]

    sent = pl.pallas_call(
        pack_amps,
        out_shape=shape_of((NO, ROWS, 256), BF16),
        in_specs=[ANY] * 3,
        out_specs=vmem(1)[0],
        scratch_shapes=[
            pltpu.VMEM((NJ, NF, NO * NI), BF16),
            pltpu.VMEM((NC, NI, NO * NI), BF16),
            pltpu.VMEM((NI, 3 * LANES), BF16),
            pltpu.VMEM((24 * NC, NO * NI), F32),
            pltpu.VMEM((256, NO * NI), BF16),
            pltpu.VMEM((ROWS, 256), F32),
            pltpu.VMEM((NI, LANES), F32),
            pltpu.SemaphoreType.DMA((3,)),
        ],
        compiler_params=room(60),
    )(jnp.transpose(amp_fit, (2, 0, 1)), jnp.transpose(amp_cabs, (0, 2, 1)), coef)
    amps = exchange(sent, "occ")

    cabs = pl.pallas_call(
        join_cabs,
        out_shape=shape_of((NC * NI, 24 * LANES), BF16),
        in_specs=[ANY],
        out_specs=vmem(1)[0],
        scratch_shapes=[pltpu.VMEM((NC, NI, 24 * LANES), BF16), pltpu.SemaphoreType.DMA],
        compiler_params=room(51),
        cost_estimate=pl.CostEstimate(flops=0, bytes_accessed=5_000_000, transcendentals=0),
    )(ints_cabs)
    sent = pl.pallas_call(
        partial_t,
        out_shape=shape_of((NA, TROWS + CROWS, LANES), BF16),
        in_specs=vmem(3) + [ANY],
        out_specs=vmem(1)[0],
        scratch_shapes=[
            pltpu.VMEM((TJ, 5 * LANES), BF16),
            pltpu.VMEM((TJ, 3 * LANES), BF16),
            pltpu.VMEM((CROWS, LANES), F32),
            pltpu.VMEM((NI * NF, 24 * LANES), BF16),
            pltpu.SemaphoreType.DMA((3,)),
        ],
        compiler_params=room(49),
    )(amps, weight, cabs, jnp.transpose(ints_fit, (1, 0, 2)).reshape(NI * NF, 24 * LANES))
    shares = exchange(sent, "aux")

    sent = pl.pallas_call(
        sum_aux,
        out_shape=shape_of((TROWS + 16, LANES), F32),
        in_specs=[SMEM] + vmem(2),
        out_specs=vmem(1)[0],
        compiler_params=PARAMS,
    )(pair_count, pair_blocks.T, shares)
    sent = jnp.broadcast_to(sent.astype(F16)[None], (NP, TROWS + 16, LANES))
    got = exchange(sent, "pair").astype(F32)

    sent = pl.pallas_call(
        all_blocks,
        out_shape=shape_of((NO, 48, LANES), F32),
        in_specs=[SMEM] + vmem(2),
        out_specs=vmem(1)[0],
        scratch_shapes=[
            pltpu.VMEM((8 * NP, LANES), jnp.int32),
            pltpu.SMEM((8 * NP, LANES), jnp.int32),
            pltpu.VMEM((NP * TJ, 6 * LANES), BF16),
            pltpu.VMEM((3, 8 * LANES, LANES), F32),
            pltpu.VMEM((NO * 48, LANES), F32),
            pltpu.SemaphoreType.DMA,
        ],
        compiler_params=PARAMS,
    )(shell_len, got, shares)
    got = exchange(sent.astype(F16), "occ").astype(F32)

    sent = pl.pallas_call(
        sum_occ,
        out_shape=shape_of((NP * NA, 16, LANES), F32),
        in_specs=vmem(1),
        out_specs=vmem(1)[0],
        scratch_shapes=[pltpu.VMEM((40, LANES), F32)],
        compiler_params=PARAMS,
    )(got)
    got = exchange(sent.astype(F16), ("pair", "aux")).astype(F32)

    return pl.pallas_call(
        unpack,
        out_shape=shape_of((40, 8, LANES), F32),
        in_specs=vmem(1),
        out_specs=vmem(1)[0],
        scratch_shapes=[pltpu.VMEM((5, NA, 8, LANES), F32)],
        compiler_params=PARAMS,
    )(got)


def solution(mesh):
    placed = (
        P("aux", None, "occ"),
        P("aux", None, "occ"),
        P("occ", None),
        P("occ"),
        P("aux", "occ", None),
        P("aux", "occ", None),
        P(),
        P("pair", None),
        P("pair"),
    )
    return jax.shard_map(
        on_device, mesh=mesh, in_specs=placed, out_specs=P("pair", "occ", None), check_vma=False
    )
```

```python
import functools
import math

import jax
import jax.numpy as jnp
from jax import lax
from jax.experimental import pallas as pl
from jax.experimental.pallas import tpu as pltpu
from jax.sharding import PartitionSpec as P

F32, BF16, F16 = jnp.float32, jnp.bfloat16, jnp.float16
LANES = 128
LN2 = math.log(2.0)
NT = (((1,), (1,)), ((), ()))
TN = (((0,), (0,)), ((), ()))


def iota(shape, dim):
    return lax.broadcasted_iota(jnp.int32, shape, dim)


def dot(a, b, dims=(((1,), (0,)), ((), ()))):
    return lax.dot_general(a, b, dims, preferred_element_type=F32)


def one_hot(cond):
    return jnp.where(cond, 1.0, 0.0).astype(BF16)


def swap_pieces(xs, piece):
    lane = iota(xs[0].shape, 1)
    bit = 1
    while bit < len(xs):
        keep = ((lane // piece) & bit) == 0
        ys = list(xs)
        for k in range(len(xs)):
            if k & bit == 0:
                lo, hi = xs[k], xs[k + bit]
                ys[k] = jnp.where(keep, lo, pltpu.roll(hi, piece * bit, 1))
                ys[k + bit] = jnp.where(keep, pltpu.roll(lo, LANES - piece * bit, 1), hi)
        xs = ys
        bit *= 2
    return xs


def vmem(n):
    return [pl.BlockSpec(memory_space=pltpu.VMEM)] * n


SMEM = pl.BlockSpec(memory_space=pltpu.SMEM)
ANY = pl.BlockSpec(memory_space=pl.ANY)

def room(mib):
    return pltpu.CompilerParams(vmem_limit_bytes=mib * 1024 * 1024)


PARAMS = room(40)


NO, NI, NA, NP, NF, NC, NJ = 16, 18, 8, 4, 32, 12, 5
CQ = 16
TJ = NO * NJ
GROUP = 8 * LANES
TROWS = 3 * TJ
ROWS = 24
CROWS = 240


def pack_amps(fit_hbm, cabs_hbm, coef_hbm, out, fit, cabs, coef, cab32, x, extra, piece, sems):
    aux, pair = lax.axis_index("aux"), lax.axis_index("pair")
    first_j = jnp.minimum(NJ * pair, NI - NJ)
    columns = pl.ds(pl.multiple_of(3 * LANES * aux, LANES), 3 * LANES)
    copies = [
        pltpu.make_async_copy(cabs_hbm, cabs, sems.at[0]),
        pltpu.make_async_copy(fit_hbm.at[pl.ds(first_j, NJ)], fit, sems.at[1]),
        pltpu.make_async_copy(coef_hbm.at[:, columns], coef, sems.at[2]),
    ]
    for c in copies:
        c.start()
    shape = (NO, ROWS, NO * NI)
    t = iota(shape, 1)
    place = jnp.where((iota(shape, 2) == NI * iota(shape, 0) + t) & (t < NI), 1.0, 0.0)
    place = place.reshape(NO * ROWS, NO * NI).astype(BF16)
    source, target = iota((LANES, LANES), 0), iota((LANES, LANES), 1)
    mine = source == 8 * (target & 15) + 2 * pair + ((target >> 4) & 1)
    for c in copies:
        c.wait()
    x[0 : NJ * NF, :] = fit[...].reshape(NJ * NF, NO * NI)
    for q in range(NC):
        cab32[24 * q : 24 * q + NI, :] = cabs[q].astype(F32)
    zero = jnp.zeros((CQ - NC, NO * NI), F32)
    for jj in range(NJ):
        picked = [cab32[pl.ds(24 * q + first_j + jj, 1), :] for q in range(NC)]
        rows = jnp.concatenate(picked + [zero], axis=0)
        x[NJ * NF + CQ * jj : NJ * NF + CQ * (jj + 1), :] = rows.astype(BF16)
    x[NJ * (NF + CQ) :, :] = jnp.zeros((256 - NJ * (NF + CQ), NO * NI), BF16)
    piece[...] = sum(
        dot(coef[:, LANES * k : LANES * (k + 1)], one_hot(mine & ((target >> 5) == k))) for k in range(3)
    )
    lane = iota((6, LANES), 1)
    third = piece[12:18, :]
    extra[...] = jnp.zeros(extra.shape, F32)
    extra[18:24, 0:LANES] = jnp.where(lane < 96, piece[0:6, :], pltpu.roll(third, 96, 1))
    extra[18:24, LANES:] = jnp.where(lane < 96, piece[6:12, :], pltpu.roll(third, 64, 1))
    extra[0:6, LANES:] = jnp.where(lane >= 112, pltpu.roll(third, 48, 1), 0.0)
    extra[6:12, LANES:] = jnp.where(lane >= 112, pltpu.roll(third, 32, 1), 0.0)
    out[...] = (dot(place, x[...], NT).reshape(NO, ROWS, 256) + extra[...][None]).astype(BF16)


def join_cabs(counts, pairs, cabs_hbm, out, slots, cabs, sem):
    copy = pltpu.make_async_copy(cabs_hbm, cabs, sem)
    copy.start()
    slots[...] = jnp.zeros(slots.shape, F32)
    slots[1:3, 0:40] = pairs[...].astype(F32)
    slots[3:4, :] = jnp.broadcast_to(counts[0].astype(F32), (1, LANES))
    copy.wait()
    for q in range(NC):
        out[NI * q : NI * (q + 1), :] = cabs[q]


def partial_t(got, weight, cabs, fit_hbm, out, a_fit, a_cab, own, fit, sems):
    spans = [pl.ds(GROUP * g, GROUP) for g in range(3)]
    copies = [pltpu.make_async_copy(fit_hbm.at[:, s], fit.at[:, s], sems.at[g]) for g, s in enumerate(spans)]
    for c in copies:
        c.start()
    messages = got[...].reshape(NO * ROWS, 256)
    shape = (NI, NO, NO * ROWS)
    pick = jnp.where(iota(shape, 2) == ROWS * iota(shape, 1) + iota(shape, 0), 1.0, 0.0)
    pick = pick.reshape(NI * NO, NO * ROWS).astype(BF16)
    amps = dot(pick, messages)
    amps = [[amps[NO * t : NO * (t + 1), LANES * h : LANES * (h + 1)] for h in (0, 1)] for t in range(NI)]
    lane = iota((NO, LANES), 1)

    def lay(width, start, store):
        per = LANES // width
        for jj in range(NJ):
            half, off = divmod(start + width * jj, LANES)
            for m in range(-(-NI // per)):
                tile = jnp.zeros((NO, LANES), F32)
                for k in range(min(per, NI - m * per)):
                    moved = amps[m * per + k][half]
                    if (width * k - off) % LANES:
                        moved = pltpu.roll(moved, (width * k - off) % LANES, 1)
                    tile = jnp.where((lane >= width * k) & (lane < width * (k + 1)), moved, tile)
                store[NO * jj : NO * (jj + 1), LANES * m : LANES * (m + 1)] = tile.astype(BF16)

    lay(NF, 0, a_fit)
    lay(CQ, NJ * NF, a_cab)
    shape = (3 * LANES, 2 * LANES)
    source, target = iota(shape, 0), iota(shape, 1)
    q = (target * 3641) >> 16
    order = one_hot((q == (source & 15)) & (target - NI * q == (source >> 4)))
    a_cab[:, : 2 * LANES] = (dot(a_cab[...], order) * weight[...]).astype(BF16)

    def pack_coefficients():
        shape = (NO * NI, NO * ROWS)
        row, source = iota(shape, 0), iota(shape, 1)
        occ = (row * 3641) >> 16
        rest = row - NI * occ
        sixth = rest - jnp.where(rest >= 12, 12, jnp.where(rest >= 6, 6, 0))
        base = source - ROWS * occ - sixth
        main = dot(one_hot(base == 18), messages)
        spare0 = dot(one_hot(base == 0), messages[:, LANES:])
        spare1 = dot(one_hot(base == 6), messages[:, LANES:])
        shape = (NO * NI, LANES)
        lane, row = iota(shape, 1), iota(shape, 0)
        rest = row - NI * ((row * 3641) >> 16)
        third = jnp.where(lane < 32, pltpu.roll(main[:, :LANES], 32, 1), pltpu.roll(main[:, LANES:], 64, 1))
        third = jnp.where(lane < 64, third, pltpu.roll(spare0, 80, 1))
        third = jnp.where(lane < 80, third, pltpu.roll(spare1, 96, 1))
        coef = jnp.where(rest < 6, main[:, :LANES], jnp.where(rest < 12, main[:, LANES:], third))
        last = coef[TROWS:]
        lane = iota((48, LANES), 1)
        for b in range(3):
            own[TJ * b : TJ * (b + 1), :] = coef[TJ * b : TJ * (b + 1)]
            moved = pltpu.roll(last, 96 - 32 * b, 1)
            own[TJ * b : TJ * b + 48, :] = jnp.where(lane < 96, coef[TJ * b : TJ * b + 48], moved)
        packed = own[...].astype(BF16)
        for p in range(NA):
            out[p, TROWS:, :] = packed

    for g in range(3):
        copies[g].wait()
        total = dot(a_fit[:, : NI * NF], fit[:, spans[g]]) + dot(a_cab[:, : NI * NC], cabs[:, spans[g]])
        pieces = swap_pieces([total[:, LANES * k : LANES * (k + 1)] for k in range(8)], 16)
        for k in range(8):
            out[k, TJ * g : TJ * (g + 1), :] = pieces[k].astype(BF16)
        if g == 0:
            pack_coefficients()


def scale_of(top):
    top = jnp.max(jnp.max(top, axis=1, keepdims=True), axis=0, keepdims=True)
    power = jnp.ceil(jnp.log(jnp.maximum(top, 1e-30)) * (1.0 / LN2))
    return power, jnp.exp(power * -LN2) * 16384.0


def unscale(power):
    return jnp.exp(power * LN2) * (1.0 / 16384.0)


def sum_aux(slots, got, out):
    total = jnp.sum(got[:, 0:TROWS, :].astype(F32), axis=0)
    power, factor = scale_of(jnp.abs(total))
    out[0:TROWS, :] = total * factor
    out[TROWS : TROWS + 8, :] = jnp.where(iota((8, LANES), 0) == 0, power, slots[...])
    out[TROWS + 8 :, :] = jnp.zeros((8, LANES), F32)


def all_blocks(lens, got, coefs, out, ints, words, tmat, dmat, msg, sem):
    aux, pair = lax.axis_index("aux"), lax.axis_index("pair")
    for y in range(NP):
        ints[8 * y : 8 * (y + 1), :] = got[y, TROWS : TROWS + 8, :].astype(jnp.int32)
    copy = pltpu.make_async_copy(ints, words, sem)
    copy.start()

    lane = iota((1, LANES), 1)
    for g in range(3):
        limit = jnp.zeros((1, LANES), jnp.int32)
        for k in range(8):
            limit = jnp.where((lane >> 4) == k, lens[8 * g + k], limit)
        kept = (lane & 15) + 16 * aux < limit
        for y in range(NP):
            part = got[y, TJ * g : TJ * (g + 1), :] * unscale(got[y, TROWS : TROWS + 1, :])
            part = jnp.where(kept, part, 0.0)
            high = part.astype(BF16)
            tmat[TJ * y : TJ * (y + 1), LANES * g : LANES * (g + 1)] = high
            low = (part - high.astype(F32)).astype(BF16)
            tmat[TJ * y : TJ * (y + 1), LANES * (g + 3) : LANES * (g + 4)] = low
    shape = (NP, NJ, NO, NO * NI)
    y, jj = iota(shape, 0), iota(shape, 1)
    j = jnp.minimum(NJ * y, NI - NJ) + jj
    pick = (iota(shape, 3) == NI * iota(shape, 2) + j) & (j >= NJ * y)
    pick = jnp.where(pick, 1.0, 0.0).reshape(NP * TJ, NO * NI).astype(BF16)
    ordered = dot(pick, tmat[...], TN).astype(BF16)

    for p in range(NA):
        limit = jnp.zeros((1, LANES), jnp.int32)
        for k in range(3):
            limit = jnp.where((lane >> 5) == k, lens[3 * p + k], limit)
        kept = 8 * (lane & 15) + 2 * pair + ((lane >> 4) & 1) < limit
        rows = [coefs[p, TROWS + TJ * b : TROWS + TJ * (b + 1), :].astype(F32) for b in range(3)]
        last = pltpu.roll(rows[0][:48], 32, 1)
        last = jnp.where(lane >= 32, pltpu.roll(rows[1][:48], 64, 1), last)
        last = jnp.where(lane >= 64, pltpu.roll(rows[2][:48], 96, 1), last)
        coef = jnp.concatenate(rows + [last], axis=0)
        coef = jnp.where(kept, coef, 0.0).astype(BF16)
        blocks = dot(coef, ordered, TN)
        blocks = blocks[:, : 3 * LANES] + blocks[:, 3 * LANES :]
        for g in range(3):
            dmat[g, LANES * p : LANES * (p + 1), :] = blocks[:, LANES * g : LANES * (g + 1)]

    copy.wait()
    lane = iota((32, LANES), 1)
    top = jnp.zeros((32, LANES), F32)
    for q in range(20):
        y = q // 5
        count = words[8 * y + 3, 0]
        tile = jnp.zeros((32, LANES), F32)
        for k in range(8):
            slot = 8 * (q % 5) + k
            a, b = words[8 * y + 1, slot], words[8 * y + 2, slot]
            third = (a * 171) >> 9
            start = pl.multiple_of(LANES * third + 32 * (a - 3 * third), 32)
            block = dmat[b >> 3, pl.ds(start, 32), :]
            block = pltpu.roll(block, (16 * (k + 8 - (b & 7))) & 127, 1)
            end = jnp.where(slot < count, 16 * (k + 1), 0)
            tile = jnp.where((lane >= 16 * k) & (lane < end), block, tile)
        top = jnp.maximum(top, jnp.abs(tile))
        for e in range(2):
            msg[pl.ds(2 * q + e, NO, stride=48), :] = tile[NO * e : NO * (e + 1)]
    power, factor = scale_of(top)
    row = iota((48, LANES), 0)
    for o in range(NO):
        scaled = jnp.where(row < 40, msg[48 * o : 48 * (o + 1), :] * factor, 0.0)
        out[o] = jnp.where(row == 40, power, scaled)


def sum_occ(got, out, total):
    blocks = sum(got[o, 0:40, :] * unscale(got[o, 40:41, :]) for o in range(NO))
    power, factor = scale_of(jnp.abs(blocks))
    total[...] = blocks * factor
    rest = jnp.where(iota((6, LANES), 0) == 0, power, 0.0)
    for y in range(NP):
        rows = total[10 * y : 10 * (y + 1), :]
        for p in range(NA):
            out[NA * y + p, 0:10, :] = rows
            out[NA * y + p, 10:16, :] = rest


def unpack(got, out, rows):
    for y in range(NP):
        for p in range(NA):
            part = got[NA * y + p]
            part = part * unscale(part[10:11, :])
            for q in range(5):
                rows[q, p, 2 * y : 2 * y + 2, :] = part[2 * q : 2 * q + 2, :]
    for q in range(5):
        blocks = swap_pieces([rows[q, p] for p in range(NA)], 16)
        for k in range(8):
            out[8 * q + k] = blocks[k]


def exchange(x, axes):
    return lax.all_to_all(x, axes, split_axis=0, concat_axis=0, tiled=True)


def shape_of(shape, dtype):
    return jax.ShapeDtypeStruct(shape, dtype)


def on_device(amp_fit, amp_cabs, coef, f12_weight, ints_fit, ints_cabs, shell_len, pair_blocks, pair_count):
    weight = jnp.pad(jnp.tile(f12_weight, NC), (0, 2 * LANES - NI * NC))[None, :]

    sent = pl.pallas_call(
        pack_amps,
        out_shape=shape_of((NO, ROWS, 256), BF16),
        in_specs=[ANY] * 3,
        out_specs=vmem(1)[0],
        scratch_shapes=[
            pltpu.VMEM((NJ, NF, NO * NI), BF16),
            pltpu.VMEM((NC, NI, NO * NI), BF16),
            pltpu.VMEM((NI, 3 * LANES), BF16),
            pltpu.VMEM((24 * NC, NO * NI), F32),
            pltpu.VMEM((256, NO * NI), BF16),
            pltpu.VMEM((ROWS, 256), F32),
            pltpu.VMEM((NI, LANES), F32),
            pltpu.SemaphoreType.DMA((3,)),
        ],
        compiler_params=room(60),
    )(jnp.transpose(amp_fit, (2, 0, 1)), jnp.transpose(amp_cabs, (0, 2, 1)), coef)
    amps = exchange(sent, "occ")

    cabs, slots = pl.pallas_call(
        join_cabs,
        out_shape=[shape_of((NC * NI, 24 * LANES), BF16), shape_of((8, LANES), F32)],
        in_specs=[SMEM] + vmem(1) + [ANY],
        out_specs=vmem(2),
        scratch_shapes=[pltpu.VMEM((NC, NI, 24 * LANES), BF16), pltpu.SemaphoreType.DMA],
        compiler_params=room(51),
        cost_estimate=pl.CostEstimate(flops=0, bytes_accessed=5_000_000, transcendentals=0),
    )(pair_count, pair_blocks.T, ints_cabs)
    sent = pl.pallas_call(
        partial_t,
        out_shape=shape_of((NA, TROWS + CROWS, LANES), BF16),
        in_specs=vmem(3) + [ANY],
        out_specs=vmem(1)[0],
        scratch_shapes=[
            pltpu.VMEM((TJ, 5 * LANES), BF16),
            pltpu.VMEM((TJ, 3 * LANES), BF16),
            pltpu.VMEM((CROWS, LANES), F32),
            pltpu.VMEM((NI * NF, 24 * LANES), BF16),
            pltpu.SemaphoreType.DMA((3,)),
        ],
        compiler_params=room(49),
    )(amps, weight, cabs, jnp.transpose(ints_fit, (1, 0, 2)).reshape(NI * NF, 24 * LANES))
    shares = exchange(sent, "aux")

    sent = pl.pallas_call(
        sum_aux,
        out_shape=shape_of((TROWS + 16, LANES), F32),
        in_specs=vmem(2),
        out_specs=vmem(1)[0],
        compiler_params=PARAMS,
    )(slots, shares)
    sent = jnp.broadcast_to(sent.astype(F16)[None], (NP, TROWS + 16, LANES))
    got = exchange(sent, "pair").astype(F32)

    sent = pl.pallas_call(
        all_blocks,
        out_shape=shape_of((NO, 48, LANES), F32),
        in_specs=[SMEM] + vmem(2),
        out_specs=vmem(1)[0],
        scratch_shapes=[
            pltpu.VMEM((8 * NP, LANES), jnp.int32),
            pltpu.SMEM((8 * NP, LANES), jnp.int32),
            pltpu.VMEM((NP * TJ, 6 * LANES), BF16),
            pltpu.VMEM((3, 8 * LANES, LANES), F32),
            pltpu.VMEM((NO * 48, LANES), F32),
            pltpu.SemaphoreType.DMA,
        ],
        compiler_params=PARAMS,
    )(shell_len, got, shares)
    got = exchange(sent.astype(F16), "occ").astype(F32)

    sent = pl.pallas_call(
        sum_occ,
        out_shape=shape_of((NP * NA, 16, LANES), F32),
        in_specs=vmem(1),
        out_specs=vmem(1)[0],
        scratch_shapes=[pltpu.VMEM((40, LANES), F32)],
        compiler_params=PARAMS,
    )(got)
    got = exchange(sent.astype(F16), ("pair", "aux")).astype(F32)

    return pl.pallas_call(
        unpack,
        out_shape=shape_of((40, 8, LANES), F32),
        in_specs=vmem(1),
        out_specs=vmem(1)[0],
        scratch_shapes=[pltpu.VMEM((5, NA, 8, LANES), F32)],
        compiler_params=PARAMS,
    )(got)


def solution(mesh):
    placed = (
        P("aux", None, "occ"),
        P("aux", None, "occ"),
        P("occ", None),
        P("occ"),
        P("aux", "occ", None),
        P("aux", "occ", None),
        P(),
        P("pair", None),
        P("pair"),
    )
    return jax.shard_map(
        on_device, mesh=mesh, in_specs=placed, out_specs=P("pair", "occ", None), check_vma=False
    )
```

```python
import functools
import math

import jax
import jax.numpy as jnp
from jax import lax
from jax.experimental import pallas as pl
from jax.experimental.pallas import tpu as pltpu
from jax.sharding import PartitionSpec as P

F32, BF16, F16 = jnp.float32, jnp.bfloat16, jnp.float16
LANES = 128
LN2 = math.log(2.0)
NT = (((1,), (1,)), ((), ()))
TN = (((0,), (0,)), ((), ()))


def iota(shape, dim):
    return lax.broadcasted_iota(jnp.int32, shape, dim)


def dot(a, b, dims=(((1,), (0,)), ((), ()))):
    return lax.dot_general(a, b, dims, preferred_element_type=F32)


def one_hot(cond):
    return jnp.where(cond, 1.0, 0.0).astype(BF16)


def swap_pieces(xs, piece):
    lane = iota(xs[0].shape, 1)
    bit = 1
    while bit < len(xs):
        keep = ((lane // piece) & bit) == 0
        ys = list(xs)
        for k in range(len(xs)):
            if k & bit == 0:
                lo, hi = xs[k], xs[k + bit]
                ys[k] = jnp.where(keep, lo, pltpu.roll(hi, piece * bit, 1))
                ys[k + bit] = jnp.where(keep, pltpu.roll(lo, LANES - piece * bit, 1), hi)
        xs = ys
        bit *= 2
    return xs


def vmem(n):
    return [pl.BlockSpec(memory_space=pltpu.VMEM)] * n


SMEM = pl.BlockSpec(memory_space=pltpu.SMEM)
ANY = pl.BlockSpec(memory_space=pl.ANY)

def room(mib):
    return pltpu.CompilerParams(vmem_limit_bytes=mib * 1024 * 1024)


PARAMS = room(40)


NO, NI, NA, NP, NF, NC, NJ = 16, 18, 8, 4, 32, 12, 5
CQ = 16
TJ = 72
GROUP = 8 * LANES
TROWS = 3 * TJ
ROWS = 24
CROWS = 216
SROWS = 3 * (TJ + 8) + 192


def first_column(occ, pair):
    return (9 * pair + 1 - (occ & 1)) >> 1


def pack_amps(fit_hbm, cabs_hbm, coef_hbm, out, fit, cabs, coef, cab32, x, extra, piece, sems):
    aux, pair = lax.axis_index("aux"), lax.axis_index("pair")
    first_j = first_column(lax.axis_index("occ"), pair)
    fifth_j = jnp.minimum(first_j + 4, NI - 1)
    columns = pl.ds(pl.multiple_of(3 * LANES * aux, LANES), 3 * LANES)
    copies = [
        pltpu.make_async_copy(cabs_hbm, cabs, sems.at[0]),
        pltpu.make_async_copy(fit_hbm.at[pl.ds(first_j, 4)], fit.at[pl.ds(0, 4)], sems.at[1]),
        pltpu.make_async_copy(fit_hbm.at[pl.ds(fifth_j, 1)], fit.at[pl.ds(4, 1)], sems.at[2]),
        pltpu.make_async_copy(coef_hbm.at[:, columns], coef, sems.at[3]),
    ]
    for c in copies:
        c.start()
    shape = (NO, ROWS, NO * NI)
    t = iota(shape, 1)
    place = jnp.where((iota(shape, 2) == NI * iota(shape, 0) + t) & (t < NI), 1.0, 0.0)
    place = place.reshape(NO * ROWS, NO * NI).astype(BF16)
    source, target = iota((LANES, LANES), 0), iota((LANES, LANES), 1)
    mine = source == 8 * (target & 15) + 2 * pair + ((target >> 4) & 1)
    for c in copies:
        c.wait()
    x[0 : NJ * NF, :] = fit[...].reshape(NJ * NF, NO * NI)
    for q in range(NC):
        cab32[24 * q : 24 * q + NI, :] = cabs[q].astype(F32)
    zero = jnp.zeros((CQ - NC, NO * NI), F32)
    for jj in range(NJ):
        j = fifth_j if jj == 4 else first_j + jj
        picked = [cab32[pl.ds(24 * q + j, 1), :] for q in range(NC)]
        rows = jnp.concatenate(picked + [zero], axis=0)
        x[NJ * NF + CQ * jj : NJ * NF + CQ * (jj + 1), :] = rows.astype(BF16)
    x[NJ * (NF + CQ) :, :] = jnp.zeros((256 - NJ * (NF + CQ), NO * NI), BF16)
    piece[...] = sum(
        dot(coef[:, LANES * k : LANES * (k + 1)], one_hot(mine & ((target >> 5) == k))) for k in range(3)
    )
    lane = iota((6, LANES), 1)
    third = piece[12:18, :]
    extra[...] = jnp.zeros(extra.shape, F32)
    extra[18:24, 0:LANES] = jnp.where(lane < 96, piece[0:6, :], pltpu.roll(third, 96, 1))
    extra[18:24, LANES:] = jnp.where(lane < 96, piece[6:12, :], pltpu.roll(third, 64, 1))
    extra[0:6, LANES:] = jnp.where(lane >= 112, pltpu.roll(third, 48, 1), 0.0)
    extra[6:12, LANES:] = jnp.where(lane >= 112, pltpu.roll(third, 32, 1), 0.0)
    out[...] = (dot(place, x[...], NT).reshape(NO, ROWS, 256) + extra[...][None]).astype(BF16)


def join_cabs(counts, pairs, cabs_hbm, out, slots, cabs, sem):
    copy = pltpu.make_async_copy(cabs_hbm, cabs, sem)
    copy.start()
    slots[...] = jnp.zeros(slots.shape, F32)
    slots[1:3, 0:40] = pairs[...].astype(F32)
    slots[3:4, :] = jnp.broadcast_to(counts[0].astype(F32), (1, LANES))
    copy.wait()
    for q in range(NC):
        out[NI * q : NI * (q + 1), :] = cabs[q]


def partial_t(got, weight, cabs, fit_hbm, out, a_fit, a_cab, own, fit, sems):
    spans = [pl.ds(GROUP * g, GROUP) for g in range(3)]
    copies = [pltpu.make_async_copy(fit_hbm.at[:, s], fit.at[:, s], sems.at[g]) for g, s in enumerate(spans)]
    for c in copies:
        c.start()
    messages = got[...].reshape(NO * ROWS, 256)
    first = lax.axis_index("pair") & 1

    def picked(step, start):
        count = NO // step
        shape = (NI, count, NO * ROWS)
        pick = iota(shape, 2) == ROWS * (step * iota(shape, 1) + start) + iota(shape, 0)
        pick = jnp.where(pick, 1.0, 0.0).reshape(NI * count, NO * ROWS).astype(BF16)
        rows = dot(pick, messages)
        return [[rows[count * t : count * (t + 1), LANES * h : LANES * (h + 1)] for h in (0, 1)] for t in range(NI)]

    amps, fifth = picked(1, 0), picked(2, first)

    def lay(width, start, store):
        per = LANES // width
        for jj in range(NJ):
            tiles = amps if jj < 4 else fifth
            count = tiles[0][0].shape[0]
            lane = iota((count, LANES), 1)
            half, off = divmod(start + width * jj, LANES)
            for m in range(-(-NI // per)):
                tile = jnp.zeros((count, LANES), F32)
                for k in range(min(per, NI - m * per)):
                    moved = tiles[m * per + k][half]
                    if (width * k - off) % LANES:
                        moved = pltpu.roll(moved, (width * k - off) % LANES, 1)
                    tile = jnp.where((lane >= width * k) & (lane < width * (k + 1)), moved, tile)
                store[NO * jj : NO * jj + count, LANES * m : LANES * (m + 1)] = tile.astype(BF16)

    lay(NF, 0, a_fit)
    lay(CQ, NJ * NF, a_cab)
    shape = (3 * LANES, 2 * LANES)
    source, target = iota(shape, 0), iota(shape, 1)
    q = (target * 3641) >> 16
    order = one_hot((q == (source & 15)) & (target - NI * q == (source >> 4)))
    a_cab[:, : 2 * LANES] = (dot(a_cab[...], order) * weight[...]).astype(BF16)

    def pack_coefficients():
        shape = (NO * NI, NO * ROWS)
        row, source = iota(shape, 0), iota(shape, 1)
        occ = (row * 3641) >> 16
        rest = row - NI * occ
        sixth = rest - jnp.where(rest >= 12, 12, jnp.where(rest >= 6, 6, 0))
        base = source - ROWS * occ - sixth
        main = dot(one_hot(base == 18), messages)
        spare0 = dot(one_hot(base == 0), messages[:, LANES:])
        spare1 = dot(one_hot(base == 6), messages[:, LANES:])
        shape = (NO * NI, LANES)
        lane, row = iota(shape, 1), iota(shape, 0)
        rest = row - NI * ((row * 3641) >> 16)
        third = jnp.where(lane < 32, pltpu.roll(main[:, :LANES], 32, 1), pltpu.roll(main[:, LANES:], 64, 1))
        third = jnp.where(lane < 64, third, pltpu.roll(spare0, 80, 1))
        third = jnp.where(lane < 80, third, pltpu.roll(spare1, 96, 1))
        coef = jnp.where(rest < 6, main[:, :LANES], jnp.where(rest < 12, main[:, LANES:], third))
        last = coef[3 * TJ :]
        lane = iota((TJ, LANES), 1)
        for b in range(3):
            moved = pltpu.roll(last, 96 - 32 * b, 1)
            own[TJ * b : TJ * (b + 1), :] = jnp.where(lane < 96, coef[TJ * b : TJ * (b + 1)], moved)
        packed = own[0:192, :].astype(BF16)
        for p in range(NA):
            out[p, SROWS - 192 :, :] = packed

    pack_coefficients()
    for g in range(3):
        copies[g].wait()
        total = dot(a_fit[:, : NI * NF], fit[:, spans[g]]) + dot(a_cab[:, : NI * NC], cabs[:, spans[g]])
        pieces = swap_pieces([total[:, LANES * k : LANES * (k + 1)] for k in range(8)], 16)
        for k in range(8):
            rows = jnp.concatenate([pieces[k], own[192 + 8 * g : 200 + 8 * g, :]], axis=0)
            out[k, (TJ + 8) * g : (TJ + 8) * (g + 1), :] = rows.astype(BF16)


def scale_of(top):
    top = jnp.max(jnp.max(top, axis=1, keepdims=True), axis=0, keepdims=True)
    power = jnp.ceil(jnp.log(jnp.maximum(top, 1e-30)) * (1.0 / LN2))
    return power, jnp.exp(power * -LN2) * 16384.0


def unscale(power):
    return jnp.exp(power * LN2) * (1.0 / 16384.0)


def sum_aux(slots, got, out):
    total = jnp.sum(got[:, 0 : 3 * (TJ + 8), :].astype(F32), axis=0)
    total = jnp.concatenate([total[(TJ + 8) * g : (TJ + 8) * g + TJ] for g in range(3)], axis=0)
    power, factor = scale_of(jnp.abs(total))
    out[0:TROWS, :] = total * factor
    out[TROWS:, :] = jnp.where(iota((8, LANES), 0) == 0, power, slots[...])


def all_blocks(lens, got, coefs, out, ints, words, tmat, dmat, msg, sem):
    aux, pair = lax.axis_index("aux"), lax.axis_index("pair")
    for y in range(NP):
        ints[8 * y : 8 * (y + 1), :] = got[y, TROWS : TROWS + 8, :].astype(jnp.int32)
    copy = pltpu.make_async_copy(ints, words, sem)
    copy.start()

    lane = iota((1, LANES), 1)
    for g in range(3):
        limit = jnp.zeros((1, LANES), jnp.int32)
        for k in range(8):
            limit = jnp.where((lane >> 4) == k, lens[8 * g + k], limit)
        kept = (lane & 15) + 16 * aux < limit
        for y in range(NP):
            part = got[y, TJ * g : TJ * (g + 1), :] * unscale(got[y, TROWS : TROWS + 1, :])
            part = jnp.where(kept, part, 0.0)
            high = part.astype(BF16).astype(F32)
            tmat[TJ * y : TJ * (y + 1), LANES * g : LANES * (g + 1)] = high
            tmat[TJ * y : TJ * (y + 1), LANES * (g + 3) : LANES * (g + 4)] = part - high
    shape = (NP, TJ, NO * NI)
    y, row = iota(shape, 0), iota(shape, 1)
    fifth = row >= 4 * NO
    occ = jnp.where(fifth, 2 * (row - 4 * NO) + (y & 1), row & (NO - 1))
    j = first_column(occ, y) + jnp.where(fifth, 4, row >> 4)
    pick = jnp.where(iota(shape, 2) == NI * occ + j, 1.0, 0.0)
    pick = pick.reshape(NP * TJ, NO * NI).astype(BF16)
    ordered = dot(pick, tmat[...].astype(BF16), TN).astype(BF16)

    for p in range(NA):
        limit = jnp.zeros((1, LANES), jnp.int32)
        for k in range(3):
            limit = jnp.where((lane >> 5) == k, lens[3 * p + k], limit)
        kept = 8 * (lane & 15) + 2 * pair + ((lane >> 4) & 1) < limit
        packed = coefs[p].astype(F32)
        spare = [packed[(TJ + 8) * g + TJ : (TJ + 8) * (g + 1)] for g in range(3)]
        packed = jnp.concatenate([packed[SROWS - 192 :]] + spare, axis=0)
        rows = [packed[TJ * b : TJ * (b + 1)] for b in range(3)]
        last = pltpu.roll(rows[0], 32, 1)
        last = jnp.where(lane >= 32, pltpu.roll(rows[1], 64, 1), last)
        last = jnp.where(lane >= 64, pltpu.roll(rows[2], 96, 1), last)
        coef = jnp.concatenate(rows + [last], axis=0)
        coef = jnp.where(kept, coef, 0.0).astype(BF16)
        blocks = dot(coef, ordered, TN)
        blocks = blocks[:, : 3 * LANES] + blocks[:, 3 * LANES :]
        for g in range(3):
            dmat[g, LANES * p : LANES * (p + 1), :] = blocks[:, LANES * g : LANES * (g + 1)]

    copy.wait()
    lane = iota((32, LANES), 1)
    top = jnp.zeros((32, LANES), F32)
    for q in range(20):
        y = q // 5
        count = words[8 * y + 3, 0]
        tile = jnp.zeros((32, LANES), F32)
        for k in range(8):
            slot = 8 * (q % 5) + k
            a, b = words[8 * y + 1, slot], words[8 * y + 2, slot]
            third = (a * 171) >> 9
            start = pl.multiple_of(LANES * third + 32 * (a - 3 * third), 32)
            block = dmat[b >> 3, pl.ds(start, 32), :]
            block = pltpu.roll(block, (16 * (k + 8 - (b & 7))) & 127, 1)
            end = jnp.where(slot < count, 16 * (k + 1), 0)
            tile = jnp.where((lane >= 16 * k) & (lane < end), block, tile)
        top = jnp.maximum(top, jnp.abs(tile))
        for e in range(2):
            msg[pl.ds(2 * q + e, NO, stride=48), :] = tile[NO * e : NO * (e + 1)]
    power, factor = scale_of(top)
    row = iota((48, LANES), 0)
    for o in range(NO):
        scaled = jnp.where(row < 40, msg[48 * o : 48 * (o + 1), :] * factor, 0.0)
        out[o] = jnp.where(row == 40, power, scaled)


def sum_occ(got, out, total):
    blocks = sum(got[o, 0:40, :] * unscale(got[o, 40:41, :]) for o in range(NO))
    power, factor = scale_of(jnp.abs(blocks))
    total[...] = blocks * factor
    rest = jnp.where(iota((6, LANES), 0) == 0, power, 0.0)
    for y in range(NP):
        rows = total[10 * y : 10 * (y + 1), :]
        for p in range(NA):
            out[NA * y + p, 0:10, :] = rows
            out[NA * y + p, 10:16, :] = rest


def unpack(got, out, rows):
    for y in range(NP):
        for p in range(NA):
            part = got[NA * y + p]
            part = part * unscale(part[10:11, :])
            for q in range(5):
                rows[q, p, 2 * y : 2 * y + 2, :] = part[2 * q : 2 * q + 2, :]
    for q in range(5):
        blocks = swap_pieces([rows[q, p] for p in range(NA)], 16)
        for k in range(8):
            out[8 * q + k] = blocks[k]


def exchange(x, axes):
    return lax.all_to_all(x, axes, split_axis=0, concat_axis=0, tiled=True)


def shape_of(shape, dtype):
    return jax.ShapeDtypeStruct(shape, dtype)


def on_device(amp_fit, amp_cabs, coef, f12_weight, ints_fit, ints_cabs, shell_len, pair_blocks, pair_count):
    weight = jnp.pad(jnp.tile(f12_weight, NC), (0, 2 * LANES - NI * NC))[None, :]

    sent = pl.pallas_call(
        pack_amps,
        out_shape=shape_of((NO, ROWS, 256), BF16),
        in_specs=[ANY] * 3,
        out_specs=vmem(1)[0],
        scratch_shapes=[
            pltpu.VMEM((NJ, NF, NO * NI), BF16),
            pltpu.VMEM((NC, NI, NO * NI), BF16),
            pltpu.VMEM((NI, 3 * LANES), BF16),
            pltpu.VMEM((24 * NC, NO * NI), F32),
            pltpu.VMEM((256, NO * NI), BF16),
            pltpu.VMEM((ROWS, 256), F32),
            pltpu.VMEM((NI, LANES), F32),
            pltpu.SemaphoreType.DMA((4,)),
        ],
        compiler_params=room(60),
    )(jnp.transpose(amp_fit, (2, 0, 1)), jnp.transpose(amp_cabs, (0, 2, 1)), coef)
    amps = exchange(sent, "occ")

    cabs, slots = pl.pallas_call(
        join_cabs,
        out_shape=[shape_of((NC * NI, 24 * LANES), BF16), shape_of((8, LANES), F32)],
        in_specs=[SMEM] + vmem(1) + [ANY],
        out_specs=vmem(2),
        scratch_shapes=[pltpu.VMEM((NC, NI, 24 * LANES), BF16), pltpu.SemaphoreType.DMA],
        compiler_params=room(51),
        cost_estimate=pl.CostEstimate(flops=0, bytes_accessed=5_000_000, transcendentals=0),
    )(pair_count, pair_blocks.T, ints_cabs)
    sent = pl.pallas_call(
        partial_t,
        out_shape=shape_of((NA, SROWS, LANES), BF16),
        in_specs=vmem(3) + [ANY],
        out_specs=vmem(1)[0],
        scratch_shapes=[
            pltpu.VMEM((TJ, 5 * LANES), BF16),
            pltpu.VMEM((TJ, 3 * LANES), BF16),
            pltpu.VMEM((CROWS, LANES), F32),
            pltpu.VMEM((NI * NF, 24 * LANES), BF16),
            pltpu.SemaphoreType.DMA((3,)),
        ],
        compiler_params=room(49),
    )(amps, weight, cabs, jnp.transpose(ints_fit, (1, 0, 2)).reshape(NI * NF, 24 * LANES))
    shares = exchange(sent, "aux")

    sent = pl.pallas_call(
        sum_aux,
        out_shape=shape_of((TROWS + 8, LANES), F32),
        in_specs=vmem(2),
        out_specs=vmem(1)[0],
        compiler_params=PARAMS,
    )(slots, shares)
    sent = jnp.broadcast_to(sent.astype(F16)[None], (NP, TROWS + 8, LANES))
    got = exchange(sent, "pair").astype(F32)

    sent = pl.pallas_call(
        all_blocks,
        out_shape=shape_of((NO, 48, LANES), F32),
        in_specs=[SMEM] + vmem(2),
        out_specs=vmem(1)[0],
        scratch_shapes=[
            pltpu.VMEM((8 * NP, LANES), jnp.int32),
            pltpu.SMEM((8 * NP, LANES), jnp.int32),
            pltpu.VMEM((NP * TJ, 6 * LANES), F32),
            pltpu.VMEM((3, 8 * LANES, LANES), F32),
            pltpu.VMEM((NO * 48, LANES), F32),
            pltpu.SemaphoreType.DMA,
        ],
        compiler_params=PARAMS,
    )(shell_len, got, shares)
    got = exchange(sent.astype(F16), "occ").astype(F32)

    sent = pl.pallas_call(
        sum_occ,
        out_shape=shape_of((NP * NA, 16, LANES), F32),
        in_specs=vmem(1),
        out_specs=vmem(1)[0],
        scratch_shapes=[pltpu.VMEM((40, LANES), F32)],
        compiler_params=PARAMS,
    )(got)
    got = exchange(sent.astype(F16), ("pair", "aux")).astype(F32)

    return pl.pallas_call(
        unpack,
        out_shape=shape_of((40, 8, LANES), F32),
        in_specs=vmem(1),
        out_specs=vmem(1)[0],
        scratch_shapes=[pltpu.VMEM((5, NA, 8, LANES), F32)],
        compiler_params=PARAMS,
    )(got)


def solution(mesh):
    placed = (
        P("aux", None, "occ"),
        P("aux", None, "occ"),
        P("occ", None),
        P("occ"),
        P("aux", "occ", None),
        P("aux", "occ", None),
        P(),
        P("pair", None),
        P("pair"),
    )
    return jax.shard_map(
        on_device, mesh=mesh, in_specs=placed, out_specs=P("pair", "occ", None), check_vma=False
    )
```

```python
import functools
import math

import jax
import jax.numpy as jnp
from jax import lax
from jax.experimental import pallas as pl
from jax.experimental.pallas import tpu as pltpu
from jax.sharding import PartitionSpec as P

F32, BF16, F16 = jnp.float32, jnp.bfloat16, jnp.float16
LANES = 128
LN2 = math.log(2.0)
NT = (((1,), (1,)), ((), ()))
TN = (((0,), (0,)), ((), ()))


def iota(shape, dim):
    return lax.broadcasted_iota(jnp.int32, shape, dim)


def dot(a, b, dims=(((1,), (0,)), ((), ()))):
    return lax.dot_general(a, b, dims, preferred_element_type=F32)


def one_hot(cond):
    return jnp.where(cond, 1.0, 0.0).astype(BF16)


def swap_pieces(xs, piece):
    lane = iota(xs[0].shape, 1)
    bit = 1
    while bit < len(xs):
        keep = ((lane // piece) & bit) == 0
        ys = list(xs)
        for k in range(len(xs)):
            if k & bit == 0:
                lo, hi = xs[k], xs[k + bit]
                ys[k] = jnp.where(keep, lo, pltpu.roll(hi, piece * bit, 1))
                ys[k + bit] = jnp.where(keep, pltpu.roll(lo, LANES - piece * bit, 1), hi)
        xs = ys
        bit *= 2
    return xs


def vmem(n):
    return [pl.BlockSpec(memory_space=pltpu.VMEM)] * n


SMEM = pl.BlockSpec(memory_space=pltpu.SMEM)
ANY = pl.BlockSpec(memory_space=pl.ANY)

def room(mib):
    return pltpu.CompilerParams(vmem_limit_bytes=mib * 1024 * 1024)


PARAMS = room(40)


NO, NI, NA, NP, NF, NC, NJ = 16, 18, 8, 4, 32, 12, 5
CQ = 16
TJ = 72
GROUP = 8 * LANES
TROWS = 3 * TJ
ROWS = 24
CROWS = 216
SROWS = 3 * (TJ + 8) + 192


def first_column(occ, pair):
    return (9 * pair + 1 - (occ & 1)) >> 1


def pack_amps(fit_hbm, cabs_hbm, coef_hbm, out, fit, cabs, coef, cab32, x, extra, piece, sems):
    aux, pair = lax.axis_index("aux"), lax.axis_index("pair")
    first_j = first_column(lax.axis_index("occ"), pair)
    fifth_j = jnp.minimum(first_j + 4, NI - 1)
    columns = pl.ds(pl.multiple_of(3 * LANES * aux, LANES), 3 * LANES)
    copies = [
        pltpu.make_async_copy(cabs_hbm, cabs, sems.at[0]),
        pltpu.make_async_copy(fit_hbm.at[pl.ds(first_j, 4)], fit.at[pl.ds(0, 4)], sems.at[1]),
        pltpu.make_async_copy(fit_hbm.at[pl.ds(fifth_j, 1)], fit.at[pl.ds(4, 1)], sems.at[2]),
        pltpu.make_async_copy(coef_hbm.at[:, columns], coef, sems.at[3]),
    ]
    for c in copies:
        c.start()
    shape = (NO, ROWS, NO * NI)
    t = iota(shape, 1)
    place = jnp.where((iota(shape, 2) == NI * iota(shape, 0) + t) & (t < NI), 1.0, 0.0)
    place = place.reshape(NO * ROWS, NO * NI).astype(BF16)
    source, target = iota((LANES, LANES), 0), iota((LANES, LANES), 1)
    mine = source == 8 * (target & 15) + 2 * pair + ((target >> 4) & 1)
    for c in copies:
        c.wait()
    x[0 : NJ * NF, :] = fit[...].reshape(NJ * NF, NO * NI)
    for q in range(NC):
        cab32[24 * q : 24 * q + NI, :] = cabs[q].astype(F32)
    zero = jnp.zeros((CQ - NC, NO * NI), F32)
    for jj in range(NJ):
        j = fifth_j if jj == 4 else first_j + jj
        picked = [cab32[pl.ds(24 * q + j, 1), :] for q in range(NC)]
        rows = jnp.concatenate(picked + [zero], axis=0)
        x[NJ * NF + CQ * jj : NJ * NF + CQ * (jj + 1), :] = rows.astype(BF16)
    x[NJ * (NF + CQ) :, :] = jnp.zeros((256 - NJ * (NF + CQ), NO * NI), BF16)
    piece[...] = sum(
        dot(coef[:, LANES * k : LANES * (k + 1)], one_hot(mine & ((target >> 5) == k))) for k in range(3)
    )
    lane = iota((6, LANES), 1)
    third = piece[12:18, :]
    extra[...] = jnp.zeros(extra.shape, F32)
    extra[18:24, 0:LANES] = jnp.where(lane < 96, piece[0:6, :], pltpu.roll(third, 96, 1))
    extra[18:24, LANES:] = jnp.where(lane < 96, piece[6:12, :], pltpu.roll(third, 64, 1))
    extra[0:6, LANES:] = jnp.where(lane >= 112, pltpu.roll(third, 48, 1), 0.0)
    extra[6:12, LANES:] = jnp.where(lane >= 112, pltpu.roll(third, 32, 1), 0.0)
    out[...] = (dot(place, x[...], NT).reshape(NO, ROWS, 256) + extra[...][None]).astype(BF16)


def join_cabs(counts, pairs, cabs_hbm, out, slots, cabs, sem):
    copy = pltpu.make_async_copy(cabs_hbm, cabs, sem)
    copy.start()
    slots[...] = jnp.zeros(slots.shape, F32)
    slots[1:3, 0:40] = pairs[...].astype(F32)
    slots[3:4, :] = jnp.broadcast_to(counts[0].astype(F32), (1, LANES))
    copy.wait()
    for q in range(NC):
        out[NI * q : NI * (q + 1), :] = cabs[q]


def partial_t(got, weight, cabs, fit_hbm, out, a_fit, a_cab, own, fit, sems):
    spans = [pl.ds(GROUP * g, GROUP) for g in range(3)]
    copies = [pltpu.make_async_copy(fit_hbm.at[:, s], fit.at[:, s], sems.at[g]) for g, s in enumerate(spans)]
    for c in copies:
        c.start()
    messages = got[...].reshape(NO * ROWS, 256)
    first = lax.axis_index("pair") & 1

    def picked(step, start):
        count = NO // step
        shape = (NI, count, NO * ROWS)
        pick = iota(shape, 2) == ROWS * (step * iota(shape, 1) + start) + iota(shape, 0)
        pick = jnp.where(pick, 1.0, 0.0).reshape(NI * count, NO * ROWS).astype(BF16)
        rows = dot(pick, messages)
        return [[rows[count * t : count * (t + 1), LANES * h : LANES * (h + 1)] for h in (0, 1)] for t in range(NI)]

    amps, fifth = picked(1, 0), picked(2, first)

    def lay(width, start, store):
        per = LANES // width
        for jj in range(NJ):
            tiles = amps if jj < 4 else fifth
            count = tiles[0][0].shape[0]
            lane = iota((count, LANES), 1)
            half, off = divmod(start + width * jj, LANES)
            for m in range(-(-NI // per)):
                tile = jnp.zeros((count, LANES), F32)
                for k in range(min(per, NI - m * per)):
                    moved = tiles[m * per + k][half]
                    if (width * k - off) % LANES:
                        moved = pltpu.roll(moved, (width * k - off) % LANES, 1)
                    tile = jnp.where((lane >= width * k) & (lane < width * (k + 1)), moved, tile)
                store[NO * jj : NO * jj + count, LANES * m : LANES * (m + 1)] = tile.astype(BF16)

    lay(NF, 0, a_fit)
    lay(CQ, NJ * NF, a_cab)
    shape = (3 * LANES, 2 * LANES)
    source, target = iota(shape, 0), iota(shape, 1)
    q = (target * 3641) >> 16
    order = one_hot((q == (source & 15)) & (target - NI * q == (source >> 4)))
    a_cab[:, : 2 * LANES] = (dot(a_cab[...], order) * weight[...]).astype(BF16)

    def pack_coefficients():
        shape = (NO * NI, NO * ROWS)
        row, source = iota(shape, 0), iota(shape, 1)
        occ = (row * 3641) >> 16
        rest = row - NI * occ
        sixth = rest - jnp.where(rest >= 12, 12, jnp.where(rest >= 6, 6, 0))
        base = source - ROWS * occ - sixth
        main = dot(one_hot(base == 18), messages)
        spare0 = dot(one_hot(base == 0), messages[:, LANES:])
        spare1 = dot(one_hot(base == 6), messages[:, LANES:])
        shape = (NO * NI, LANES)
        lane, row = iota(shape, 1), iota(shape, 0)
        rest = row - NI * ((row * 3641) >> 16)
        third = jnp.where(lane < 32, pltpu.roll(main[:, :LANES], 32, 1), pltpu.roll(main[:, LANES:], 64, 1))
        third = jnp.where(lane < 64, third, pltpu.roll(spare0, 80, 1))
        third = jnp.where(lane < 80, third, pltpu.roll(spare1, 96, 1))
        coef = jnp.where(rest < 6, main[:, :LANES], jnp.where(rest < 12, main[:, LANES:], third))
        last = coef[3 * TJ :]
        lane = iota((TJ, LANES), 1)
        for b in range(3):
            moved = pltpu.roll(last, 96 - 32 * b, 1)
            own[TJ * b : TJ * (b + 1), :] = jnp.where(lane < 96, coef[TJ * b : TJ * (b + 1)], moved)
        packed = own[0:192, :].astype(BF16)
        for p in range(NA):
            out[p, SROWS - 192 :, :] = packed

    for g in range(3):
        copies[g].wait()
        total = dot(a_fit[:, : NI * NF], fit[:, spans[g]]) + dot(a_cab[:, : NI * NC], cabs[:, spans[g]])
        if g == 0:
            pack_coefficients()
        pieces = swap_pieces([total[:, LANES * k : LANES * (k + 1)] for k in range(8)], 16)
        for k in range(8):
            rows = jnp.concatenate([pieces[k], own[192 + 8 * g : 200 + 8 * g, :]], axis=0)
            out[k, (TJ + 8) * g : (TJ + 8) * (g + 1), :] = rows.astype(BF16)


def scale_of(top):
    top = jnp.max(jnp.max(top, axis=1, keepdims=True), axis=0, keepdims=True)
    power = jnp.ceil(jnp.log(jnp.maximum(top, 1e-30)) * (1.0 / LN2))
    return power, jnp.exp(power * -LN2) * 16384.0


def unscale(power):
    return jnp.exp(power * LN2) * (1.0 / 16384.0)


def sum_aux(slots, got, out):
    total = jnp.sum(got[:, 0 : 3 * (TJ + 8), :].astype(F32), axis=0)
    total = jnp.concatenate([total[(TJ + 8) * g : (TJ + 8) * g + TJ] for g in range(3)], axis=0)
    power, factor = scale_of(jnp.abs(total))
    out[0:TROWS, :] = total * factor
    out[TROWS:, :] = jnp.where(iota((8, LANES), 0) == 0, power, slots[...])


def all_blocks(lens, got, coefs, out, ints, words, tmat, dmat, msg, sem):
    aux, pair = lax.axis_index("aux"), lax.axis_index("pair")
    for y in range(NP):
        ints[8 * y : 8 * (y + 1), :] = got[y, TROWS : TROWS + 8, :].astype(jnp.int32)
    copy = pltpu.make_async_copy(ints, words, sem)
    copy.start()

    lane = iota((1, LANES), 1)
    for g in range(3):
        limit = jnp.zeros((1, LANES), jnp.int32)
        for k in range(8):
            limit = jnp.where((lane >> 4) == k, lens[8 * g + k], limit)
        kept = (lane & 15) + 16 * aux < limit
        for y in range(NP):
            part = got[y, TJ * g : TJ * (g + 1), :] * unscale(got[y, TROWS : TROWS + 1, :])
            part = jnp.where(kept, part, 0.0)
            high = part.astype(BF16).astype(F32)
            tmat[TJ * y : TJ * (y + 1), LANES * g : LANES * (g + 1)] = high
            tmat[TJ * y : TJ * (y + 1), LANES * (g + 3) : LANES * (g + 4)] = part - high
    shape = (NP, TJ, NO * NI)
    y, row = iota(shape, 0), iota(shape, 1)
    fifth = row >= 4 * NO
    occ = jnp.where(fifth, 2 * (row - 4 * NO) + (y & 1), row & (NO - 1))
    j = first_column(occ, y) + jnp.where(fifth, 4, row >> 4)
    pick = jnp.where(iota(shape, 2) == NI * occ + j, 1.0, 0.0)
    pick = pick.reshape(NP * TJ, NO * NI).astype(BF16)
    ordered = dot(pick, tmat[...].astype(BF16), TN).astype(BF16)

    for p in range(NA):
        limit = jnp.zeros((1, LANES), jnp.int32)
        for k in range(3):
            limit = jnp.where((lane >> 5) == k, lens[3 * p + k], limit)
        kept = 8 * (lane & 15) + 2 * pair + ((lane >> 4) & 1) < limit
        packed = coefs[p].astype(F32)
        spare = [packed[(TJ + 8) * g + TJ : (TJ + 8) * (g + 1)] for g in range(3)]
        packed = jnp.concatenate([packed[SROWS - 192 :]] + spare, axis=0)
        rows = [packed[TJ * b : TJ * (b + 1)] for b in range(3)]
        last = pltpu.roll(rows[0], 32, 1)
        last = jnp.where(lane >= 32, pltpu.roll(rows[1], 64, 1), last)
        last = jnp.where(lane >= 64, pltpu.roll(rows[2], 96, 1), last)
        coef = jnp.concatenate(rows + [last], axis=0)
        coef = jnp.where(kept, coef, 0.0).astype(BF16)
        blocks = dot(coef, ordered, TN)
        blocks = blocks[:, : 3 * LANES] + blocks[:, 3 * LANES :]
        for g in range(3):
            dmat[g, LANES * p : LANES * (p + 1), :] = blocks[:, LANES * g : LANES * (g + 1)]

    copy.wait()
    lane = iota((32, LANES), 1)
    top = jnp.zeros((32, LANES), F32)
    for q in range(20):
        y = q // 5
        count = words[8 * y + 3, 0]
        tile = jnp.zeros((32, LANES), F32)
        for k in range(8):
            slot = 8 * (q % 5) + k
            a, b = words[8 * y + 1, slot], words[8 * y + 2, slot]
            third = (a * 171) >> 9
            start = pl.multiple_of(LANES * third + 32 * (a - 3 * third), 32)
            block = dmat[b >> 3, pl.ds(start, 32), :]
            block = pltpu.roll(block, (16 * (k + 8 - (b & 7))) & 127, 1)
            end = jnp.where(slot < count, 16 * (k + 1), 0)
            tile = jnp.where((lane >= 16 * k) & (lane < end), block, tile)
        top = jnp.maximum(top, jnp.abs(tile))
        for e in range(2):
            msg[pl.ds(2 * q + e, NO, stride=48), :] = tile[NO * e : NO * (e + 1)]
    power, factor = scale_of(top)
    row = iota((48, LANES), 0)
    for o in range(NO):
        scaled = jnp.where(row < 40, msg[48 * o : 48 * (o + 1), :] * factor, 0.0)
        out[o] = jnp.where(row == 40, power, scaled)


def sum_occ(got, out, total):
    blocks = sum(got[o, 0:40, :] * unscale(got[o, 40:41, :]) for o in range(NO))
    power, factor = scale_of(jnp.abs(blocks))
    total[...] = blocks * factor
    rest = jnp.where(iota((6, LANES), 0) == 0, power, 0.0)
    for y in range(NP):
        rows = total[10 * y : 10 * (y + 1), :]
        for p in range(NA):
            out[NA * y + p, 0:10, :] = rows
            out[NA * y + p, 10:16, :] = rest


def unpack(got, out, rows):
    for y in range(NP):
        for p in range(NA):
            part = got[NA * y + p]
            part = part * unscale(part[10:11, :])
            for q in range(5):
                rows[q, p, 2 * y : 2 * y + 2, :] = part[2 * q : 2 * q + 2, :]
    for q in range(5):
        blocks = swap_pieces([rows[q, p] for p in range(NA)], 16)
        for k in range(8):
            out[8 * q + k] = blocks[k]


def exchange(x, axes):
    return lax.all_to_all(x, axes, split_axis=0, concat_axis=0, tiled=True)


def shape_of(shape, dtype):
    return jax.ShapeDtypeStruct(shape, dtype)


def on_device(amp_fit, amp_cabs, coef, f12_weight, ints_fit, ints_cabs, shell_len, pair_blocks, pair_count):
    weight = jnp.pad(jnp.tile(f12_weight, NC), (0, 2 * LANES - NI * NC))[None, :]

    sent = pl.pallas_call(
        pack_amps,
        out_shape=shape_of((NO, ROWS, 256), BF16),
        in_specs=[ANY] * 3,
        out_specs=vmem(1)[0],
        scratch_shapes=[
            pltpu.VMEM((NJ, NF, NO * NI), BF16),
            pltpu.VMEM((NC, NI, NO * NI), BF16),
            pltpu.VMEM((NI, 3 * LANES), BF16),
            pltpu.VMEM((24 * NC, NO * NI), F32),
            pltpu.VMEM((256, NO * NI), BF16),
            pltpu.VMEM((ROWS, 256), F32),
            pltpu.VMEM((NI, LANES), F32),
            pltpu.SemaphoreType.DMA((4,)),
        ],
        compiler_params=room(60),
    )(jnp.transpose(amp_fit, (2, 0, 1)), jnp.transpose(amp_cabs, (0, 2, 1)), coef)
    amps = exchange(sent, "occ")

    cabs, slots = pl.pallas_call(
        join_cabs,
        out_shape=[shape_of((NC * NI, 24 * LANES), BF16), shape_of((8, LANES), F32)],
        in_specs=[SMEM] + vmem(1) + [ANY],
        out_specs=vmem(2),
        scratch_shapes=[pltpu.VMEM((NC, NI, 24 * LANES), BF16), pltpu.SemaphoreType.DMA],
        compiler_params=room(51),
        cost_estimate=pl.CostEstimate(flops=0, bytes_accessed=5_000_000, transcendentals=0),
    )(pair_count, pair_blocks.T, ints_cabs)
    sent = pl.pallas_call(
        partial_t,
        out_shape=shape_of((NA, SROWS, LANES), BF16),
        in_specs=vmem(3) + [ANY],
        out_specs=vmem(1)[0],
        scratch_shapes=[
            pltpu.VMEM((TJ, 5 * LANES), BF16),
            pltpu.VMEM((TJ, 3 * LANES), BF16),
            pltpu.VMEM((CROWS, LANES), F32),
            pltpu.VMEM((NI * NF, 24 * LANES), BF16),
            pltpu.SemaphoreType.DMA((3,)),
        ],
        compiler_params=room(49),
    )(amps, weight, cabs, jnp.transpose(ints_fit, (1, 0, 2)).reshape(NI * NF, 24 * LANES))
    shares = exchange(sent, "aux")

    sent = pl.pallas_call(
        sum_aux,
        out_shape=shape_of((TROWS + 8, LANES), F32),
        in_specs=vmem(2),
        out_specs=vmem(1)[0],
        compiler_params=PARAMS,
    )(slots, shares)
    sent = jnp.broadcast_to(sent.astype(F16)[None], (NP, TROWS + 8, LANES))
    got = exchange(sent, "pair").astype(F32)

    sent = pl.pallas_call(
        all_blocks,
        out_shape=shape_of((NO, 48, LANES), F32),
        in_specs=[SMEM] + vmem(2),
        out_specs=vmem(1)[0],
        scratch_shapes=[
            pltpu.VMEM((8 * NP, LANES), jnp.int32),
            pltpu.SMEM((8 * NP, LANES), jnp.int32),
            pltpu.VMEM((NP * TJ, 6 * LANES), F32),
            pltpu.VMEM((3, 8 * LANES, LANES), F32),
            pltpu.VMEM((NO * 48, LANES), F32),
            pltpu.SemaphoreType.DMA,
        ],
        compiler_params=PARAMS,
    )(shell_len, got, shares)
    got = exchange(sent.astype(F16), "occ").astype(F32)

    sent = pl.pallas_call(
        sum_occ,
        out_shape=shape_of((NP * NA, 16, LANES), F32),
        in_specs=vmem(1),
        out_specs=vmem(1)[0],
        scratch_shapes=[pltpu.VMEM((40, LANES), F32)],
        compiler_params=PARAMS,
    )(got)
    got = exchange(sent.astype(F16), ("pair", "aux")).astype(F32)

    return pl.pallas_call(
        unpack,
        out_shape=shape_of((40, 8, LANES), F32),
        in_specs=vmem(1),
        out_specs=vmem(1)[0],
        scratch_shapes=[pltpu.VMEM((5, NA, 8, LANES), F32)],
        compiler_params=PARAMS,
    )(got)


def solution(mesh):
    placed = (
        P("aux", None, "occ"),
        P("aux", None, "occ"),
        P("occ", None),
        P("occ"),
        P("aux", "occ", None),
        P("aux", "occ", None),
        P(),
        P("pair", None),
        P("pair"),
    )
    return jax.shard_map(
        on_device, mesh=mesh, in_specs=placed, out_specs=P("pair", "occ", None), check_vma=False
    )
```

```python
import functools
import math

import jax
import jax.numpy as jnp
from jax import lax
from jax.experimental import pallas as pl
from jax.experimental.pallas import tpu as pltpu
from jax.sharding import PartitionSpec as P

F32, BF16, F16 = jnp.float32, jnp.bfloat16, jnp.float16
LANES = 128
LN2 = math.log(2.0)
NT = (((1,), (1,)), ((), ()))
TN = (((0,), (0,)), ((), ()))


def iota(shape, dim):
    return lax.broadcasted_iota(jnp.int32, shape, dim)


def dot(a, b, dims=(((1,), (0,)), ((), ()))):
    return lax.dot_general(a, b, dims, preferred_element_type=F32)


def one_hot(cond):
    return jnp.where(cond, 1.0, 0.0).astype(BF16)


def swap_pieces(xs, piece):
    lane = iota(xs[0].shape, 1)
    bit = 1
    while bit < len(xs):
        keep = ((lane // piece) & bit) == 0
        ys = list(xs)
        for k in range(len(xs)):
            if k & bit == 0:
                lo, hi = xs[k], xs[k + bit]
                ys[k] = jnp.where(keep, lo, pltpu.roll(hi, piece * bit, 1))
                ys[k + bit] = jnp.where(keep, pltpu.roll(lo, LANES - piece * bit, 1), hi)
        xs = ys
        bit *= 2
    return xs


def vmem(n):
    return [pl.BlockSpec(memory_space=pltpu.VMEM)] * n


SMEM = pl.BlockSpec(memory_space=pltpu.SMEM)
ANY = pl.BlockSpec(memory_space=pl.ANY)

def room(mib):
    return pltpu.CompilerParams(vmem_limit_bytes=mib * 1024 * 1024)


PARAMS = room(40)


NO, NI, NA, NP, NF, NC, NJ = 16, 18, 8, 4, 32, 12, 5
CQ = 16
TJ = 72
GROUP = 8 * LANES
TROWS = 3 * TJ
ROOT, STEP, BACK = 11, 7, 7
FROM_ROOT = [[(STEP * k + ROOT) % NO for k in range(NO)]]
ROWS = 24
CROWS = 216
SROWS = 3 * (TJ + 8) + 192


def slot_of(occ):
    return (BACK * (occ + NO - ROOT)) & (NO - 1)


def first_column(occ, pair):
    return (9 * pair + 1 - (occ & 1)) >> 1


def pack_amps(fit_hbm, cabs_hbm, coef_hbm, out, fit, cabs, coef, cab32, x, extra, piece, sems):
    aux, pair = lax.axis_index("aux"), lax.axis_index("pair")
    first_j = first_column(lax.axis_index("occ"), pair)
    fifth_j = jnp.minimum(first_j + 4, NI - 1)
    columns = pl.ds(pl.multiple_of(3 * LANES * aux, LANES), 3 * LANES)
    copies = [
        pltpu.make_async_copy(cabs_hbm, cabs, sems.at[0]),
        pltpu.make_async_copy(fit_hbm.at[pl.ds(first_j, 4)], fit.at[pl.ds(0, 4)], sems.at[1]),
        pltpu.make_async_copy(fit_hbm.at[pl.ds(fifth_j, 1)], fit.at[pl.ds(4, 1)], sems.at[2]),
        pltpu.make_async_copy(coef_hbm.at[:, columns], coef, sems.at[3]),
    ]
    for c in copies:
        c.start()
    shape = (NO, ROWS, NO * NI)
    t = iota(shape, 1)
    place = jnp.where((iota(shape, 2) == NI * ((STEP * iota(shape, 0) + ROOT) & (NO - 1)) + t) & (t < NI), 1.0, 0.0)
    place = place.reshape(NO * ROWS, NO * NI).astype(BF16)
    source, target = iota((LANES, LANES), 0), iota((LANES, LANES), 1)
    mine = source == 8 * (target & 15) + 2 * pair + ((target >> 4) & 1)
    for c in copies:
        c.wait()
    x[0 : NJ * NF, :] = fit[...].reshape(NJ * NF, NO * NI)
    for q in range(NC):
        cab32[24 * q : 24 * q + NI, :] = cabs[q].astype(F32)
    zero = jnp.zeros((CQ - NC, NO * NI), F32)
    for jj in range(NJ):
        j = fifth_j if jj == 4 else first_j + jj
        picked = [cab32[pl.ds(24 * q + j, 1), :] for q in range(NC)]
        rows = jnp.concatenate(picked + [zero], axis=0)
        x[NJ * NF + CQ * jj : NJ * NF + CQ * (jj + 1), :] = rows.astype(BF16)
    x[NJ * (NF + CQ) :, :] = jnp.zeros((256 - NJ * (NF + CQ), NO * NI), BF16)
    piece[...] = sum(
        dot(coef[:, LANES * k : LANES * (k + 1)], one_hot(mine & ((target >> 5) == k))) for k in range(3)
    )
    lane = iota((6, LANES), 1)
    third = piece[12:18, :]
    extra[...] = jnp.zeros(extra.shape, F32)
    extra[18:24, 0:LANES] = jnp.where(lane < 96, piece[0:6, :], pltpu.roll(third, 96, 1))
    extra[18:24, LANES:] = jnp.where(lane < 96, piece[6:12, :], pltpu.roll(third, 64, 1))
    extra[0:6, LANES:] = jnp.where(lane >= 112, pltpu.roll(third, 48, 1), 0.0)
    extra[6:12, LANES:] = jnp.where(lane >= 112, pltpu.roll(third, 32, 1), 0.0)
    out[...] = (dot(place, x[...], NT).reshape(NO, ROWS, 256) + extra[...][None]).astype(BF16)


def join_cabs(counts, pairs, cabs_hbm, out, slots, cabs, sem):
    copy = pltpu.make_async_copy(cabs_hbm, cabs, sem)
    copy.start()
    slots[...] = jnp.zeros(slots.shape, F32)
    slots[1:3, 0:40] = pairs[...].astype(F32)
    slots[3:4, :] = jnp.broadcast_to(counts[0].astype(F32), (1, LANES))
    copy.wait()
    for q in range(NC):
        out[NI * q : NI * (q + 1), :] = cabs[q]


def partial_t(got, weight, cabs, fit_hbm, out, a_fit, a_cab, own, fit, sems):
    spans = [pl.ds(GROUP * g, GROUP) for g in range(3)]
    copies = [pltpu.make_async_copy(fit_hbm.at[:, s], fit.at[:, s], sems.at[g]) for g, s in enumerate(spans)]
    for c in copies:
        c.start()
    messages = got[...].reshape(NO * ROWS, 256)
    first = lax.axis_index("pair") & 1

    def picked(step, start):
        count = NO // step
        shape = (NI, count, NO * ROWS)
        pick = iota(shape, 2) == ROWS * slot_of(step * iota(shape, 1) + start) + iota(shape, 0)
        pick = jnp.where(pick, 1.0, 0.0).reshape(NI * count, NO * ROWS).astype(BF16)
        rows = dot(pick, messages)
        return [[rows[count * t : count * (t + 1), LANES * h : LANES * (h + 1)] for h in (0, 1)] for t in range(NI)]

    amps, fifth = picked(1, 0), picked(2, first)

    def lay(width, start, store):
        per = LANES // width
        for jj in range(NJ):
            tiles = amps if jj < 4 else fifth
            count = tiles[0][0].shape[0]
            lane = iota((count, LANES), 1)
            half, off = divmod(start + width * jj, LANES)
            for m in range(-(-NI // per)):
                tile = jnp.zeros((count, LANES), F32)
                for k in range(min(per, NI - m * per)):
                    moved = tiles[m * per + k][half]
                    if (width * k - off) % LANES:
                        moved = pltpu.roll(moved, (width * k - off) % LANES, 1)
                    tile = jnp.where((lane >= width * k) & (lane < width * (k + 1)), moved, tile)
                store[NO * jj : NO * jj + count, LANES * m : LANES * (m + 1)] = tile.astype(BF16)

    lay(NF, 0, a_fit)
    lay(CQ, NJ * NF, a_cab)
    shape = (3 * LANES, 2 * LANES)
    source, target = iota(shape, 0), iota(shape, 1)
    q = (target * 3641) >> 16
    order = one_hot((q == (source & 15)) & (target - NI * q == (source >> 4)))
    a_cab[:, : 2 * LANES] = (dot(a_cab[...], order) * weight[...]).astype(BF16)

    def pack_coefficients():
        shape = (NO * NI, NO * ROWS)
        row, source = iota(shape, 0), iota(shape, 1)
        occ = (row * 3641) >> 16
        rest = row - NI * occ
        sixth = rest - jnp.where(rest >= 12, 12, jnp.where(rest >= 6, 6, 0))
        base = source - ROWS * slot_of(occ) - sixth
        main = dot(one_hot(base == 18), messages)
        spare0 = dot(one_hot(base == 0), messages[:, LANES:])
        spare1 = dot(one_hot(base == 6), messages[:, LANES:])
        shape = (NO * NI, LANES)
        lane, row = iota(shape, 1), iota(shape, 0)
        rest = row - NI * ((row * 3641) >> 16)
        third = jnp.where(lane < 32, pltpu.roll(main[:, :LANES], 32, 1), pltpu.roll(main[:, LANES:], 64, 1))
        third = jnp.where(lane < 64, third, pltpu.roll(spare0, 80, 1))
        third = jnp.where(lane < 80, third, pltpu.roll(spare1, 96, 1))
        coef = jnp.where(rest < 6, main[:, :LANES], jnp.where(rest < 12, main[:, LANES:], third))
        last = coef[3 * TJ :]
        lane = iota((TJ, LANES), 1)
        for b in range(3):
            moved = pltpu.roll(last, 96 - 32 * b, 1)
            own[TJ * b : TJ * (b + 1), :] = jnp.where(lane < 96, coef[TJ * b : TJ * (b + 1)], moved)
        packed = own[0:192, :].astype(BF16)
        for p in range(NA):
            out[p, SROWS - 192 :, :] = packed

    for g in range(3):
        copies[g].wait()
        total = dot(a_fit[:, : NI * NF], fit[:, spans[g]]) + dot(a_cab[:, : NI * NC], cabs[:, spans[g]])
        if g == 0:
            pack_coefficients()
        pieces = swap_pieces([total[:, LANES * k : LANES * (k + 1)] for k in range(8)], 16)
        for k in range(8):
            rows = jnp.concatenate([pieces[k], own[192 + 8 * g : 200 + 8 * g, :]], axis=0)
            out[k, (TJ + 8) * g : (TJ + 8) * (g + 1), :] = rows.astype(BF16)


def scale_of(top):
    top = jnp.max(jnp.max(top, axis=1, keepdims=True), axis=0, keepdims=True)
    power = jnp.ceil(jnp.log(jnp.maximum(top, 1e-30)) * (1.0 / LN2))
    return power, jnp.exp(power * -LN2) * 16384.0


def unscale(power):
    return jnp.exp(power * LN2) * (1.0 / 16384.0)


def sum_aux(slots, got, out):
    total = jnp.sum(got[:, 0 : 3 * (TJ + 8), :].astype(F32), axis=0)
    total = jnp.concatenate([total[(TJ + 8) * g : (TJ + 8) * g + TJ] for g in range(3)], axis=0)
    power, factor = scale_of(jnp.abs(total))
    out[0:TROWS, :] = total * factor
    out[TROWS:, :] = jnp.where(iota((8, LANES), 0) == 0, power, slots[...])


def all_blocks(lens, got, coefs, out, ints, words, tmat, dmat, msg, sem):
    aux, pair = lax.axis_index("aux"), lax.axis_index("pair")
    for y in range(NP):
        ints[8 * y : 8 * (y + 1), :] = got[y, TROWS : TROWS + 8, :].astype(jnp.int32)
    copy = pltpu.make_async_copy(ints, words, sem)
    copy.start()

    lane = iota((1, LANES), 1)
    for g in range(3):
        limit = jnp.zeros((1, LANES), jnp.int32)
        for k in range(8):
            limit = jnp.where((lane >> 4) == k, lens[8 * g + k], limit)
        kept = (lane & 15) + 16 * aux < limit
        for y in range(NP):
            part = got[y, TJ * g : TJ * (g + 1), :] * unscale(got[y, TROWS : TROWS + 1, :])
            part = jnp.where(kept, part, 0.0)
            high = part.astype(BF16).astype(F32)
            tmat[TJ * y : TJ * (y + 1), LANES * g : LANES * (g + 1)] = high
            tmat[TJ * y : TJ * (y + 1), LANES * (g + 3) : LANES * (g + 4)] = part - high
    shape = (NP, TJ, NO * NI)
    y, row = iota(shape, 0), iota(shape, 1)
    fifth = row >= 4 * NO
    occ = jnp.where(fifth, 2 * (row - 4 * NO) + (y & 1), row & (NO - 1))
    j = first_column(occ, y) + jnp.where(fifth, 4, row >> 4)
    pick = jnp.where(iota(shape, 2) == NI * occ + j, 1.0, 0.0)
    pick = pick.reshape(NP * TJ, NO * NI).astype(BF16)
    ordered = dot(pick, tmat[...].astype(BF16), TN).astype(BF16)

    for p in range(NA):
        limit = jnp.zeros((1, LANES), jnp.int32)
        for k in range(3):
            limit = jnp.where((lane >> 5) == k, lens[3 * p + k], limit)
        kept = 8 * (lane & 15) + 2 * pair + ((lane >> 4) & 1) < limit
        packed = coefs[p].astype(F32)
        spare = [packed[(TJ + 8) * g + TJ : (TJ + 8) * (g + 1)] for g in range(3)]
        packed = jnp.concatenate([packed[SROWS - 192 :]] + spare, axis=0)
        rows = [packed[TJ * b : TJ * (b + 1)] for b in range(3)]
        last = pltpu.roll(rows[0], 32, 1)
        last = jnp.where(lane >= 32, pltpu.roll(rows[1], 64, 1), last)
        last = jnp.where(lane >= 64, pltpu.roll(rows[2], 96, 1), last)
        coef = jnp.concatenate(rows + [last], axis=0)
        coef = jnp.where(kept, coef, 0.0).astype(BF16)
        blocks = dot(coef, ordered, TN)
        blocks = blocks[:, : 3 * LANES] + blocks[:, 3 * LANES :]
        for g in range(3):
            dmat[g, LANES * p : LANES * (p + 1), :] = blocks[:, LANES * g : LANES * (g + 1)]

    copy.wait()
    lane = iota((32, LANES), 1)
    top = jnp.zeros((32, LANES), F32)
    for q in range(20):
        y = q // 5
        count = words[8 * y + 3, 0]
        tile = jnp.zeros((32, LANES), F32)
        for k in range(8):
            slot = 8 * (q % 5) + k
            a, b = words[8 * y + 1, slot], words[8 * y + 2, slot]
            third = (a * 171) >> 9
            start = pl.multiple_of(LANES * third + 32 * (a - 3 * third), 32)
            block = dmat[b >> 3, pl.ds(start, 32), :]
            block = pltpu.roll(block, (16 * (k + 8 - (b & 7))) & 127, 1)
            end = jnp.where(slot < count, 16 * (k + 1), 0)
            tile = jnp.where((lane >= 16 * k) & (lane < end), block, tile)
        top = jnp.maximum(top, jnp.abs(tile))
        for e in range(2):
            msg[pl.ds(2 * q + e, NO, stride=48), :] = tile[NO * e : NO * (e + 1)]
    power, factor = scale_of(top)
    row = iota((48, LANES), 0)
    for o in range(NO):
        scaled = jnp.where(row < 40, msg[48 * o : 48 * (o + 1), :] * factor, 0.0)
        out[slot_of(o)] = jnp.where(row == 40, power, scaled)


def sum_occ(got, out, total):
    blocks = sum(got[o, 0:40, :] * unscale(got[o, 40:41, :]) for o in range(NO))
    power, factor = scale_of(jnp.abs(blocks))
    total[...] = blocks * factor
    rest = jnp.where(iota((6, LANES), 0) == 0, power, 0.0)
    for y in range(NP):
        rows = total[10 * y : 10 * (y + 1), :]
        for p in range(NA):
            out[NA * y + p, 0:10, :] = rows
            out[NA * y + p, 10:16, :] = rest


def unpack(got, out, rows):
    for y in range(NP):
        for p in range(NA):
            part = got[NA * y + p]
            part = part * unscale(part[10:11, :])
            for q in range(5):
                rows[q, p, 2 * y : 2 * y + 2, :] = part[2 * q : 2 * q + 2, :]
    for q in range(5):
        blocks = swap_pieces([rows[q, p] for p in range(NA)], 16)
        for k in range(8):
            out[8 * q + k] = blocks[k]


def exchange(x, axes, groups=None):
    return lax.all_to_all(x, axes, split_axis=0, concat_axis=0, tiled=True, axis_index_groups=groups)


def shape_of(shape, dtype):
    return jax.ShapeDtypeStruct(shape, dtype)


def on_device(amp_fit, amp_cabs, coef, f12_weight, ints_fit, ints_cabs, shell_len, pair_blocks, pair_count):
    weight = jnp.pad(jnp.tile(f12_weight, NC), (0, 2 * LANES - NI * NC))[None, :]

    sent = pl.pallas_call(
        pack_amps,
        out_shape=shape_of((NO, ROWS, 256), BF16),
        in_specs=[ANY] * 3,
        out_specs=vmem(1)[0],
        scratch_shapes=[
            pltpu.VMEM((NJ, NF, NO * NI), BF16),
            pltpu.VMEM((NC, NI, NO * NI), BF16),
            pltpu.VMEM((NI, 3 * LANES), BF16),
            pltpu.VMEM((24 * NC, NO * NI), F32),
            pltpu.VMEM((256, NO * NI), BF16),
            pltpu.VMEM((ROWS, 256), F32),
            pltpu.VMEM((NI, LANES), F32),
            pltpu.SemaphoreType.DMA((4,)),
        ],
        compiler_params=room(60),
    )(jnp.transpose(amp_fit, (2, 0, 1)), jnp.transpose(amp_cabs, (0, 2, 1)), coef)
    amps = exchange(sent, "occ", FROM_ROOT)

    cabs, slots = pl.pallas_call(
        join_cabs,
        out_shape=[shape_of((NC * NI, 24 * LANES), BF16), shape_of((8, LANES), F32)],
        in_specs=[SMEM] + vmem(1) + [ANY],
        out_specs=vmem(2),
        scratch_shapes=[pltpu.VMEM((NC, NI, 24 * LANES), BF16), pltpu.SemaphoreType.DMA],
        compiler_params=room(51),
        cost_estimate=pl.CostEstimate(flops=0, bytes_accessed=5_000_000, transcendentals=0),
    )(pair_count, pair_blocks.T, ints_cabs)
    sent = pl.pallas_call(
        partial_t,
        out_shape=shape_of((NA, SROWS, LANES), BF16),
        in_specs=vmem(3) + [ANY],
        out_specs=vmem(1)[0],
        scratch_shapes=[
            pltpu.VMEM((TJ, 5 * LANES), BF16),
            pltpu.VMEM((TJ, 3 * LANES), BF16),
            pltpu.VMEM((CROWS, LANES), F32),
            pltpu.VMEM((NI * NF, 24 * LANES), BF16),
            pltpu.SemaphoreType.DMA((3,)),
        ],
        compiler_params=room(49),
    )(amps, weight, cabs, jnp.transpose(ints_fit, (1, 0, 2)).reshape(NI * NF, 24 * LANES))
    shares = exchange(sent, "aux")

    sent = pl.pallas_call(
        sum_aux,
        out_shape=shape_of((TROWS + 8, LANES), F32),
        in_specs=vmem(2),
        out_specs=vmem(1)[0],
        compiler_params=PARAMS,
    )(slots, shares)
    sent = jnp.broadcast_to(sent.astype(F16)[None], (NP, TROWS + 8, LANES))
    got = exchange(sent, "pair").astype(F32)

    sent = pl.pallas_call(
        all_blocks,
        out_shape=shape_of((NO, 48, LANES), F32),
        in_specs=[SMEM] + vmem(2),
        out_specs=vmem(1)[0],
        scratch_shapes=[
            pltpu.VMEM((8 * NP, LANES), jnp.int32),
            pltpu.SMEM((8 * NP, LANES), jnp.int32),
            pltpu.VMEM((NP * TJ, 6 * LANES), F32),
            pltpu.VMEM((3, 8 * LANES, LANES), F32),
            pltpu.VMEM((NO * 48, LANES), F32),
            pltpu.SemaphoreType.DMA,
        ],
        compiler_params=PARAMS,
    )(shell_len, got, shares)
    got = exchange(sent.astype(F16), "occ", FROM_ROOT).astype(F32)

    sent = pl.pallas_call(
        sum_occ,
        out_shape=shape_of((NP * NA, 16, LANES), F32),
        in_specs=vmem(1),
        out_specs=vmem(1)[0],
        scratch_shapes=[pltpu.VMEM((40, LANES), F32)],
        compiler_params=PARAMS,
    )(got)
    got = exchange(sent.astype(F16), ("pair", "aux")).astype(F32)

    return pl.pallas_call(
        unpack,
        out_shape=shape_of((40, 8, LANES), F32),
        in_specs=vmem(1),
        out_specs=vmem(1)[0],
        scratch_shapes=[pltpu.VMEM((5, NA, 8, LANES), F32)],
        compiler_params=PARAMS,
    )(got)


def solution(mesh):
    placed = (
        P("aux", None, "occ"),
        P("aux", None, "occ"),
        P("occ", None),
        P("occ"),
        P("aux", "occ", None),
        P("aux", "occ", None),
        P(),
        P("pair", None),
        P("pair"),
    )
    return jax.shard_map(
        on_device, mesh=mesh, in_specs=placed, out_specs=P("pair", "occ", None), check_vma=False
    )
```

```python
import functools
import math

import jax
import jax.numpy as jnp
from jax import lax
from jax.experimental import pallas as pl
from jax.experimental.pallas import tpu as pltpu
from jax.sharding import PartitionSpec as P

F32, BF16, F16 = jnp.float32, jnp.bfloat16, jnp.float16
LANES = 128
LN2 = math.log(2.0)
NT = (((1,), (1,)), ((), ()))
TN = (((0,), (0,)), ((), ()))


def iota(shape, dim):
    return lax.broadcasted_iota(jnp.int32, shape, dim)


def dot(a, b, dims=(((1,), (0,)), ((), ()))):
    return lax.dot_general(a, b, dims, preferred_element_type=F32)


def one_hot(cond):
    return jnp.where(cond, 1.0, 0.0).astype(BF16)


def swap_pieces(xs, piece):
    lane = iota(xs[0].shape, 1)
    bit = 1
    while bit < len(xs):
        keep = ((lane // piece) & bit) == 0
        ys = list(xs)
        for k in range(len(xs)):
            if k & bit == 0:
                lo, hi = xs[k], xs[k + bit]
                ys[k] = jnp.where(keep, lo, pltpu.roll(hi, piece * bit, 1))
                ys[k + bit] = jnp.where(keep, pltpu.roll(lo, LANES - piece * bit, 1), hi)
        xs = ys
        bit *= 2
    return xs


def vmem(n):
    return [pl.BlockSpec(memory_space=pltpu.VMEM)] * n


SMEM = pl.BlockSpec(memory_space=pltpu.SMEM)
ANY = pl.BlockSpec(memory_space=pl.ANY)

def room(mib):
    return pltpu.CompilerParams(vmem_limit_bytes=mib * 1024 * 1024)


PARAMS = room(40)


NO, NI, NA, NP, NF, NC, NJ = 16, 18, 8, 4, 32, 12, 5
CQ = 16
TJ = 72
GROUP = 8 * LANES
TROWS = 3 * TJ
ROOT, STEP, BACK = 11, 7, 7
FROM_ROOT = [[(STEP * k + ROOT) % NO for k in range(NO)]]
FROM_AUX = [[(k + 6) % NA for k in range(NA)]]
FROM_PAIR = [[(k + 3) % NP for k in range(NP)]]
FROM_BOTH = [[NA * y + p for y in FROM_PAIR[0] for p in FROM_AUX[0]]]
ROWS = 24
CROWS = 216
SROWS = 3 * (TJ + 8) + 192


def slot_of(occ):
    return (BACK * (occ + NO - ROOT)) & (NO - 1)


def aux_slot(aux):
    return (aux + NA - 6) % NA


def pair_slot(pair):
    return (pair + NP - 3) % NP


def both_slot(pair, aux):
    return NA * pair_slot(pair) + aux_slot(aux)


def first_column(occ, pair):
    return (9 * pair + 1 - (occ & 1)) >> 1


def pack_amps(fit_hbm, cabs_hbm, coef_hbm, out, fit, cabs, coef, cab32, x, extra, piece, sems):
    aux, pair = lax.axis_index("aux"), lax.axis_index("pair")
    first_j = first_column(lax.axis_index("occ"), pair)
    fifth_j = jnp.minimum(first_j + 4, NI - 1)
    columns = pl.ds(pl.multiple_of(3 * LANES * aux, LANES), 3 * LANES)
    copies = [
        pltpu.make_async_copy(cabs_hbm, cabs, sems.at[0]),
        pltpu.make_async_copy(fit_hbm.at[pl.ds(first_j, 4)], fit.at[pl.ds(0, 4)], sems.at[1]),
        pltpu.make_async_copy(fit_hbm.at[pl.ds(fifth_j, 1)], fit.at[pl.ds(4, 1)], sems.at[2]),
        pltpu.make_async_copy(coef_hbm.at[:, columns], coef, sems.at[3]),
    ]
    for c in copies:
        c.start()
    shape = (NO, ROWS, NO * NI)
    t = iota(shape, 1)
    place = jnp.where((iota(shape, 2) == NI * ((STEP * iota(shape, 0) + ROOT) & (NO - 1)) + t) & (t < NI), 1.0, 0.0)
    place = place.reshape(NO * ROWS, NO * NI).astype(BF16)
    source, target = iota((LANES, LANES), 0), iota((LANES, LANES), 1)
    mine = source == 8 * (target & 15) + 2 * pair + ((target >> 4) & 1)
    for c in copies:
        c.wait()
    x[0 : NJ * NF, :] = fit[...].reshape(NJ * NF, NO * NI)
    for q in range(NC):
        cab32[24 * q : 24 * q + NI, :] = cabs[q].astype(F32)
    zero = jnp.zeros((CQ - NC, NO * NI), F32)
    for jj in range(NJ):
        j = fifth_j if jj == 4 else first_j + jj
        picked = [cab32[pl.ds(24 * q + j, 1), :] for q in range(NC)]
        rows = jnp.concatenate(picked + [zero], axis=0)
        x[NJ * NF + CQ * jj : NJ * NF + CQ * (jj + 1), :] = rows.astype(BF16)
    x[NJ * (NF + CQ) :, :] = jnp.zeros((256 - NJ * (NF + CQ), NO * NI), BF16)
    piece[...] = sum(
        dot(coef[:, LANES * k : LANES * (k + 1)], one_hot(mine & ((target >> 5) == k))) for k in range(3)
    )
    lane = iota((6, LANES), 1)
    third = piece[12:18, :]
    extra[...] = jnp.zeros(extra.shape, F32)
    extra[18:24, 0:LANES] = jnp.where(lane < 96, piece[0:6, :], pltpu.roll(third, 96, 1))
    extra[18:24, LANES:] = jnp.where(lane < 96, piece[6:12, :], pltpu.roll(third, 64, 1))
    extra[0:6, LANES:] = jnp.where(lane >= 112, pltpu.roll(third, 48, 1), 0.0)
    extra[6:12, LANES:] = jnp.where(lane >= 112, pltpu.roll(third, 32, 1), 0.0)
    out[...] = (dot(place, x[...], NT).reshape(NO, ROWS, 256) + extra[...][None]).astype(BF16)


def join_cabs(counts, pairs, cabs_hbm, out, slots, cabs, sem):
    copy = pltpu.make_async_copy(cabs_hbm, cabs, sem)
    copy.start()
    slots[...] = jnp.zeros(slots.shape, F32)
    slots[1:3, 0:40] = pairs[...].astype(F32)
    slots[3:4, :] = jnp.broadcast_to(counts[0].astype(F32), (1, LANES))
    copy.wait()
    for q in range(NC):
        out[NI * q : NI * (q + 1), :] = cabs[q]


def partial_t(got, weight, cabs, fit_hbm, out, a_fit, a_cab, own, fit, sems):
    spans = [pl.ds(GROUP * g, GROUP) for g in range(3)]
    copies = [pltpu.make_async_copy(fit_hbm.at[:, s], fit.at[:, s], sems.at[g]) for g, s in enumerate(spans)]
    for c in copies:
        c.start()
    messages = got[...].reshape(NO * ROWS, 256)
    first = lax.axis_index("pair") & 1

    def picked(step, start):
        count = NO // step
        shape = (NI, count, NO * ROWS)
        pick = iota(shape, 2) == ROWS * slot_of(step * iota(shape, 1) + start) + iota(shape, 0)
        pick = jnp.where(pick, 1.0, 0.0).reshape(NI * count, NO * ROWS).astype(BF16)
        rows = dot(pick, messages)
        return [[rows[count * t : count * (t + 1), LANES * h : LANES * (h + 1)] for h in (0, 1)] for t in range(NI)]

    amps, fifth = picked(1, 0), picked(2, first)

    def lay(width, start, store):
        per = LANES // width
        for jj in range(NJ):
            tiles = amps if jj < 4 else fifth
            count = tiles[0][0].shape[0]
            lane = iota((count, LANES), 1)
            half, off = divmod(start + width * jj, LANES)
            for m in range(-(-NI // per)):
                tile = jnp.zeros((count, LANES), F32)
                for k in range(min(per, NI - m * per)):
                    moved = tiles[m * per + k][half]
                    if (width * k - off) % LANES:
                        moved = pltpu.roll(moved, (width * k - off) % LANES, 1)
                    tile = jnp.where((lane >= width * k) & (lane < width * (k + 1)), moved, tile)
                store[NO * jj : NO * jj + count, LANES * m : LANES * (m + 1)] = tile.astype(BF16)

    lay(NF, 0, a_fit)
    lay(CQ, NJ * NF, a_cab)
    shape = (3 * LANES, 2 * LANES)
    source, target = iota(shape, 0), iota(shape, 1)
    q = (target * 3641) >> 16
    order = one_hot((q == (source & 15)) & (target - NI * q == (source >> 4)))
    a_cab[:, : 2 * LANES] = (dot(a_cab[...], order) * weight[...]).astype(BF16)

    def pack_coefficients():
        shape = (NO * NI, NO * ROWS)
        row, source = iota(shape, 0), iota(shape, 1)
        occ = (row * 3641) >> 16
        rest = row - NI * occ
        sixth = rest - jnp.where(rest >= 12, 12, jnp.where(rest >= 6, 6, 0))
        base = source - ROWS * slot_of(occ) - sixth
        main = dot(one_hot(base == 18), messages)
        spare0 = dot(one_hot(base == 0), messages[:, LANES:])
        spare1 = dot(one_hot(base == 6), messages[:, LANES:])
        shape = (NO * NI, LANES)
        lane, row = iota(shape, 1), iota(shape, 0)
        rest = row - NI * ((row * 3641) >> 16)
        third = jnp.where(lane < 32, pltpu.roll(main[:, :LANES], 32, 1), pltpu.roll(main[:, LANES:], 64, 1))
        third = jnp.where(lane < 64, third, pltpu.roll(spare0, 80, 1))
        third = jnp.where(lane < 80, third, pltpu.roll(spare1, 96, 1))
        coef = jnp.where(rest < 6, main[:, :LANES], jnp.where(rest < 12, main[:, LANES:], third))
        last = coef[3 * TJ :]
        lane = iota((TJ, LANES), 1)
        for b in range(3):
            moved = pltpu.roll(last, 96 - 32 * b, 1)
            own[TJ * b : TJ * (b + 1), :] = jnp.where(lane < 96, coef[TJ * b : TJ * (b + 1)], moved)
        packed = own[0:192, :].astype(BF16)
        for p in range(NA):
            out[p, SROWS - 192 :, :] = packed

    for g in range(3):
        copies[g].wait()
        total = dot(a_fit[:, : NI * NF], fit[:, spans[g]]) + dot(a_cab[:, : NI * NC], cabs[:, spans[g]])
        if g == 0:
            pack_coefficients()
        pieces = swap_pieces([total[:, LANES * k : LANES * (k + 1)] for k in range(8)], 16)
        for k in range(8):
            rows = jnp.concatenate([pieces[k], own[192 + 8 * g : 200 + 8 * g, :]], axis=0)
            out[aux_slot(k), (TJ + 8) * g : (TJ + 8) * (g + 1), :] = rows.astype(BF16)


def scale_of(top):
    top = jnp.max(jnp.max(top, axis=1, keepdims=True), axis=0, keepdims=True)
    power = jnp.ceil(jnp.log(jnp.maximum(top, 1e-30)) * (1.0 / LN2))
    return power, jnp.exp(power * -LN2) * 16384.0


def unscale(power):
    return jnp.exp(power * LN2) * (1.0 / 16384.0)


def sum_aux(slots, got, out):
    total = jnp.sum(got[:, 0 : 3 * (TJ + 8), :].astype(F32), axis=0)
    total = jnp.concatenate([total[(TJ + 8) * g : (TJ + 8) * g + TJ] for g in range(3)], axis=0)
    power, factor = scale_of(jnp.abs(total))
    out[0:TROWS, :] = total * factor
    out[TROWS:, :] = jnp.where(iota((8, LANES), 0) == 0, power, slots[...])


def all_blocks(lens, got, coefs, out, ints, words, tmat, dmat, msg, sem):
    aux, pair = lax.axis_index("aux"), lax.axis_index("pair")
    for y in range(NP):
        ints[8 * y : 8 * (y + 1), :] = got[pair_slot(y), TROWS : TROWS + 8, :].astype(jnp.int32)
    copy = pltpu.make_async_copy(ints, words, sem)
    copy.start()

    lane = iota((1, LANES), 1)
    for g in range(3):
        limit = jnp.zeros((1, LANES), jnp.int32)
        for k in range(8):
            limit = jnp.where((lane >> 4) == k, lens[8 * g + k], limit)
        kept = (lane & 15) + 16 * aux < limit
        for y in range(NP):
            slot = pair_slot(y)
            part = got[slot, TJ * g : TJ * (g + 1), :] * unscale(got[slot, TROWS : TROWS + 1, :])
            part = jnp.where(kept, part, 0.0)
            high = part.astype(BF16).astype(F32)
            tmat[TJ * y : TJ * (y + 1), LANES * g : LANES * (g + 1)] = high
            tmat[TJ * y : TJ * (y + 1), LANES * (g + 3) : LANES * (g + 4)] = part - high
    shape = (NP, TJ, NO * NI)
    y, row = iota(shape, 0), iota(shape, 1)
    fifth = row >= 4 * NO
    occ = jnp.where(fifth, 2 * (row - 4 * NO) + (y & 1), row & (NO - 1))
    j = first_column(occ, y) + jnp.where(fifth, 4, row >> 4)
    pick = jnp.where(iota(shape, 2) == NI * occ + j, 1.0, 0.0)
    pick = pick.reshape(NP * TJ, NO * NI).astype(BF16)
    ordered = dot(pick, tmat[...].astype(BF16), TN).astype(BF16)

    for p in range(NA):
        limit = jnp.zeros((1, LANES), jnp.int32)
        for k in range(3):
            limit = jnp.where((lane >> 5) == k, lens[3 * p + k], limit)
        kept = 8 * (lane & 15) + 2 * pair + ((lane >> 4) & 1) < limit
        packed = coefs[aux_slot(p)].astype(F32)
        spare = [packed[(TJ + 8) * g + TJ : (TJ + 8) * (g + 1)] for g in range(3)]
        packed = jnp.concatenate([packed[SROWS - 192 :]] + spare, axis=0)
        rows = [packed[TJ * b : TJ * (b + 1)] for b in range(3)]
        last = pltpu.roll(rows[0], 32, 1)
        last = jnp.where(lane >= 32, pltpu.roll(rows[1], 64, 1), last)
        last = jnp.where(lane >= 64, pltpu.roll(rows[2], 96, 1), last)
        coef = jnp.concatenate(rows + [last], axis=0)
        coef = jnp.where(kept, coef, 0.0).astype(BF16)
        blocks = dot(coef, ordered, TN)
        blocks = blocks[:, : 3 * LANES] + blocks[:, 3 * LANES :]
        for g in range(3):
            dmat[g, LANES * p : LANES * (p + 1), :] = blocks[:, LANES * g : LANES * (g + 1)]

    copy.wait()
    lane = iota((32, LANES), 1)
    top = jnp.zeros((32, LANES), F32)
    for q in range(20):
        y = q // 5
        count = words[8 * y + 3, 0]
        tile = jnp.zeros((32, LANES), F32)
        for k in range(8):
            slot = 8 * (q % 5) + k
            a, b = words[8 * y + 1, slot], words[8 * y + 2, slot]
            third = (a * 171) >> 9
            start = pl.multiple_of(LANES * third + 32 * (a - 3 * third), 32)
            block = dmat[b >> 3, pl.ds(start, 32), :]
            block = pltpu.roll(block, (16 * (k + 8 - (b & 7))) & 127, 1)
            end = jnp.where(slot < count, 16 * (k + 1), 0)
            tile = jnp.where((lane >= 16 * k) & (lane < end), block, tile)
        top = jnp.maximum(top, jnp.abs(tile))
        for e in range(2):
            msg[pl.ds(2 * q + e, NO, stride=48), :] = tile[NO * e : NO * (e + 1)]
    power, factor = scale_of(top)
    row = iota((48, LANES), 0)
    for o in range(NO):
        scaled = jnp.where(row < 40, msg[48 * o : 48 * (o + 1), :] * factor, 0.0)
        out[slot_of(o)] = jnp.where(row == 40, power, scaled)


def sum_occ(got, out, total):
    blocks = sum(got[o, 0:40, :] * unscale(got[o, 40:41, :]) for o in range(NO))
    power, factor = scale_of(jnp.abs(blocks))
    total[...] = blocks * factor
    rest = jnp.where(iota((6, LANES), 0) == 0, power, 0.0)
    for y in range(NP):
        rows = total[10 * y : 10 * (y + 1), :]
        for p in range(NA):
            out[both_slot(y, p), 0:10, :] = rows
            out[both_slot(y, p), 10:16, :] = rest


def unpack(got, out, rows):
    for y in range(NP):
        for p in range(NA):
            part = got[both_slot(y, p)]
            part = part * unscale(part[10:11, :])
            for q in range(5):
                rows[q, p, 2 * y : 2 * y + 2, :] = part[2 * q : 2 * q + 2, :]
    for q in range(5):
        blocks = swap_pieces([rows[q, p] for p in range(NA)], 16)
        for k in range(8):
            out[8 * q + k] = blocks[k]


def exchange(x, axes, groups=None):
    return lax.all_to_all(x, axes, split_axis=0, concat_axis=0, tiled=True, axis_index_groups=groups)


def shape_of(shape, dtype):
    return jax.ShapeDtypeStruct(shape, dtype)


def on_device(amp_fit, amp_cabs, coef, f12_weight, ints_fit, ints_cabs, shell_len, pair_blocks, pair_count):
    weight = jnp.pad(jnp.tile(f12_weight, NC), (0, 2 * LANES - NI * NC))[None, :]

    sent = pl.pallas_call(
        pack_amps,
        out_shape=shape_of((NO, ROWS, 256), BF16),
        in_specs=[ANY] * 3,
        out_specs=vmem(1)[0],
        scratch_shapes=[
            pltpu.VMEM((NJ, NF, NO * NI), BF16),
            pltpu.VMEM((NC, NI, NO * NI), BF16),
            pltpu.VMEM((NI, 3 * LANES), BF16),
            pltpu.VMEM((24 * NC, NO * NI), F32),
            pltpu.VMEM((256, NO * NI), BF16),
            pltpu.VMEM((ROWS, 256), F32),
            pltpu.VMEM((NI, LANES), F32),
            pltpu.SemaphoreType.DMA((4,)),
        ],
        compiler_params=room(60),
    )(jnp.transpose(amp_fit, (2, 0, 1)), jnp.transpose(amp_cabs, (0, 2, 1)), coef)
    amps = exchange(sent, "occ", FROM_ROOT)

    cabs, slots = pl.pallas_call(
        join_cabs,
        out_shape=[shape_of((NC * NI, 24 * LANES), BF16), shape_of((8, LANES), F32)],
        in_specs=[SMEM] + vmem(1) + [ANY],
        out_specs=vmem(2),
        scratch_shapes=[pltpu.VMEM((NC, NI, 24 * LANES), BF16), pltpu.SemaphoreType.DMA],
        compiler_params=room(51),
        cost_estimate=pl.CostEstimate(flops=0, bytes_accessed=5_000_000, transcendentals=0),
    )(pair_count, pair_blocks.T, ints_cabs)
    sent = pl.pallas_call(
        partial_t,
        out_shape=shape_of((NA, SROWS, LANES), BF16),
        in_specs=vmem(3) + [ANY],
        out_specs=vmem(1)[0],
        scratch_shapes=[
            pltpu.VMEM((TJ, 5 * LANES), BF16),
            pltpu.VMEM((TJ, 3 * LANES), BF16),
            pltpu.VMEM((CROWS, LANES), F32),
            pltpu.VMEM((NI * NF, 24 * LANES), BF16),
            pltpu.SemaphoreType.DMA((3,)),
        ],
        compiler_params=room(49),
    )(amps, weight, cabs, jnp.transpose(ints_fit, (1, 0, 2)).reshape(NI * NF, 24 * LANES))
    shares = exchange(sent, "aux", FROM_AUX)

    sent = pl.pallas_call(
        sum_aux,
        out_shape=shape_of((TROWS + 8, LANES), F32),
        in_specs=vmem(2),
        out_specs=vmem(1)[0],
        compiler_params=PARAMS,
    )(slots, shares)
    sent = jnp.broadcast_to(sent.astype(F16)[None], (NP, TROWS + 8, LANES))
    got = exchange(sent, "pair", FROM_PAIR).astype(F32)

    sent = pl.pallas_call(
        all_blocks,
        out_shape=shape_of((NO, 48, LANES), F32),
        in_specs=[SMEM] + vmem(2),
        out_specs=vmem(1)[0],
        scratch_shapes=[
            pltpu.VMEM((8 * NP, LANES), jnp.int32),
            pltpu.SMEM((8 * NP, LANES), jnp.int32),
            pltpu.VMEM((NP * TJ, 6 * LANES), F32),
            pltpu.VMEM((3, 8 * LANES, LANES), F32),
            pltpu.VMEM((NO * 48, LANES), F32),
            pltpu.SemaphoreType.DMA,
        ],
        compiler_params=PARAMS,
    )(shell_len, got, shares)
    got = exchange(sent.astype(F16), "occ", FROM_ROOT).astype(F32)

    sent = pl.pallas_call(
        sum_occ,
        out_shape=shape_of((NP * NA, 16, LANES), F32),
        in_specs=vmem(1),
        out_specs=vmem(1)[0],
        scratch_shapes=[pltpu.VMEM((40, LANES), F32)],
        compiler_params=PARAMS,
    )(got)
    got = exchange(sent.astype(F16), ("pair", "aux"), FROM_BOTH).astype(F32)

    return pl.pallas_call(
        unpack,
        out_shape=shape_of((40, 8, LANES), F32),
        in_specs=vmem(1),
        out_specs=vmem(1)[0],
        scratch_shapes=[pltpu.VMEM((5, NA, 8, LANES), F32)],
        compiler_params=PARAMS,
    )(got)


def solution(mesh):
    placed = (
        P("aux", None, "occ"),
        P("aux", None, "occ"),
        P("occ", None),
        P("occ"),
        P("aux", "occ", None),
        P("aux", "occ", None),
        P(),
        P("pair", None),
        P("pair"),
    )
    return jax.shard_map(
        on_device, mesh=mesh, in_specs=placed, out_specs=P("pair", "occ", None), check_vma=False
    )
```

```python
import functools
import math

import jax
import jax.numpy as jnp
from jax import lax
from jax.experimental import pallas as pl
from jax.experimental.pallas import tpu as pltpu
from jax.sharding import PartitionSpec as P

F32, BF16, F16 = jnp.float32, jnp.bfloat16, jnp.float16
LANES = 128
LN2 = math.log(2.0)
NT = (((1,), (1,)), ((), ()))
TN = (((0,), (0,)), ((), ()))


def iota(shape, dim):
    return lax.broadcasted_iota(jnp.int32, shape, dim)


def dot(a, b, dims=(((1,), (0,)), ((), ()))):
    return lax.dot_general(a, b, dims, preferred_element_type=F32)


def one_hot(cond):
    return jnp.where(cond, 1.0, 0.0).astype(BF16)


def swap_pieces(xs, piece):
    lane = iota(xs[0].shape, 1)
    bit = 1
    while bit < len(xs):
        keep = ((lane // piece) & bit) == 0
        ys = list(xs)
        for k in range(len(xs)):
            if k & bit == 0:
                lo, hi = xs[k], xs[k + bit]
                ys[k] = jnp.where(keep, lo, pltpu.roll(hi, piece * bit, 1))
                ys[k + bit] = jnp.where(keep, pltpu.roll(lo, LANES - piece * bit, 1), hi)
        xs = ys
        bit *= 2
    return xs


def vmem(n):
    return [pl.BlockSpec(memory_space=pltpu.VMEM)] * n


SMEM = pl.BlockSpec(memory_space=pltpu.SMEM)
ANY = pl.BlockSpec(memory_space=pl.ANY)

def room(mib):
    return pltpu.CompilerParams(vmem_limit_bytes=mib * 1024 * 1024)


PARAMS = room(40)


NO, NI, NA, NP, NF, NC, NJ = 16, 18, 8, 4, 32, 12, 5
CQ = 16
TJ = 72
GROUP = 8 * LANES
TROWS = 3 * TJ
ROOT, STEP, BACK = 11, 7, 7
FROM_ROOT = [[(STEP * k + ROOT) % NO for k in range(NO)]]
FROM_AUX = [[(k + 6) % NA for k in range(NA)]]
FROM_PAIR = [[(k + 3) % NP for k in range(NP)]]
FROM_BOTH = [[NA * y + p for y in FROM_PAIR[0] for p in FROM_AUX[0]]]
ROWS = 24
CROWS = 216
SROWS = TROWS + 8 + CROWS


def slot_of(occ):
    return (BACK * (occ + NO - ROOT)) & (NO - 1)


def aux_slot(aux):
    return (aux + NA - 6) % NA


def pair_slot(pair):
    return (pair + NP - 3) % NP


def both_slot(pair, aux):
    return NA * pair_slot(pair) + aux_slot(aux)


def first_column(occ, pair):
    return (9 * pair + 1 - (occ & 1)) >> 1


def pack_amps(fit_hbm, cabs_hbm, coef_hbm, out, fit, cabs, coef, cab32, x, extra, piece, sems):
    aux, pair = lax.axis_index("aux"), lax.axis_index("pair")
    first_j = first_column(lax.axis_index("occ"), pair)
    fifth_j = jnp.minimum(first_j + 4, NI - 1)
    columns = pl.ds(pl.multiple_of(3 * LANES * aux, LANES), 3 * LANES)
    copies = [
        pltpu.make_async_copy(cabs_hbm, cabs, sems.at[0]),
        pltpu.make_async_copy(fit_hbm.at[pl.ds(first_j, 4)], fit.at[pl.ds(0, 4)], sems.at[1]),
        pltpu.make_async_copy(fit_hbm.at[pl.ds(fifth_j, 1)], fit.at[pl.ds(4, 1)], sems.at[2]),
        pltpu.make_async_copy(coef_hbm.at[:, columns], coef, sems.at[3]),
    ]
    for c in copies:
        c.start()
    shape = (NO, ROWS, NO * NI)
    t = iota(shape, 1)
    place = jnp.where((iota(shape, 2) == NI * ((STEP * iota(shape, 0) + ROOT) & (NO - 1)) + t) & (t < NI), 1.0, 0.0)
    place = place.reshape(NO * ROWS, NO * NI).astype(BF16)
    source, target = iota((LANES, LANES), 0), iota((LANES, LANES), 1)
    mine = source == 8 * (target & 15) + 2 * pair + ((target >> 4) & 1)
    for c in copies:
        c.wait()
    x[0 : NJ * NF, :] = fit[...].reshape(NJ * NF, NO * NI)
    for q in range(NC):
        cab32[24 * q : 24 * q + NI, :] = cabs[q].astype(F32)
    zero = jnp.zeros((CQ - NC, NO * NI), F32)
    for jj in range(NJ):
        j = fifth_j if jj == 4 else first_j + jj
        picked = [cab32[pl.ds(24 * q + j, 1), :] for q in range(NC)]
        rows = jnp.concatenate(picked + [zero], axis=0)
        x[NJ * NF + CQ * jj : NJ * NF + CQ * (jj + 1), :] = rows.astype(BF16)
    x[NJ * (NF + CQ) :, :] = jnp.zeros((256 - NJ * (NF + CQ), NO * NI), BF16)
    piece[...] = sum(
        dot(coef[:, LANES * k : LANES * (k + 1)], one_hot(mine & ((target >> 5) == k))) for k in range(3)
    )
    lane = iota((6, LANES), 1)
    third = piece[12:18, :]
    extra[...] = jnp.zeros(extra.shape, F32)
    extra[18:24, 0:LANES] = jnp.where(lane < 96, piece[0:6, :], pltpu.roll(third, 96, 1))
    extra[18:24, LANES:] = jnp.where(lane < 96, piece[6:12, :], pltpu.roll(third, 64, 1))
    extra[0:6, LANES:] = jnp.where(lane >= 112, pltpu.roll(third, 48, 1), 0.0)
    extra[6:12, LANES:] = jnp.where(lane >= 112, pltpu.roll(third, 32, 1), 0.0)
    out[...] = (dot(place, x[...], NT).reshape(NO, ROWS, 256) + extra[...][None]).astype(BF16)


def join_cabs(counts, pairs, cabs_hbm, out, slots, cabs, sem):
    copy = pltpu.make_async_copy(cabs_hbm, cabs, sem)
    copy.start()
    slots[...] = jnp.zeros(slots.shape, F32)
    slots[1:3, 0:40] = pairs[...].astype(F32)
    slots[3:4, :] = jnp.broadcast_to(counts[0].astype(F32), (1, LANES))
    copy.wait()
    for q in range(NC):
        out[NI * q : NI * (q + 1), :] = cabs[q]


def partial_t(got, weight, cabs, fit_hbm, out, factors, a_fit, a_cab, own, fit, sems):
    spans = [pl.ds(GROUP * g, GROUP) for g in range(3)]
    copies = [pltpu.make_async_copy(fit_hbm.at[:, s], fit.at[:, s], sems.at[g]) for g, s in enumerate(spans)]
    for c in copies:
        c.start()
    messages = got[...].reshape(NO * ROWS, 256)
    first = lax.axis_index("pair") & 1

    def picked(step, start):
        count = NO // step
        shape = (NI, count, NO * ROWS)
        pick = iota(shape, 2) == ROWS * slot_of(step * iota(shape, 1) + start) + iota(shape, 0)
        pick = jnp.where(pick, 1.0, 0.0).reshape(NI * count, NO * ROWS).astype(BF16)
        rows = dot(pick, messages)
        return [[rows[count * t : count * (t + 1), LANES * h : LANES * (h + 1)] for h in (0, 1)] for t in range(NI)]

    amps, fifth = picked(1, 0), picked(2, first)

    def lay(width, start, store):
        per = LANES // width
        for jj in range(NJ):
            tiles = amps if jj < 4 else fifth
            count = tiles[0][0].shape[0]
            lane = iota((count, LANES), 1)
            half, off = divmod(start + width * jj, LANES)
            for m in range(-(-NI // per)):
                tile = jnp.zeros((count, LANES), F32)
                for k in range(min(per, NI - m * per)):
                    moved = tiles[m * per + k][half]
                    if (width * k - off) % LANES:
                        moved = pltpu.roll(moved, (width * k - off) % LANES, 1)
                    tile = jnp.where((lane >= width * k) & (lane < width * (k + 1)), moved, tile)
                store[NO * jj : NO * jj + count, LANES * m : LANES * (m + 1)] = tile.astype(BF16)

    lay(NF, 0, a_fit)
    lay(CQ, NJ * NF, a_cab)
    shape = (3 * LANES, 2 * LANES)
    source, target = iota(shape, 0), iota(shape, 1)
    q = (target * 3641) >> 16
    order = one_hot((q == (source & 15)) & (target - NI * q == (source >> 4)))
    a_cab[:, : 2 * LANES] = (dot(a_cab[...], order) * weight[...]).astype(BF16)

    def pack_coefficients():
        shape = (NO * NI, NO * ROWS)
        row, source = iota(shape, 0), iota(shape, 1)
        occ = (row * 3641) >> 16
        rest = row - NI * occ
        sixth = rest - jnp.where(rest >= 12, 12, jnp.where(rest >= 6, 6, 0))
        base = source - ROWS * slot_of(occ) - sixth
        main = dot(one_hot(base == 18), messages)
        spare0 = dot(one_hot(base == 0), messages[:, LANES:])
        spare1 = dot(one_hot(base == 6), messages[:, LANES:])
        shape = (NO * NI, LANES)
        lane, row = iota(shape, 1), iota(shape, 0)
        rest = row - NI * ((row * 3641) >> 16)
        third = jnp.where(lane < 32, pltpu.roll(main[:, :LANES], 32, 1), pltpu.roll(main[:, LANES:], 64, 1))
        third = jnp.where(lane < 64, third, pltpu.roll(spare0, 80, 1))
        third = jnp.where(lane < 80, third, pltpu.roll(spare1, 96, 1))
        coef = jnp.where(rest < 6, main[:, :LANES], jnp.where(rest < 12, main[:, LANES:], third))
        last = coef[3 * TJ :]
        lane = iota((TJ, LANES), 1)
        for b in range(3):
            moved = pltpu.roll(last, 96 - 32 * b, 1)
            own[TJ * b : TJ * (b + 1), :] = jnp.where(lane < 96, coef[TJ * b : TJ * (b + 1)], moved)
        for p in range(NA):
            out[p, TROWS + 8 :, :] = own[...]

    top = jnp.zeros((TJ, LANES), F32)

    for g in range(3):
        copies[g].wait()
        total = dot(a_fit[:, : NI * NF], fit[:, spans[g]]) + dot(a_cab[:, : NI * NC], cabs[:, spans[g]])
        if g == 0:
            pack_coefficients()
        pieces = swap_pieces([total[:, LANES * k : LANES * (k + 1)] for k in range(8)], 16)
        top = functools.reduce(jnp.maximum, [jnp.abs(piece) for piece in pieces], top)
        for k in range(8):
            out[aux_slot(k), TJ * g : TJ * (g + 1), :] = pieces[k]
    power_t, factor_t = scale_of(top)
    power_c, factor_c = scale_of(jnp.abs(own[...]))
    factors[0:TROWS, :] = jnp.broadcast_to(factor_t, (TROWS, LANES))
    factors[TROWS : TROWS + 8, :] = jnp.ones((8, LANES), F32)
    factors[TROWS + 8 :, :] = jnp.broadcast_to(factor_c, (CROWS, LANES))
    powers = jnp.where(iota((8, LANES), 0) == 0, power_t, power_c)
    for p in range(NA):
        out[p, TROWS : TROWS + 8, :] = powers


def scale_of(top):
    top = jnp.max(jnp.max(top, axis=1, keepdims=True), axis=0, keepdims=True)
    power = jnp.ceil(jnp.log(jnp.maximum(top, 1e-30)) * (1.0 / LN2))
    return power, jnp.exp(power * -LN2) * 16384.0


def unscale(power):
    return jnp.exp(power * LN2) * (1.0 / 16384.0)


def sum_aux(slots, got, out):
    total = sum(got[p, 0:TROWS, :] * unscale(got[p, TROWS : TROWS + 1, :]) for p in range(NA))
    power, factor = scale_of(jnp.abs(total))
    out[0:TROWS, :] = total * factor
    out[TROWS:, :] = jnp.where(iota((8, LANES), 0) == 0, power, slots[...])


def all_blocks(lens, got, coefs, out, ints, words, tmat, dmat, msg, sem):
    aux, pair = lax.axis_index("aux"), lax.axis_index("pair")
    for y in range(NP):
        ints[8 * y : 8 * (y + 1), :] = got[pair_slot(y), TROWS : TROWS + 8, :].astype(jnp.int32)
    copy = pltpu.make_async_copy(ints, words, sem)
    copy.start()

    lane = iota((1, LANES), 1)
    for g in range(3):
        limit = jnp.zeros((1, LANES), jnp.int32)
        for k in range(8):
            limit = jnp.where((lane >> 4) == k, lens[8 * g + k], limit)
        kept = (lane & 15) + 16 * aux < limit
        for y in range(NP):
            slot = pair_slot(y)
            part = got[slot, TJ * g : TJ * (g + 1), :] * unscale(got[slot, TROWS : TROWS + 1, :])
            part = jnp.where(kept, part, 0.0)
            high = part.astype(BF16).astype(F32)
            tmat[TJ * y : TJ * (y + 1), LANES * g : LANES * (g + 1)] = high
            tmat[TJ * y : TJ * (y + 1), LANES * (g + 3) : LANES * (g + 4)] = part - high
    shape = (NP, TJ, NO * NI)
    y, row = iota(shape, 0), iota(shape, 1)
    fifth = row >= 4 * NO
    occ = jnp.where(fifth, 2 * (row - 4 * NO) + (y & 1), row & (NO - 1))
    j = first_column(occ, y) + jnp.where(fifth, 4, row >> 4)
    pick = jnp.where(iota(shape, 2) == NI * occ + j, 1.0, 0.0)
    pick = pick.reshape(NP * TJ, NO * NI).astype(BF16)
    ordered = dot(pick, tmat[...].astype(BF16), TN).astype(BF16)

    for p in range(NA):
        limit = jnp.zeros((1, LANES), jnp.int32)
        for k in range(3):
            limit = jnp.where((lane >> 5) == k, lens[3 * p + k], limit)
        kept = 8 * (lane & 15) + 2 * pair + ((lane >> 4) & 1) < limit
        packed = coefs[aux_slot(p)]
        packed = packed[8:] * unscale(packed[1:2])
        rows = [packed[TJ * b : TJ * (b + 1)] for b in range(3)]
        last = pltpu.roll(rows[0], 32, 1)
        last = jnp.where(lane >= 32, pltpu.roll(rows[1], 64, 1), last)
        last = jnp.where(lane >= 64, pltpu.roll(rows[2], 96, 1), last)
        coef = jnp.concatenate(rows + [last], axis=0)
        coef = jnp.where(kept, coef, 0.0).astype(BF16)
        blocks = dot(coef, ordered, TN)
        blocks = blocks[:, : 3 * LANES] + blocks[:, 3 * LANES :]
        for g in range(3):
            dmat[g, LANES * p : LANES * (p + 1), :] = blocks[:, LANES * g : LANES * (g + 1)]

    copy.wait()
    lane = iota((32, LANES), 1)
    for q in range(20):
        y = q // 5
        count = words[8 * y + 3, 0]
        tile = jnp.zeros((32, LANES), F32)
        for k in range(8):
            slot = 8 * (q % 5) + k
            a, b = words[8 * y + 1, slot], words[8 * y + 2, slot]
            third = (a * 171) >> 9
            start = pl.multiple_of(LANES * third + 32 * (a - 3 * third), 32)
            block = dmat[b >> 3, pl.ds(start, 32), :]
            block = pltpu.roll(block, (16 * (k + 8 - (b & 7))) & 127, 1)
            end = jnp.where(slot < count, 16 * (k + 1), 0)
            tile = jnp.where((lane >= 16 * k) & (lane < end), block, tile)
        for e in range(2):
            msg[pl.ds(2 * q + e, NO, stride=40), :] = tile[NO * e : NO * (e + 1)]
    for o in range(NO):
        out[slot_of(o)] = msg[40 * o : 40 * (o + 1), :].astype(BF16)


def sum_occ(got, out, total):
    blocks = jnp.sum(got[...].astype(F32), axis=0)
    power, factor = scale_of(jnp.abs(blocks))
    total[...] = blocks * factor
    rest = jnp.where(iota((6, LANES), 0) == 0, power, 0.0)
    for y in range(NP):
        rows = total[10 * y : 10 * (y + 1), :]
        for p in range(NA):
            out[both_slot(y, p), 0:10, :] = rows
            out[both_slot(y, p), 10:16, :] = rest


def unpack(got, out, rows):
    for y in range(NP):
        for p in range(NA):
            part = got[both_slot(y, p)]
            part = part * unscale(part[10:11, :])
            for q in range(5):
                rows[q, p, 2 * y : 2 * y + 2, :] = part[2 * q : 2 * q + 2, :]
    for q in range(5):
        blocks = swap_pieces([rows[q, p] for p in range(NA)], 16)
        for k in range(8):
            out[8 * q + k] = blocks[k]


def exchange(x, axes, groups=None):
    return lax.all_to_all(x, axes, split_axis=0, concat_axis=0, tiled=True, axis_index_groups=groups)


def shape_of(shape, dtype):
    return jax.ShapeDtypeStruct(shape, dtype)


def on_device(amp_fit, amp_cabs, coef, f12_weight, ints_fit, ints_cabs, shell_len, pair_blocks, pair_count):
    weight = jnp.pad(jnp.tile(f12_weight, NC), (0, 2 * LANES - NI * NC))[None, :]

    sent = pl.pallas_call(
        pack_amps,
        out_shape=shape_of((NO, ROWS, 256), BF16),
        in_specs=[ANY] * 3,
        out_specs=vmem(1)[0],
        scratch_shapes=[
            pltpu.VMEM((NJ, NF, NO * NI), BF16),
            pltpu.VMEM((NC, NI, NO * NI), BF16),
            pltpu.VMEM((NI, 3 * LANES), BF16),
            pltpu.VMEM((24 * NC, NO * NI), F32),
            pltpu.VMEM((256, NO * NI), BF16),
            pltpu.VMEM((ROWS, 256), F32),
            pltpu.VMEM((NI, LANES), F32),
            pltpu.SemaphoreType.DMA((4,)),
        ],
        compiler_params=room(60),
    )(jnp.transpose(amp_fit, (2, 0, 1)), jnp.transpose(amp_cabs, (0, 2, 1)), coef)
    amps = exchange(sent, "occ", FROM_ROOT)

    cabs, slots = pl.pallas_call(
        join_cabs,
        out_shape=[shape_of((NC * NI, 24 * LANES), BF16), shape_of((8, LANES), F32)],
        in_specs=[SMEM] + vmem(1) + [ANY],
        out_specs=vmem(2),
        scratch_shapes=[pltpu.VMEM((NC, NI, 24 * LANES), BF16), pltpu.SemaphoreType.DMA],
        compiler_params=room(51),
        cost_estimate=pl.CostEstimate(flops=0, bytes_accessed=5_000_000, transcendentals=0),
    )(pair_count, pair_blocks.T, ints_cabs)
    sent, factors = pl.pallas_call(
        partial_t,
        out_shape=[shape_of((NA, SROWS, LANES), F32), shape_of((SROWS, LANES), F32)],
        in_specs=vmem(3) + [ANY],
        out_specs=vmem(2),
        scratch_shapes=[
            pltpu.VMEM((TJ, 5 * LANES), BF16),
            pltpu.VMEM((TJ, 3 * LANES), BF16),
            pltpu.VMEM((CROWS, LANES), F32),
            pltpu.VMEM((NI * NF, 24 * LANES), BF16),
            pltpu.SemaphoreType.DMA((3,)),
        ],
        compiler_params=room(49),
    )(amps, weight, cabs, jnp.transpose(ints_fit, (1, 0, 2)).reshape(NI * NF, 24 * LANES))
    shares = exchange((sent * factors[None]).astype(F16), "aux", FROM_AUX)

    sent = pl.pallas_call(
        sum_aux,
        out_shape=shape_of((TROWS + 8, LANES), F32),
        in_specs=vmem(2),
        out_specs=vmem(1)[0],
        compiler_params=PARAMS,
    )(slots, shares[:, : TROWS + 8].astype(F32))
    sent = jnp.broadcast_to(sent.astype(F16)[None], (NP, TROWS + 8, LANES))
    got = exchange(sent, "pair", FROM_PAIR).astype(F32)

    sent = pl.pallas_call(
        all_blocks,
        out_shape=shape_of((NO, 40, LANES), BF16),
        in_specs=[SMEM] + vmem(2),
        out_specs=vmem(1)[0],
        scratch_shapes=[
            pltpu.VMEM((8 * NP, LANES), jnp.int32),
            pltpu.SMEM((8 * NP, LANES), jnp.int32),
            pltpu.VMEM((NP * TJ, 6 * LANES), F32),
            pltpu.VMEM((3, 8 * LANES, LANES), F32),
            pltpu.VMEM((NO * 40, LANES), F32),
            pltpu.SemaphoreType.DMA,
        ],
        compiler_params=PARAMS,
    )(shell_len, got, shares[:, TROWS:].astype(F32))
    got = exchange(sent, "occ", FROM_ROOT)

    sent = pl.pallas_call(
        sum_occ,
        out_shape=shape_of((NP * NA, 16, LANES), F32),
        in_specs=vmem(1),
        out_specs=vmem(1)[0],
        scratch_shapes=[pltpu.VMEM((40, LANES), F32)],
        compiler_params=PARAMS,
    )(got)
    got = exchange(sent.astype(F16), ("pair", "aux"), FROM_BOTH).astype(F32)

    return pl.pallas_call(
        unpack,
        out_shape=shape_of((40, 8, LANES), F32),
        in_specs=vmem(1),
        out_specs=vmem(1)[0],
        scratch_shapes=[pltpu.VMEM((5, NA, 8, LANES), F32)],
        compiler_params=PARAMS,
    )(got)


def solution(mesh):
    placed = (
        P("aux", None, "occ"),
        P("aux", None, "occ"),
        P("occ", None),
        P("occ"),
        P("aux", "occ", None),
        P("aux", "occ", None),
        P(),
        P("pair", None),
        P("pair"),
    )
    return jax.shard_map(
        on_device, mesh=mesh, in_specs=placed, out_specs=P("pair", "occ", None), check_vma=False
    )
```

```python
import functools
import math

import jax
import jax.numpy as jnp
from jax import lax
from jax.experimental import pallas as pl
from jax.experimental.pallas import tpu as pltpu
from jax.sharding import PartitionSpec as P

F32, BF16, F16 = jnp.float32, jnp.bfloat16, jnp.float16
LANES = 128
LN2 = math.log(2.0)
NT = (((1,), (1,)), ((), ()))
TN = (((0,), (0,)), ((), ()))


def iota(shape, dim):
    return lax.broadcasted_iota(jnp.int32, shape, dim)


def dot(a, b, dims=(((1,), (0,)), ((), ()))):
    return lax.dot_general(a, b, dims, preferred_element_type=F32)


def one_hot(cond):
    return jnp.where(cond, 1.0, 0.0).astype(BF16)


def swap_pieces(xs, piece):
    lane = iota(xs[0].shape, 1)
    bit = 1
    while bit < len(xs):
        keep = ((lane // piece) & bit) == 0
        ys = list(xs)
        for k in range(len(xs)):
            if k & bit == 0:
                lo, hi = xs[k], xs[k + bit]
                ys[k] = jnp.where(keep, lo, pltpu.roll(hi, piece * bit, 1))
                ys[k + bit] = jnp.where(keep, pltpu.roll(lo, LANES - piece * bit, 1), hi)
        xs = ys
        bit *= 2
    return xs


def vmem(n):
    return [pl.BlockSpec(memory_space=pltpu.VMEM)] * n


SMEM = pl.BlockSpec(memory_space=pltpu.SMEM)
ANY = pl.BlockSpec(memory_space=pl.ANY)

def room(mib):
    return pltpu.CompilerParams(vmem_limit_bytes=mib * 1024 * 1024)


PARAMS = room(40)


NO, NI, NA, NP, NF, NC, NJ = 16, 18, 8, 4, 32, 12, 5
CQ = 16
TJ = 72
GROUP = 8 * LANES
TROWS = 3 * TJ
ROOT, STEP, BACK = 11, 7, 7
FROM_ROOT = [[(STEP * k + ROOT) % NO for k in range(NO)]]
FROM_AUX = [[(k + 6) % NA for k in range(NA)]]
FROM_PAIR = [[(k + 3) % NP for k in range(NP)]]
FROM_BOTH = [[NA * y + p for y in FROM_PAIR[0] for p in FROM_AUX[0]]]
ROWS = 24
CROWS = 216
SROWS = TROWS + 8 + CROWS


def slot_of(occ):
    return (BACK * (occ + NO - ROOT)) & (NO - 1)


def aux_slot(aux):
    return (aux + NA - 6) % NA


def pair_slot(pair):
    return (pair + NP - 3) % NP


def both_slot(pair, aux):
    return NA * pair_slot(pair) + aux_slot(aux)


def first_column(occ, pair):
    return (9 * pair + 1 - (occ & 1)) >> 1


def pack_amps(fit_hbm, cabs_hbm, coef_hbm, out, fit, cabs, coef, cab32, x, extra, piece, sems):
    aux, pair = lax.axis_index("aux"), lax.axis_index("pair")
    first_j = first_column(lax.axis_index("occ"), pair)
    fifth_j = jnp.minimum(first_j + 4, NI - 1)
    columns = pl.ds(pl.multiple_of(3 * LANES * aux, LANES), 3 * LANES)
    copies = [
        pltpu.make_async_copy(cabs_hbm, cabs, sems.at[0]),
        pltpu.make_async_copy(fit_hbm.at[pl.ds(first_j, 4)], fit.at[pl.ds(0, 4)], sems.at[1]),
        pltpu.make_async_copy(fit_hbm.at[pl.ds(fifth_j, 1)], fit.at[pl.ds(4, 1)], sems.at[2]),
        pltpu.make_async_copy(coef_hbm.at[:, columns], coef, sems.at[3]),
    ]
    for c in copies:
        c.start()
    shape = (NO, ROWS, NO * NI)
    t = iota(shape, 1)
    place = jnp.where((iota(shape, 2) == NI * ((STEP * iota(shape, 0) + ROOT) & (NO - 1)) + t) & (t < NI), 1.0, 0.0)
    place = place.reshape(NO * ROWS, NO * NI).astype(BF16)
    source, target = iota((LANES, LANES), 0), iota((LANES, LANES), 1)
    mine = source == 8 * (target & 15) + 2 * pair + ((target >> 4) & 1)
    for c in copies:
        c.wait()
    x[0 : NJ * NF, :] = fit[...].reshape(NJ * NF, NO * NI)
    for q in range(NC):
        cab32[24 * q : 24 * q + NI, :] = cabs[q].astype(F32)
    zero = jnp.zeros((CQ - NC, NO * NI), F32)
    for jj in range(NJ):
        j = fifth_j if jj == 4 else first_j + jj
        picked = [cab32[pl.ds(24 * q + j, 1), :] for q in range(NC)]
        rows = jnp.concatenate(picked + [zero], axis=0)
        x[NJ * NF + CQ * jj : NJ * NF + CQ * (jj + 1), :] = rows.astype(BF16)
    x[NJ * (NF + CQ) :, :] = jnp.zeros((256 - NJ * (NF + CQ), NO * NI), BF16)
    piece[...] = sum(
        dot(coef[:, LANES * k : LANES * (k + 1)], one_hot(mine & ((target >> 5) == k))) for k in range(3)
    )
    lane = iota((6, LANES), 1)
    third = piece[12:18, :]
    extra[...] = jnp.zeros(extra.shape, F32)
    extra[18:24, 0:LANES] = jnp.where(lane < 96, piece[0:6, :], pltpu.roll(third, 96, 1))
    extra[18:24, LANES:] = jnp.where(lane < 96, piece[6:12, :], pltpu.roll(third, 64, 1))
    extra[0:6, LANES:] = jnp.where(lane >= 112, pltpu.roll(third, 48, 1), 0.0)
    extra[6:12, LANES:] = jnp.where(lane >= 112, pltpu.roll(third, 32, 1), 0.0)
    out[...] = (dot(place, x[...], NT).reshape(NO, ROWS, 256) + extra[...][None]).astype(BF16)


def join_cabs(counts, pairs, cabs_hbm, out, slots, cabs, sem):
    copy = pltpu.make_async_copy(cabs_hbm, cabs, sem)
    copy.start()
    slots[...] = jnp.zeros(slots.shape, F32)
    slots[1:3, 0:40] = pairs[...].astype(F32)
    slots[3:4, :] = jnp.broadcast_to(counts[0].astype(F32), (1, LANES))
    copy.wait()
    for q in range(NC):
        out[NI * q : NI * (q + 1), :] = cabs[q]


def partial_t(got, weight, cabs, fit_hbm, out, factors, a_fit, a_cab, own, fit, sems):
    spans = [pl.ds(GROUP * g, GROUP) for g in range(3)]
    copies = [pltpu.make_async_copy(fit_hbm.at[:, s], fit.at[:, s], sems.at[g]) for g, s in enumerate(spans)]
    for c in copies:
        c.start()
    messages = got[...].reshape(NO * ROWS, 256)
    first = lax.axis_index("pair") & 1

    def picked(step, start):
        count = NO // step
        shape = (NI, count, NO * ROWS)
        pick = iota(shape, 2) == ROWS * slot_of(step * iota(shape, 1) + start) + iota(shape, 0)
        pick = jnp.where(pick, 1.0, 0.0).reshape(NI * count, NO * ROWS).astype(BF16)
        rows = dot(pick, messages)
        return [[rows[count * t : count * (t + 1), LANES * h : LANES * (h + 1)] for h in (0, 1)] for t in range(NI)]

    amps, fifth = picked(1, 0), picked(2, first)

    def lay(width, start, store):
        per = LANES // width
        for jj in range(NJ):
            tiles = amps if jj < 4 else fifth
            count = tiles[0][0].shape[0]
            lane = iota((count, LANES), 1)
            half, off = divmod(start + width * jj, LANES)
            for m in range(-(-NI // per)):
                tile = jnp.zeros((count, LANES), F32)
                for k in range(min(per, NI - m * per)):
                    moved = tiles[m * per + k][half]
                    if (width * k - off) % LANES:
                        moved = pltpu.roll(moved, (width * k - off) % LANES, 1)
                    tile = jnp.where((lane >= width * k) & (lane < width * (k + 1)), moved, tile)
                store[NO * jj : NO * jj + count, LANES * m : LANES * (m + 1)] = tile.astype(BF16)

    lay(NF, 0, a_fit)
    lay(CQ, NJ * NF, a_cab)
    shape = (3 * LANES, 2 * LANES)
    source, target = iota(shape, 0), iota(shape, 1)
    q = (target * 3641) >> 16
    order = one_hot((q == (source & 15)) & (target - NI * q == (source >> 4)))
    weighted = dot(a_cab[0:TJ, :], order) * weight[...]
    high = weighted.astype(BF16).astype(F32)
    gap = jnp.zeros((8, 2 * LANES), F32)
    both = jnp.concatenate([high, gap, weighted - high, gap], axis=0)
    a_cab[:, : 2 * LANES] = both.astype(BF16)

    def pack_coefficients():
        shape = (NO * NI, NO * ROWS)
        row, source = iota(shape, 0), iota(shape, 1)
        occ = (row * 3641) >> 16
        rest = row - NI * occ
        sixth = rest - jnp.where(rest >= 12, 12, jnp.where(rest >= 6, 6, 0))
        base = source - ROWS * slot_of(occ) - sixth
        main = dot(one_hot(base == 18), messages)
        spare0 = dot(one_hot(base == 0), messages[:, LANES:])
        spare1 = dot(one_hot(base == 6), messages[:, LANES:])
        shape = (NO * NI, LANES)
        lane, row = iota(shape, 1), iota(shape, 0)
        rest = row - NI * ((row * 3641) >> 16)
        third = jnp.where(lane < 32, pltpu.roll(main[:, :LANES], 32, 1), pltpu.roll(main[:, LANES:], 64, 1))
        third = jnp.where(lane < 64, third, pltpu.roll(spare0, 80, 1))
        third = jnp.where(lane < 80, third, pltpu.roll(spare1, 96, 1))
        coef = jnp.where(rest < 6, main[:, :LANES], jnp.where(rest < 12, main[:, LANES:], third))
        last = coef[3 * TJ :]
        lane = iota((TJ, LANES), 1)
        for b in range(3):
            moved = pltpu.roll(last, 96 - 32 * b, 1)
            own[TJ * b : TJ * (b + 1), :] = jnp.where(lane < 96, coef[TJ * b : TJ * (b + 1)], moved)
        for p in range(NA):
            out[p, TROWS + 8 :, :] = own[...]

    top = jnp.zeros((TJ, LANES), F32)

    for g in range(3):
        copies[g].wait()
        two = dot(a_cab[:, : NI * NC], cabs[:, spans[g]])
        total = dot(a_fit[:, : NI * NF], fit[:, spans[g]]) + two[0:TJ] + two[TJ + 8 : 2 * TJ + 8]
        if g == 0:
            pack_coefficients()
        pieces = swap_pieces([total[:, LANES * k : LANES * (k + 1)] for k in range(8)], 16)
        top = functools.reduce(jnp.maximum, [jnp.abs(piece) for piece in pieces], top)
        for k in range(8):
            out[aux_slot(k), TJ * g : TJ * (g + 1), :] = pieces[k]
    power_t, factor_t = scale_of(top)
    power_c, factor_c = scale_of(jnp.abs(own[...]))
    factors[0:TROWS, :] = jnp.broadcast_to(factor_t, (TROWS, LANES))
    factors[TROWS : TROWS + 8, :] = jnp.ones((8, LANES), F32)
    factors[TROWS + 8 :, :] = jnp.broadcast_to(factor_c, (CROWS, LANES))
    powers = jnp.where(iota((8, LANES), 0) == 0, power_t, power_c)
    for p in range(NA):
        out[p, TROWS : TROWS + 8, :] = powers


def scale_of(top):
    top = jnp.max(jnp.max(top, axis=1, keepdims=True), axis=0, keepdims=True)
    power = jnp.ceil(jnp.log(jnp.maximum(top, 1e-30)) * (1.0 / LN2))
    return power, jnp.exp(power * -LN2) * 16384.0


def unscale(power):
    return jnp.exp(power * LN2) * (1.0 / 16384.0)


def sum_aux(slots, got, out):
    total = sum(got[p, 0:TROWS, :] * unscale(got[p, TROWS : TROWS + 1, :]) for p in range(NA))
    power, factor = scale_of(jnp.abs(total))
    out[0:TROWS, :] = total * factor
    out[TROWS:, :] = jnp.where(iota((8, LANES), 0) == 0, power, slots[...])


def all_blocks(lens, got, coefs, out, ints, words, tmat, dmat, msg, sem):
    aux, pair = lax.axis_index("aux"), lax.axis_index("pair")
    for y in range(NP):
        slots = got[pair_slot(y), TROWS : TROWS + 8, :].astype(jnp.int32)
        a, b, count = slots[1:2], slots[2:3], slots[3:4]
        third = (a * 171) >> 9
        ints[8 * y : 8 * y + 1, :] = LANES * third + 32 * (a - 3 * third)
        ints[8 * y + 1 : 8 * y + 2, :] = b >> 3
        ints[8 * y + 2 : 8 * y + 3, :] = LANES - 16 * (b & 7)
        ints[8 * y + 3 : 8 * y + 4, :] = jnp.where(iota((1, LANES), 1) < count, LANES, 0)
        ints[8 * y + 4 : 8 * y + 8, :] = slots[4:8]
    copy = pltpu.make_async_copy(ints, words, sem)
    copy.start()

    lane = iota((1, LANES), 1)
    for g in range(3):
        limit = jnp.zeros((1, LANES), jnp.int32)
        for k in range(8):
            limit = jnp.where((lane >> 4) == k, lens[8 * g + k], limit)
        kept = (lane & 15) + 16 * aux < limit
        for y in range(NP):
            slot = pair_slot(y)
            part = got[slot, TJ * g : TJ * (g + 1), :] * unscale(got[slot, TROWS : TROWS + 1, :])
            part = jnp.where(kept, part, 0.0)
            high = part.astype(BF16).astype(F32)
            tmat[TJ * y : TJ * (y + 1), LANES * g : LANES * (g + 1)] = high
            tmat[TJ * y : TJ * (y + 1), LANES * (g + 3) : LANES * (g + 4)] = part - high
    shape = (NP, TJ, NO * NI)
    y, row = iota(shape, 0), iota(shape, 1)
    fifth = row >= 4 * NO
    occ = jnp.where(fifth, 2 * (row - 4 * NO) + (y & 1), row & (NO - 1))
    j = first_column(occ, y) + jnp.where(fifth, 4, row >> 4)
    pick = jnp.where(iota(shape, 2) == NI * occ + j, 1.0, 0.0)
    pick = pick.reshape(NP * TJ, NO * NI).astype(BF16)
    ordered = dot(pick, tmat[...].astype(BF16), TN).astype(BF16)

    for p in range(NA):
        limit = jnp.zeros((1, LANES), jnp.int32)
        for k in range(3):
            limit = jnp.where((lane >> 5) == k, lens[3 * p + k], limit)
        kept = 8 * (lane & 15) + 2 * pair + ((lane >> 4) & 1) < limit
        packed = coefs[aux_slot(p)]
        packed = packed[8:] * unscale(packed[1:2])
        rows = [packed[TJ * b : TJ * (b + 1)] for b in range(3)]
        last = pltpu.roll(rows[0], 32, 1)
        last = jnp.where(lane >= 32, pltpu.roll(rows[1], 64, 1), last)
        last = jnp.where(lane >= 64, pltpu.roll(rows[2], 96, 1), last)
        coef = jnp.concatenate(rows + [last], axis=0)
        coef = jnp.where(kept, coef, 0.0).astype(BF16)
        blocks = dot(coef, ordered, TN)
        blocks = blocks[:, : 3 * LANES] + blocks[:, 3 * LANES :]
        for g in range(3):
            dmat[g, LANES * p : LANES * (p + 1), :] = blocks[:, LANES * g : LANES * (g + 1)]

    copy.wait()
    lane = iota((32, LANES), 1)
    for q in range(20):
        y = q // 5
        tile = jnp.zeros((32, LANES), F32)
        for k in range(8):
            slot = 8 * (q % 5) + k
            start = pl.multiple_of(words[8 * y, slot], 32)
            block = dmat[words[8 * y + 1, slot], pl.ds(start, 32), :]
            block = pltpu.roll(block, (words[8 * y + 2, slot] + 16 * k) & 127, 1)
            end = jnp.minimum(words[8 * y + 3, slot], 16 * (k + 1))
            tile = jnp.where((lane >= 16 * k) & (lane < end), block, tile)
        for e in range(2):
            msg[pl.ds(2 * q + e, NO, stride=40), :] = tile[NO * e : NO * (e + 1)]
    for o in range(NO):
        out[slot_of(o)] = msg[40 * o : 40 * (o + 1), :].astype(BF16)


def sum_occ(got, out, total):
    blocks = jnp.sum(got[...].astype(F32), axis=0)
    power, factor = scale_of(jnp.abs(blocks))
    total[...] = blocks * factor
    rest = jnp.where(iota((6, LANES), 0) == 0, power, 0.0)
    for y in range(NP):
        rows = total[10 * y : 10 * (y + 1), :]
        for p in range(NA):
            out[both_slot(y, p), 0:10, :] = rows
            out[both_slot(y, p), 10:16, :] = rest


def unpack(got, out, rows):
    for y in range(NP):
        for p in range(NA):
            part = got[both_slot(y, p)]
            part = part * unscale(part[10:11, :])
            for q in range(5):
                rows[q, p, 2 * y : 2 * y + 2, :] = part[2 * q : 2 * q + 2, :]
    for q in range(5):
        blocks = swap_pieces([rows[q, p] for p in range(NA)], 16)
        for k in range(8):
            out[8 * q + k] = blocks[k]


def exchange(x, axes, groups=None):
    return lax.all_to_all(x, axes, split_axis=0, concat_axis=0, tiled=True, axis_index_groups=groups)


def shape_of(shape, dtype):
    return jax.ShapeDtypeStruct(shape, dtype)


def on_device(amp_fit, amp_cabs, coef, f12_weight, ints_fit, ints_cabs, shell_len, pair_blocks, pair_count):
    weight = jnp.pad(jnp.tile(f12_weight, NC), (0, 2 * LANES - NI * NC))[None, :]

    sent = pl.pallas_call(
        pack_amps,
        out_shape=shape_of((NO, ROWS, 256), BF16),
        in_specs=[ANY] * 3,
        out_specs=vmem(1)[0],
        scratch_shapes=[
            pltpu.VMEM((NJ, NF, NO * NI), BF16),
            pltpu.VMEM((NC, NI, NO * NI), BF16),
            pltpu.VMEM((NI, 3 * LANES), BF16),
            pltpu.VMEM((24 * NC, NO * NI), F32),
            pltpu.VMEM((256, NO * NI), BF16),
            pltpu.VMEM((ROWS, 256), F32),
            pltpu.VMEM((NI, LANES), F32),
            pltpu.SemaphoreType.DMA((4,)),
        ],
        compiler_params=room(60),
    )(jnp.transpose(amp_fit, (2, 0, 1)), jnp.transpose(amp_cabs, (0, 2, 1)), coef)
    amps = exchange(sent, "occ", FROM_ROOT)

    cabs, slots = pl.pallas_call(
        join_cabs,
        out_shape=[shape_of((NC * NI, 24 * LANES), BF16), shape_of((8, LANES), F32)],
        in_specs=[SMEM] + vmem(1) + [ANY],
        out_specs=vmem(2),
        scratch_shapes=[pltpu.VMEM((NC, NI, 24 * LANES), BF16), pltpu.SemaphoreType.DMA],
        compiler_params=room(51),
        cost_estimate=pl.CostEstimate(flops=0, bytes_accessed=5_000_000, transcendentals=0),
    )(pair_count, pair_blocks.T, ints_cabs)
    sent, factors = pl.pallas_call(
        partial_t,
        out_shape=[shape_of((NA, SROWS, LANES), F32), shape_of((SROWS, LANES), F32)],
        in_specs=vmem(3) + [ANY],
        out_specs=vmem(2),
        scratch_shapes=[
            pltpu.VMEM((TJ, 5 * LANES), BF16),
            pltpu.VMEM((2 * TJ + 16, 3 * LANES), BF16),
            pltpu.VMEM((CROWS, LANES), F32),
            pltpu.VMEM((NI * NF, 24 * LANES), BF16),
            pltpu.SemaphoreType.DMA((3,)),
        ],
        compiler_params=room(49),
    )(amps, weight, cabs, jnp.transpose(ints_fit, (1, 0, 2)).reshape(NI * NF, 24 * LANES))
    shares = exchange((sent * factors[None]).astype(F16), "aux", FROM_AUX)

    sent = pl.pallas_call(
        sum_aux,
        out_shape=shape_of((TROWS + 8, LANES), F32),
        in_specs=vmem(2),
        out_specs=vmem(1)[0],
        compiler_params=PARAMS,
    )(slots, shares[:, : TROWS + 8].astype(F32))
    sent = jnp.broadcast_to(sent.astype(F16)[None], (NP, TROWS + 8, LANES))
    got = exchange(sent, "pair", FROM_PAIR).astype(F32)

    sent = pl.pallas_call(
        all_blocks,
        out_shape=shape_of((NO, 40, LANES), BF16),
        in_specs=[SMEM] + vmem(2),
        out_specs=vmem(1)[0],
        scratch_shapes=[
            pltpu.VMEM((8 * NP, LANES), jnp.int32),
            pltpu.SMEM((8 * NP, LANES), jnp.int32),
            pltpu.VMEM((NP * TJ, 6 * LANES), F32),
            pltpu.VMEM((3, 8 * LANES, LANES), F32),
            pltpu.VMEM((NO * 40, LANES), F32),
            pltpu.SemaphoreType.DMA,
        ],
        compiler_params=PARAMS,
    )(shell_len, got, shares[:, TROWS:].astype(F32))
    got = exchange(sent, "occ", FROM_ROOT)

    sent = pl.pallas_call(
        sum_occ,
        out_shape=shape_of((NP * NA, 16, LANES), F32),
        in_specs=vmem(1),
        out_specs=vmem(1)[0],
        scratch_shapes=[pltpu.VMEM((40, LANES), F32)],
        compiler_params=PARAMS,
    )(got)
    got = exchange(sent.astype(F16), ("pair", "aux"), FROM_BOTH).astype(F32)

    return pl.pallas_call(
        unpack,
        out_shape=shape_of((40, 8, LANES), F32),
        in_specs=vmem(1),
        out_specs=vmem(1)[0],
        scratch_shapes=[pltpu.VMEM((5, NA, 8, LANES), F32)],
        compiler_params=PARAMS,
    )(got)


def solution(mesh):
    placed = (
        P("aux", None, "occ"),
        P("aux", None, "occ"),
        P("occ", None),
        P("occ"),
        P("aux", "occ", None),
        P("aux", "occ", None),
        P(),
        P("pair", None),
        P("pair"),
    )
    return jax.shard_map(
        on_device, mesh=mesh, in_specs=placed, out_specs=P("pair", "occ", None), check_vma=False
    )
```

```python
import functools
import math

import jax
import jax.numpy as jnp
from jax import lax
from jax.experimental import pallas as pl
from jax.experimental.pallas import tpu as pltpu
from jax.sharding import PartitionSpec as P

F32, BF16, F16 = jnp.float32, jnp.bfloat16, jnp.float16
LANES = 128
LN2 = math.log(2.0)
NT = (((1,), (1,)), ((), ()))
TN = (((0,), (0,)), ((), ()))


def iota(shape, dim):
    return lax.broadcasted_iota(jnp.int32, shape, dim)


def dot(a, b, dims=(((1,), (0,)), ((), ()))):
    return lax.dot_general(a, b, dims, preferred_element_type=F32)


def one_hot(cond):
    return jnp.where(cond, 1.0, 0.0).astype(BF16)


def swap_pieces(xs, piece):
    lane = iota(xs[0].shape, 1)
    bit = 1
    while bit < len(xs):
        keep = ((lane // piece) & bit) == 0
        ys = list(xs)
        for k in range(len(xs)):
            if k & bit == 0:
                lo, hi = xs[k], xs[k + bit]
                ys[k] = jnp.where(keep, lo, pltpu.roll(hi, piece * bit, 1))
                ys[k + bit] = jnp.where(keep, pltpu.roll(lo, LANES - piece * bit, 1), hi)
        xs = ys
        bit *= 2
    return xs


def vmem(n):
    return [pl.BlockSpec(memory_space=pltpu.VMEM)] * n


SMEM = pl.BlockSpec(memory_space=pltpu.SMEM)
ANY = pl.BlockSpec(memory_space=pl.ANY)

def room(mib):
    return pltpu.CompilerParams(vmem_limit_bytes=mib * 1024 * 1024)


PARAMS = room(40)


NO, NI, NA, NP, NF, NC, NJ = 16, 18, 8, 4, 32, 12, 5
CQ = 16
TJ = 72
GROUP = 8 * LANES
TROWS = 3 * TJ
ROOT, STEP, BACK = 11, 7, 7
FROM_ROOT = [[(STEP * k + ROOT) % NO for k in range(NO)]]
FROM_AUX = [[(k + 4) % NA for k in range(NA)]]
FROM_PAIR = [[(k + 2) % NP for k in range(NP)]]
FROM_BOTH = [[NA * y + p for y in FROM_PAIR[0] for p in FROM_AUX[0]]]
ROWS = 24
CROWS = 216
SROWS = TROWS + 8 + CROWS


def slot_of(occ):
    return (BACK * (occ + NO - ROOT)) & (NO - 1)


def aux_slot(aux):
    return (aux + NA - 4) % NA


def pair_slot(pair):
    return (pair + NP - 2) % NP


def both_slot(pair, aux):
    return NA * pair_slot(pair) + aux_slot(aux)


def first_column(occ, pair):
    return (9 * pair + 1 - (occ & 1)) >> 1


def pack_amps(fit_hbm, cabs_hbm, coef_hbm, out, fit, cabs, coef, cab32, x, extra, piece, sems):
    aux, pair = lax.axis_index("aux"), lax.axis_index("pair")
    first_j = first_column(lax.axis_index("occ"), pair)
    fifth_j = jnp.minimum(first_j + 4, NI - 1)
    columns = pl.ds(pl.multiple_of(3 * LANES * aux, LANES), 3 * LANES)
    copies = [
        pltpu.make_async_copy(cabs_hbm, cabs, sems.at[0]),
        pltpu.make_async_copy(fit_hbm.at[pl.ds(first_j, 4)], fit.at[pl.ds(0, 4)], sems.at[1]),
        pltpu.make_async_copy(fit_hbm.at[pl.ds(fifth_j, 1)], fit.at[pl.ds(4, 1)], sems.at[2]),
        pltpu.make_async_copy(coef_hbm.at[:, columns], coef, sems.at[3]),
    ]
    for c in copies:
        c.start()
    shape = (NO, ROWS, NO * NI)
    t = iota(shape, 1)
    place = jnp.where((iota(shape, 2) == NI * ((STEP * iota(shape, 0) + ROOT) & (NO - 1)) + t) & (t < NI), 1.0, 0.0)
    place = place.reshape(NO * ROWS, NO * NI).astype(BF16)
    source, target = iota((LANES, LANES), 0), iota((LANES, LANES), 1)
    mine = source == 8 * (target & 15) + 2 * pair + ((target >> 4) & 1)
    for c in copies:
        c.wait()
    x[0 : NJ * NF, :] = fit[...].reshape(NJ * NF, NO * NI)
    for q in range(NC):
        cab32[24 * q : 24 * q + NI, :] = cabs[q].astype(F32)
    zero = jnp.zeros((CQ - NC, NO * NI), F32)
    for jj in range(NJ):
        j = fifth_j if jj == 4 else first_j + jj
        picked = [cab32[pl.ds(24 * q + j, 1), :] for q in range(NC)]
        rows = jnp.concatenate(picked + [zero], axis=0)
        x[NJ * NF + CQ * jj : NJ * NF + CQ * (jj + 1), :] = rows.astype(BF16)
    x[NJ * (NF + CQ) :, :] = jnp.zeros((256 - NJ * (NF + CQ), NO * NI), BF16)
    piece[...] = sum(
        dot(coef[:, LANES * k : LANES * (k + 1)], one_hot(mine & ((target >> 5) == k))) for k in range(3)
    )
    lane = iota((6, LANES), 1)
    third = piece[12:18, :]
    extra[...] = jnp.zeros(extra.shape, F32)
    extra[18:24, 0:LANES] = jnp.where(lane < 96, piece[0:6, :], pltpu.roll(third, 96, 1))
    extra[18:24, LANES:] = jnp.where(lane < 96, piece[6:12, :], pltpu.roll(third, 64, 1))
    extra[0:6, LANES:] = jnp.where(lane >= 112, pltpu.roll(third, 48, 1), 0.0)
    extra[6:12, LANES:] = jnp.where(lane >= 112, pltpu.roll(third, 32, 1), 0.0)
    out[...] = (dot(place, x[...], NT).reshape(NO, ROWS, 256) + extra[...][None]).astype(BF16)


def join_cabs(counts, pairs, cabs_hbm, out, slots, cabs, sem):
    copy = pltpu.make_async_copy(cabs_hbm, cabs, sem)
    copy.start()
    slots[...] = jnp.zeros(slots.shape, F32)
    slots[1:3, 0:40] = pairs[...].astype(F32)
    slots[3:4, :] = jnp.broadcast_to(counts[0].astype(F32), (1, LANES))
    copy.wait()
    for q in range(NC):
        out[NI * q : NI * (q + 1), :] = cabs[q]


def partial_t(got, weight, cabs, fit_hbm, out, factors, a_fit, a_cab, own, fit, sems):
    spans = [pl.ds(GROUP * g, GROUP) for g in range(3)]
    copies = [pltpu.make_async_copy(fit_hbm.at[:, s], fit.at[:, s], sems.at[g]) for g, s in enumerate(spans)]
    for c in copies:
        c.start()
    messages = got[...].reshape(NO * ROWS, 256)
    first = lax.axis_index("pair") & 1

    def picked(step, start):
        count = NO // step
        shape = (NI, count, NO * ROWS)
        pick = iota(shape, 2) == ROWS * slot_of(step * iota(shape, 1) + start) + iota(shape, 0)
        pick = jnp.where(pick, 1.0, 0.0).reshape(NI * count, NO * ROWS).astype(BF16)
        rows = dot(pick, messages)
        return [[rows[count * t : count * (t + 1), LANES * h : LANES * (h + 1)] for h in (0, 1)] for t in range(NI)]

    amps, fifth = picked(1, 0), picked(2, first)

    def lay(width, start, store):
        per = LANES // width
        for jj in range(NJ):
            tiles = amps if jj < 4 else fifth
            count = tiles[0][0].shape[0]
            lane = iota((count, LANES), 1)
            half, off = divmod(start + width * jj, LANES)
            for m in range(-(-NI // per)):
                tile = jnp.zeros((count, LANES), F32)
                for k in range(min(per, NI - m * per)):
                    moved = tiles[m * per + k][half]
                    if (width * k - off) % LANES:
                        moved = pltpu.roll(moved, (width * k - off) % LANES, 1)
                    tile = jnp.where((lane >= width * k) & (lane < width * (k + 1)), moved, tile)
                store[NO * jj : NO * jj + count, LANES * m : LANES * (m + 1)] = tile.astype(BF16)

    lay(NF, 0, a_fit)
    lay(CQ, NJ * NF, a_cab)
    shape = (3 * LANES, 2 * LANES)
    source, target = iota(shape, 0), iota(shape, 1)
    q = (target * 3641) >> 16
    order = one_hot((q == (source & 15)) & (target - NI * q == (source >> 4)))
    weighted = dot(a_cab[0:TJ, :], order) * weight[...]
    high = weighted.astype(BF16).astype(F32)
    gap = jnp.zeros((8, 2 * LANES), F32)
    both = jnp.concatenate([high, gap, weighted - high, gap], axis=0)
    a_cab[:, : 2 * LANES] = both.astype(BF16)

    def pack_coefficients():
        shape = (NO * NI, NO * ROWS)
        row, source = iota(shape, 0), iota(shape, 1)
        occ = (row * 3641) >> 16
        rest = row - NI * occ
        sixth = rest - jnp.where(rest >= 12, 12, jnp.where(rest >= 6, 6, 0))
        base = source - ROWS * slot_of(occ) - sixth
        main = dot(one_hot(base == 18), messages)
        spare0 = dot(one_hot(base == 0), messages[:, LANES:])
        spare1 = dot(one_hot(base == 6), messages[:, LANES:])
        shape = (NO * NI, LANES)
        lane, row = iota(shape, 1), iota(shape, 0)
        rest = row - NI * ((row * 3641) >> 16)
        third = jnp.where(lane < 32, pltpu.roll(main[:, :LANES], 32, 1), pltpu.roll(main[:, LANES:], 64, 1))
        third = jnp.where(lane < 64, third, pltpu.roll(spare0, 80, 1))
        third = jnp.where(lane < 80, third, pltpu.roll(spare1, 96, 1))
        coef = jnp.where(rest < 6, main[:, :LANES], jnp.where(rest < 12, main[:, LANES:], third))
        last = coef[3 * TJ :]
        lane = iota((TJ, LANES), 1)
        for b in range(3):
            moved = pltpu.roll(last, 96 - 32 * b, 1)
            own[TJ * b : TJ * (b + 1), :] = jnp.where(lane < 96, coef[TJ * b : TJ * (b + 1)], moved)
        for p in range(NA):
            out[p, TROWS + 8 :, :] = own[...]

    top = jnp.zeros((TJ, LANES), F32)

    for g in range(3):
        copies[g].wait()
        two = dot(a_cab[:, : NI * NC], cabs[:, spans[g]])
        total = dot(a_fit[:, : NI * NF], fit[:, spans[g]]) + two[0:TJ] + two[TJ + 8 : 2 * TJ + 8]
        if g == 0:
            pack_coefficients()
        pieces = swap_pieces([total[:, LANES * k : LANES * (k + 1)] for k in range(8)], 16)
        top = functools.reduce(jnp.maximum, [jnp.abs(piece) for piece in pieces], top)
        for k in range(8):
            out[aux_slot(k), TJ * g : TJ * (g + 1), :] = pieces[k]
    power_t, factor_t = scale_of(top)
    power_c, factor_c = scale_of(jnp.abs(own[...]))
    factors[0:TROWS, :] = jnp.broadcast_to(factor_t, (TROWS, LANES))
    factors[TROWS : TROWS + 8, :] = jnp.ones((8, LANES), F32)
    factors[TROWS + 8 :, :] = jnp.broadcast_to(factor_c, (CROWS, LANES))
    powers = jnp.where(iota((8, LANES), 0) == 0, power_t, power_c)
    for p in range(NA):
        out[p, TROWS : TROWS + 8, :] = powers


def scale_of(top):
    top = jnp.max(jnp.max(top, axis=1, keepdims=True), axis=0, keepdims=True)
    power = jnp.ceil(jnp.log(jnp.maximum(top, 1e-30)) * (1.0 / LN2))
    return power, jnp.exp(power * -LN2) * 16384.0


def unscale(power):
    return jnp.exp(power * LN2) * (1.0 / 16384.0)


def sum_aux(slots, got, out):
    total = sum(got[p, 0:TROWS, :] * unscale(got[p, TROWS : TROWS + 1, :]) for p in range(NA))
    power, factor = scale_of(jnp.abs(total))
    out[0:TROWS, :] = total * factor
    out[TROWS:, :] = jnp.where(iota((8, LANES), 0) == 0, power, slots[...])


def all_blocks(lens, got, coefs, out, ints, words, tmat, dmat, msg, sem):
    aux, pair = lax.axis_index("aux"), lax.axis_index("pair")
    for y in range(NP):
        slots = got[pair_slot(y), TROWS : TROWS + 8, :].astype(jnp.int32)
        a, b, count = slots[1:2], slots[2:3], slots[3:4]
        third = (a * 171) >> 9
        ints[8 * y : 8 * y + 1, :] = LANES * third + 32 * (a - 3 * third)
        ints[8 * y + 1 : 8 * y + 2, :] = b >> 3
        ints[8 * y + 2 : 8 * y + 3, :] = LANES - 16 * (b & 7)
        ints[8 * y + 3 : 8 * y + 4, :] = jnp.where(iota((1, LANES), 1) < count, LANES, 0)
        ints[8 * y + 4 : 8 * y + 8, :] = slots[4:8]
    copy = pltpu.make_async_copy(ints, words, sem)
    copy.start()

    lane = iota((1, LANES), 1)
    for g in range(3):
        limit = jnp.zeros((1, LANES), jnp.int32)
        for k in range(8):
            limit = jnp.where((lane >> 4) == k, lens[8 * g + k], limit)
        kept = (lane & 15) + 16 * aux < limit
        for y in range(NP):
            slot = pair_slot(y)
            part = got[slot, TJ * g : TJ * (g + 1), :] * unscale(got[slot, TROWS : TROWS + 1, :])
            part = jnp.where(kept, part, 0.0)
            high = part.astype(BF16).astype(F32)
            tmat[TJ * y : TJ * (y + 1), LANES * g : LANES * (g + 1)] = high
            tmat[TJ * y : TJ * (y + 1), LANES * (g + 3) : LANES * (g + 4)] = part - high
    shape = (NP, TJ, NO * NI)
    y, row = iota(shape, 0), iota(shape, 1)
    fifth = row >= 4 * NO
    occ = jnp.where(fifth, 2 * (row - 4 * NO) + (y & 1), row & (NO - 1))
    j = first_column(occ, y) + jnp.where(fifth, 4, row >> 4)
    pick = jnp.where(iota(shape, 2) == NI * occ + j, 1.0, 0.0)
    pick = pick.reshape(NP * TJ, NO * NI).astype(BF16)
    ordered = dot(pick, tmat[...].astype(BF16), TN).astype(BF16)

    for p in range(NA):
        limit = jnp.zeros((1, LANES), jnp.int32)
        for k in range(3):
            limit = jnp.where((lane >> 5) == k, lens[3 * p + k], limit)
        kept = 8 * (lane & 15) + 2 * pair + ((lane >> 4) & 1) < limit
        packed = coefs[aux_slot(p)]
        packed = packed[8:] * unscale(packed[1:2])
        rows = [packed[TJ * b : TJ * (b + 1)] for b in range(3)]
        last = pltpu.roll(rows[0], 32, 1)
        last = jnp.where(lane >= 32, pltpu.roll(rows[1], 64, 1), last)
        last = jnp.where(lane >= 64, pltpu.roll(rows[2], 96, 1), last)
        coef = jnp.concatenate(rows + [last], axis=0)
        coef = jnp.where(kept, coef, 0.0).astype(BF16)
        blocks = dot(coef, ordered, TN)
        blocks = blocks[:, : 3 * LANES] + blocks[:, 3 * LANES :]
        for g in range(3):
            dmat[g, LANES * p : LANES * (p + 1), :] = blocks[:, LANES * g : LANES * (g + 1)]

    copy.wait()
    lane = iota((32, LANES), 1)
    for q in range(20):
        y = q // 5
        tile = jnp.zeros((32, LANES), F32)
        for k in range(8):
            slot = 8 * (q % 5) + k
            start = pl.multiple_of(words[8 * y, slot], 32)
            block = dmat[words[8 * y + 1, slot], pl.ds(start, 32), :]
            block = pltpu.roll(block, (words[8 * y + 2, slot] + 16 * k) & 127, 1)
            end = jnp.minimum(words[8 * y + 3, slot], 16 * (k + 1))
            tile = jnp.where((lane >= 16 * k) & (lane < end), block, tile)
        for e in range(2):
            msg[pl.ds(2 * q + e, NO, stride=40), :] = tile[NO * e : NO * (e + 1)]
    for o in range(NO):
        out[slot_of(o)] = msg[40 * o : 40 * (o + 1), :].astype(BF16)


def sum_occ(got, out, total):
    blocks = jnp.sum(got[...].astype(F32), axis=0)
    power, factor = scale_of(jnp.abs(blocks))
    total[...] = blocks * factor
    rest = jnp.where(iota((6, LANES), 0) == 0, power, 0.0)
    for y in range(NP):
        rows = total[10 * y : 10 * (y + 1), :]
        for p in range(NA):
            out[both_slot(y, p), 0:10, :] = rows
            out[both_slot(y, p), 10:16, :] = rest


def unpack(got, out, rows):
    for y in range(NP):
        for p in range(NA):
            part = got[both_slot(y, p)]
            part = part * unscale(part[10:11, :])
            for q in range(5):
                rows[q, p, 2 * y : 2 * y + 2, :] = part[2 * q : 2 * q + 2, :]
    for q in range(5):
        blocks = swap_pieces([rows[q, p] for p in range(NA)], 16)
        for k in range(8):
            out[8 * q + k] = blocks[k]


def exchange(x, axes, groups=None):
    return lax.all_to_all(x, axes, split_axis=0, concat_axis=0, tiled=True, axis_index_groups=groups)


def shape_of(shape, dtype):
    return jax.ShapeDtypeStruct(shape, dtype)


def on_device(amp_fit, amp_cabs, coef, f12_weight, ints_fit, ints_cabs, shell_len, pair_blocks, pair_count):
    weight = jnp.pad(jnp.tile(f12_weight, NC), (0, 2 * LANES - NI * NC))[None, :]

    sent = pl.pallas_call(
        pack_amps,
        out_shape=shape_of((NO, ROWS, 256), BF16),
        in_specs=[ANY] * 3,
        out_specs=vmem(1)[0],
        scratch_shapes=[
            pltpu.VMEM((NJ, NF, NO * NI), BF16),
            pltpu.VMEM((NC, NI, NO * NI), BF16),
            pltpu.VMEM((NI, 3 * LANES), BF16),
            pltpu.VMEM((24 * NC, NO * NI), F32),
            pltpu.VMEM((256, NO * NI), BF16),
            pltpu.VMEM((ROWS, 256), F32),
            pltpu.VMEM((NI, LANES), F32),
            pltpu.SemaphoreType.DMA((4,)),
        ],
        compiler_params=room(60),
    )(jnp.transpose(amp_fit, (2, 0, 1)), jnp.transpose(amp_cabs, (0, 2, 1)), coef)
    amps = exchange(sent, "occ", FROM_ROOT)

    cabs, slots = pl.pallas_call(
        join_cabs,
        out_shape=[shape_of((NC * NI, 24 * LANES), BF16), shape_of((8, LANES), F32)],
        in_specs=[SMEM] + vmem(1) + [ANY],
        out_specs=vmem(2),
        scratch_shapes=[pltpu.VMEM((NC, NI, 24 * LANES), BF16), pltpu.SemaphoreType.DMA],
        compiler_params=room(51),
        cost_estimate=pl.CostEstimate(flops=0, bytes_accessed=5_000_000, transcendentals=0),
    )(pair_count, pair_blocks.T, ints_cabs)
    sent, factors = pl.pallas_call(
        partial_t,
        out_shape=[shape_of((NA, SROWS, LANES), F32), shape_of((SROWS, LANES), F32)],
        in_specs=vmem(3) + [ANY],
        out_specs=vmem(2),
        scratch_shapes=[
            pltpu.VMEM((TJ, 5 * LANES), BF16),
            pltpu.VMEM((2 * TJ + 16, 3 * LANES), BF16),
            pltpu.VMEM((CROWS, LANES), F32),
            pltpu.VMEM((NI * NF, 24 * LANES), BF16),
            pltpu.SemaphoreType.DMA((3,)),
        ],
        compiler_params=room(49),
    )(amps, weight, cabs, jnp.transpose(ints_fit, (1, 0, 2)).reshape(NI * NF, 24 * LANES))
    shares = exchange((sent * factors[None]).astype(F16), "aux", FROM_AUX)

    sent = pl.pallas_call(
        sum_aux,
        out_shape=shape_of((TROWS + 8, LANES), F32),
        in_specs=vmem(2),
        out_specs=vmem(1)[0],
        compiler_params=PARAMS,
    )(slots, shares[:, : TROWS + 8].astype(F32))
    sent = jnp.broadcast_to(sent.astype(F16)[None], (NP, TROWS + 8, LANES))
    got = exchange(sent, "pair", FROM_PAIR).astype(F32)

    sent = pl.pallas_call(
        all_blocks,
        out_shape=shape_of((NO, 40, LANES), BF16),
        in_specs=[SMEM] + vmem(2),
        out_specs=vmem(1)[0],
        scratch_shapes=[
            pltpu.VMEM((8 * NP, LANES), jnp.int32),
            pltpu.SMEM((8 * NP, LANES), jnp.int32),
            pltpu.VMEM((NP * TJ, 6 * LANES), F32),
            pltpu.VMEM((3, 8 * LANES, LANES), F32),
            pltpu.VMEM((NO * 40, LANES), F32),
            pltpu.SemaphoreType.DMA,
        ],
        compiler_params=PARAMS,
    )(shell_len, got, shares[:, TROWS:].astype(F32))
    got = exchange(sent, "occ", FROM_ROOT)

    sent = pl.pallas_call(
        sum_occ,
        out_shape=shape_of((NP * NA, 16, LANES), F32),
        in_specs=vmem(1),
        out_specs=vmem(1)[0],
        scratch_shapes=[pltpu.VMEM((40, LANES), F32)],
        compiler_params=PARAMS,
    )(got)
    got = exchange(sent.astype(F16), ("pair", "aux"), FROM_BOTH).astype(F32)

    return pl.pallas_call(
        unpack,
        out_shape=shape_of((40, 8, LANES), F32),
        in_specs=vmem(1),
        out_specs=vmem(1)[0],
        scratch_shapes=[pltpu.VMEM((5, NA, 8, LANES), F32)],
        compiler_params=PARAMS,
    )(got)


def solution(mesh):
    placed = (
        P("aux", None, "occ"),
        P("aux", None, "occ"),
        P("occ", None),
        P("occ"),
        P("aux", "occ", None),
        P("aux", "occ", None),
        P(),
        P("pair", None),
        P("pair"),
    )
    return jax.shard_map(
        on_device, mesh=mesh, in_specs=placed, out_specs=P("pair", "occ", None), check_vma=False
    )
```

```python
import functools
import math

import jax
import jax.numpy as jnp
from jax import lax
from jax.experimental import pallas as pl
from jax.experimental.pallas import tpu as pltpu
from jax.sharding import PartitionSpec as P

F32, BF16, F16 = jnp.float32, jnp.bfloat16, jnp.float16
LANES = 128
LN2 = math.log(2.0)
NT = (((1,), (1,)), ((), ()))
TN = (((0,), (0,)), ((), ()))


def iota(shape, dim):
    return lax.broadcasted_iota(jnp.int32, shape, dim)


def dot(a, b, dims=(((1,), (0,)), ((), ()))):
    return lax.dot_general(a, b, dims, preferred_element_type=F32)


def one_hot(cond):
    return jnp.where(cond, 1.0, 0.0).astype(BF16)


def swap_pieces(xs, piece):
    lane = iota(xs[0].shape, 1)
    bit = 1
    while bit < len(xs):
        keep = ((lane // piece) & bit) == 0
        ys = list(xs)
        for k in range(len(xs)):
            if k & bit == 0:
                lo, hi = xs[k], xs[k + bit]
                ys[k] = jnp.where(keep, lo, pltpu.roll(hi, piece * bit, 1))
                ys[k + bit] = jnp.where(keep, pltpu.roll(lo, LANES - piece * bit, 1), hi)
        xs = ys
        bit *= 2
    return xs


def vmem(n):
    return [pl.BlockSpec(memory_space=pltpu.VMEM)] * n


SMEM = pl.BlockSpec(memory_space=pltpu.SMEM)
ANY = pl.BlockSpec(memory_space=pl.ANY)

def room(mib):
    return pltpu.CompilerParams(vmem_limit_bytes=mib * 1024 * 1024)


PARAMS = room(40)


NO, NI, NA, NP, NF, NC, NJ = 16, 18, 8, 4, 32, 12, 5
CQ = 16
TJ = 72
GROUP = 8 * LANES
TROWS = 3 * TJ
ROOT, STEP, BACK = 11, 7, 7
FROM_ROOT = [[(STEP * k + ROOT) % NO for k in range(NO)]]
FROM_AUX = [[(k + 5) % NA for k in range(NA)]]
FROM_PAIR = [[(k + 2) % NP for k in range(NP)]]
FROM_BOTH = [[NA * y + p for y in FROM_PAIR[0] for p in FROM_AUX[0]]]
ROWS = 24
CROWS = 216
SROWS = TROWS + 8 + CROWS


def slot_of(occ):
    return (BACK * (occ + NO - ROOT)) & (NO - 1)


def aux_slot(aux):
    return (aux + NA - 5) % NA


def pair_slot(pair):
    return (pair + NP - 2) % NP


def both_slot(pair, aux):
    return NA * pair_slot(pair) + aux_slot(aux)


def first_column(occ, pair):
    return (9 * pair + 1 - (occ & 1)) >> 1


def pack_amps(fit_hbm, cabs_hbm, coef_hbm, out, fit, cabs, coef, cab32, x, extra, piece, sems):
    aux, pair = lax.axis_index("aux"), lax.axis_index("pair")
    first_j = first_column(lax.axis_index("occ"), pair)
    fifth_j = jnp.minimum(first_j + 4, NI - 1)
    columns = pl.ds(pl.multiple_of(3 * LANES * aux, LANES), 3 * LANES)
    copies = [
        pltpu.make_async_copy(cabs_hbm, cabs, sems.at[0]),
        pltpu.make_async_copy(fit_hbm.at[pl.ds(first_j, 4)], fit.at[pl.ds(0, 4)], sems.at[1]),
        pltpu.make_async_copy(fit_hbm.at[pl.ds(fifth_j, 1)], fit.at[pl.ds(4, 1)], sems.at[2]),
        pltpu.make_async_copy(coef_hbm.at[:, columns], coef, sems.at[3]),
    ]
    for c in copies:
        c.start()
    shape = (NO, ROWS, NO * NI)
    t = iota(shape, 1)
    place = jnp.where((iota(shape, 2) == NI * ((STEP * iota(shape, 0) + ROOT) & (NO - 1)) + t) & (t < NI), 1.0, 0.0)
    place = place.reshape(NO * ROWS, NO * NI).astype(BF16)
    source, target = iota((LANES, LANES), 0), iota((LANES, LANES), 1)
    mine = source == 8 * (target & 15) + 2 * pair + ((target >> 4) & 1)
    for c in copies:
        c.wait()
    x[0 : NJ * NF, :] = fit[...].reshape(NJ * NF, NO * NI)
    for q in range(NC):
        cab32[24 * q : 24 * q + NI, :] = cabs[q].astype(F32)
    zero = jnp.zeros((CQ - NC, NO * NI), F32)
    for jj in range(NJ):
        j = fifth_j if jj == 4 else first_j + jj
        picked = [cab32[pl.ds(24 * q + j, 1), :] for q in range(NC)]
        rows = jnp.concatenate(picked + [zero], axis=0)
        x[NJ * NF + CQ * jj : NJ * NF + CQ * (jj + 1), :] = rows.astype(BF16)
    x[NJ * (NF + CQ) :, :] = jnp.zeros((256 - NJ * (NF + CQ), NO * NI), BF16)
    piece[...] = sum(
        dot(coef[:, LANES * k : LANES * (k + 1)], one_hot(mine & ((target >> 5) == k))) for k in range(3)
    )
    lane = iota((6, LANES), 1)
    third = piece[12:18, :]
    extra[...] = jnp.zeros(extra.shape, F32)
    extra[18:24, 0:LANES] = jnp.where(lane < 96, piece[0:6, :], pltpu.roll(third, 96, 1))
    extra[18:24, LANES:] = jnp.where(lane < 96, piece[6:12, :], pltpu.roll(third, 64, 1))
    extra[0:6, LANES:] = jnp.where(lane >= 112, pltpu.roll(third, 48, 1), 0.0)
    extra[6:12, LANES:] = jnp.where(lane >= 112, pltpu.roll(third, 32, 1), 0.0)
    out[...] = (dot(place, x[...], NT).reshape(NO, ROWS, 256) + extra[...][None]).astype(BF16)


def join_cabs(counts, pairs, cabs_hbm, out, slots, cabs, sem):
    copy = pltpu.make_async_copy(cabs_hbm, cabs, sem)
    copy.start()
    slots[...] = jnp.zeros(slots.shape, F32)
    slots[1:3, 0:40] = pairs[...].astype(F32)
    slots[3:4, :] = jnp.broadcast_to(counts[0].astype(F32), (1, LANES))
    copy.wait()
    for q in range(NC):
        out[NI * q : NI * (q + 1), :] = cabs[q]


def partial_t(got, weight, cabs, fit_hbm, out, factors, a_fit, a_cab, own, fit, sems):
    spans = [pl.ds(GROUP * g, GROUP) for g in range(3)]
    copies = [pltpu.make_async_copy(fit_hbm.at[:, s], fit.at[:, s], sems.at[g]) for g, s in enumerate(spans)]
    for c in copies:
        c.start()
    messages = got[...].reshape(NO * ROWS, 256)
    first = lax.axis_index("pair") & 1

    def picked(step, start):
        count = NO // step
        shape = (NI, count, NO * ROWS)
        pick = iota(shape, 2) == ROWS * slot_of(step * iota(shape, 1) + start) + iota(shape, 0)
        pick = jnp.where(pick, 1.0, 0.0).reshape(NI * count, NO * ROWS).astype(BF16)
        rows = dot(pick, messages)
        return [[rows[count * t : count * (t + 1), LANES * h : LANES * (h + 1)] for h in (0, 1)] for t in range(NI)]

    amps, fifth = picked(1, 0), picked(2, first)

    def lay(width, start, store):
        per = LANES // width
        for jj in range(NJ):
            tiles = amps if jj < 4 else fifth
            count = tiles[0][0].shape[0]
            lane = iota((count, LANES), 1)
            half, off = divmod(start + width * jj, LANES)
            for m in range(-(-NI // per)):
                tile = jnp.zeros((count, LANES), F32)
                for k in range(min(per, NI - m * per)):
                    moved = tiles[m * per + k][half]
                    if (width * k - off) % LANES:
                        moved = pltpu.roll(moved, (width * k - off) % LANES, 1)
                    tile = jnp.where((lane >= width * k) & (lane < width * (k + 1)), moved, tile)
                store[NO * jj : NO * jj + count, LANES * m : LANES * (m + 1)] = tile.astype(BF16)

    lay(NF, 0, a_fit)
    lay(CQ, NJ * NF, a_cab)
    shape = (3 * LANES, 2 * LANES)
    source, target = iota(shape, 0), iota(shape, 1)
    q = (target * 3641) >> 16
    order = one_hot((q == (source & 15)) & (target - NI * q == (source >> 4)))
    weighted = dot(a_cab[0:TJ, :], order) * weight[...]
    high = weighted.astype(BF16).astype(F32)
    gap = jnp.zeros((8, 2 * LANES), F32)
    both = jnp.concatenate([high, gap, weighted - high, gap], axis=0)
    a_cab[:, : 2 * LANES] = both.astype(BF16)

    def pack_coefficients():
        shape = (NO * NI, NO * ROWS)
        row, source = iota(shape, 0), iota(shape, 1)
        occ = (row * 3641) >> 16
        rest = row - NI * occ
        sixth = rest - jnp.where(rest >= 12, 12, jnp.where(rest >= 6, 6, 0))
        base = source - ROWS * slot_of(occ) - sixth
        main = dot(one_hot(base == 18), messages)
        spare0 = dot(one_hot(base == 0), messages[:, LANES:])
        spare1 = dot(one_hot(base == 6), messages[:, LANES:])
        shape = (NO * NI, LANES)
        lane, row = iota(shape, 1), iota(shape, 0)
        rest = row - NI * ((row * 3641) >> 16)
        third = jnp.where(lane < 32, pltpu.roll(main[:, :LANES], 32, 1), pltpu.roll(main[:, LANES:], 64, 1))
        third = jnp.where(lane < 64, third, pltpu.roll(spare0, 80, 1))
        third = jnp.where(lane < 80, third, pltpu.roll(spare1, 96, 1))
        coef = jnp.where(rest < 6, main[:, :LANES], jnp.where(rest < 12, main[:, LANES:], third))
        last = coef[3 * TJ :]
        lane = iota((TJ, LANES), 1)
        for b in range(3):
            moved = pltpu.roll(last, 96 - 32 * b, 1)
            own[TJ * b : TJ * (b + 1), :] = jnp.where(lane < 96, coef[TJ * b : TJ * (b + 1)], moved)
        for p in range(NA):
            out[p, TROWS + 8 :, :] = own[...]

    top = jnp.zeros((TJ, LANES), F32)

    for g in range(3):
        copies[g].wait()
        two = dot(a_cab[:, : NI * NC], cabs[:, spans[g]])
        total = dot(a_fit[:, : NI * NF], fit[:, spans[g]]) + two[0:TJ] + two[TJ + 8 : 2 * TJ + 8]
        if g == 0:
            pack_coefficients()
        pieces = swap_pieces([total[:, LANES * k : LANES * (k + 1)] for k in range(8)], 16)
        top = functools.reduce(jnp.maximum, [jnp.abs(piece) for piece in pieces], top)
        for k in range(8):
            out[aux_slot(k), TJ * g : TJ * (g + 1), :] = pieces[k]
    power_t, factor_t = scale_of(top)
    power_c, factor_c = scale_of(jnp.abs(own[...]))
    factors[0:TROWS, :] = jnp.broadcast_to(factor_t, (TROWS, LANES))
    factors[TROWS : TROWS + 8, :] = jnp.ones((8, LANES), F32)
    factors[TROWS + 8 :, :] = jnp.broadcast_to(factor_c, (CROWS, LANES))
    powers = jnp.where(iota((8, LANES), 0) == 0, power_t, power_c)
    for p in range(NA):
        out[p, TROWS : TROWS + 8, :] = powers


def scale_of(top):
    top = jnp.max(jnp.max(top, axis=1, keepdims=True), axis=0, keepdims=True)
    power = jnp.ceil(jnp.log(jnp.maximum(top, 1e-30)) * (1.0 / LN2))
    return power, jnp.exp(power * -LN2) * 16384.0


def unscale(power):
    return jnp.exp(power * LN2) * (1.0 / 16384.0)


def sum_aux(slots, got, out):
    total = sum(got[p, 0:TROWS, :] * unscale(got[p, TROWS : TROWS + 1, :]) for p in range(NA))
    power, factor = scale_of(jnp.abs(total))
    out[0:TROWS, :] = total * factor
    out[TROWS:, :] = jnp.where(iota((8, LANES), 0) == 0, power, slots[...])


def all_blocks(lens, got, coefs, out, ints, words, tmat, dmat, msg, sem):
    aux, pair = lax.axis_index("aux"), lax.axis_index("pair")
    for y in range(NP):
        slots = got[pair_slot(y), TROWS : TROWS + 8, :].astype(jnp.int32)
        a, b, count = slots[1:2], slots[2:3], slots[3:4]
        third = (a * 171) >> 9
        ints[8 * y : 8 * y + 1, :] = LANES * third + 32 * (a - 3 * third)
        ints[8 * y + 1 : 8 * y + 2, :] = b >> 3
        ints[8 * y + 2 : 8 * y + 3, :] = LANES - 16 * (b & 7)
        ints[8 * y + 3 : 8 * y + 4, :] = jnp.where(iota((1, LANES), 1) < count, LANES, 0)
        ints[8 * y + 4 : 8 * y + 8, :] = slots[4:8]
    copy = pltpu.make_async_copy(ints, words, sem)
    copy.start()

    lane = iota((1, LANES), 1)
    for g in range(3):
        limit = jnp.zeros((1, LANES), jnp.int32)
        for k in range(8):
            limit = jnp.where((lane >> 4) == k, lens[8 * g + k], limit)
        kept = (lane & 15) + 16 * aux < limit
        for y in range(NP):
            slot = pair_slot(y)
            part = got[slot, TJ * g : TJ * (g + 1), :] * unscale(got[slot, TROWS : TROWS + 1, :])
            part = jnp.where(kept, part, 0.0)
            high = part.astype(BF16).astype(F32)
            tmat[TJ * y : TJ * (y + 1), LANES * g : LANES * (g + 1)] = high
            tmat[TJ * y : TJ * (y + 1), LANES * (g + 3) : LANES * (g + 4)] = part - high
    shape = (NP, TJ, NO * NI)
    y, row = iota(shape, 0), iota(shape, 1)
    fifth = row >= 4 * NO
    occ = jnp.where(fifth, 2 * (row - 4 * NO) + (y & 1), row & (NO - 1))
    j = first_column(occ, y) + jnp.where(fifth, 4, row >> 4)
    pick = jnp.where(iota(shape, 2) == NI * occ + j, 1.0, 0.0)
    pick = pick.reshape(NP * TJ, NO * NI).astype(BF16)
    ordered = dot(pick, tmat[...].astype(BF16), TN).astype(BF16)

    for p in range(NA):
        limit = jnp.zeros((1, LANES), jnp.int32)
        for k in range(3):
            limit = jnp.where((lane >> 5) == k, lens[3 * p + k], limit)
        kept = 8 * (lane & 15) + 2 * pair + ((lane >> 4) & 1) < limit
        packed = coefs[aux_slot(p)]
        packed = packed[8:] * unscale(packed[1:2])
        rows = [packed[TJ * b : TJ * (b + 1)] for b in range(3)]
        last = pltpu.roll(rows[0], 32, 1)
        last = jnp.where(lane >= 32, pltpu.roll(rows[1], 64, 1), last)
        last = jnp.where(lane >= 64, pltpu.roll(rows[2], 96, 1), last)
        coef = jnp.concatenate(rows + [last], axis=0)
        coef = jnp.where(kept, coef, 0.0).astype(BF16)
        blocks = dot(coef, ordered, TN)
        blocks = blocks[:, : 3 * LANES] + blocks[:, 3 * LANES :]
        for g in range(3):
            dmat[g, LANES * p : LANES * (p + 1), :] = blocks[:, LANES * g : LANES * (g + 1)]

    copy.wait()
    lane = iota((32, LANES), 1)
    for q in range(20):
        y = q // 5
        tile = jnp.zeros((32, LANES), F32)
        for k in range(8):
            slot = 8 * (q % 5) + k
            start = pl.multiple_of(words[8 * y, slot], 32)
            block = dmat[words[8 * y + 1, slot], pl.ds(start, 32), :]
            block = pltpu.roll(block, (words[8 * y + 2, slot] + 16 * k) & 127, 1)
            end = jnp.minimum(words[8 * y + 3, slot], 16 * (k + 1))
            tile = jnp.where((lane >= 16 * k) & (lane < end), block, tile)
        for e in range(2):
            msg[pl.ds(2 * q + e, NO, stride=40), :] = tile[NO * e : NO * (e + 1)]
    for o in range(NO):
        out[slot_of(o)] = msg[40 * o : 40 * (o + 1), :].astype(BF16)


def sum_occ(got, out, total):
    blocks = jnp.sum(got[...].astype(F32), axis=0)
    power, factor = scale_of(jnp.abs(blocks))
    total[...] = blocks * factor
    rest = jnp.where(iota((6, LANES), 0) == 0, power, 0.0)
    for y in range(NP):
        rows = total[10 * y : 10 * (y + 1), :]
        for p in range(NA):
            out[both_slot(y, p), 0:10, :] = rows
            out[both_slot(y, p), 10:16, :] = rest


def unpack(got, out, rows):
    for y in range(NP):
        for p in range(NA):
            part = got[both_slot(y, p)]
            part = part * unscale(part[10:11, :])
            for q in range(5):
                rows[q, p, 2 * y : 2 * y + 2, :] = part[2 * q : 2 * q + 2, :]
    for q in range(5):
        blocks = swap_pieces([rows[q, p] for p in range(NA)], 16)
        for k in range(8):
            out[8 * q + k] = blocks[k]


def exchange(x, axes, groups=None):
    return lax.all_to_all(x, axes, split_axis=0, concat_axis=0, tiled=True, axis_index_groups=groups)


def shape_of(shape, dtype):
    return jax.ShapeDtypeStruct(shape, dtype)


def on_device(amp_fit, amp_cabs, coef, f12_weight, ints_fit, ints_cabs, shell_len, pair_blocks, pair_count):
    weight = jnp.pad(jnp.tile(f12_weight, NC), (0, 2 * LANES - NI * NC))[None, :]

    sent = pl.pallas_call(
        pack_amps,
        out_shape=shape_of((NO, ROWS, 256), BF16),
        in_specs=[ANY] * 3,
        out_specs=vmem(1)[0],
        scratch_shapes=[
            pltpu.VMEM((NJ, NF, NO * NI), BF16),
            pltpu.VMEM((NC, NI, NO * NI), BF16),
            pltpu.VMEM((NI, 3 * LANES), BF16),
            pltpu.VMEM((24 * NC, NO * NI), F32),
            pltpu.VMEM((256, NO * NI), BF16),
            pltpu.VMEM((ROWS, 256), F32),
            pltpu.VMEM((NI, LANES), F32),
            pltpu.SemaphoreType.DMA((4,)),
        ],
        compiler_params=room(60),
    )(jnp.transpose(amp_fit, (2, 0, 1)), jnp.transpose(amp_cabs, (0, 2, 1)), coef)
    amps = exchange(sent, "occ", FROM_ROOT)

    cabs, slots = pl.pallas_call(
        join_cabs,
        out_shape=[shape_of((NC * NI, 24 * LANES), BF16), shape_of((8, LANES), F32)],
        in_specs=[SMEM] + vmem(1) + [ANY],
        out_specs=vmem(2),
        scratch_shapes=[pltpu.VMEM((NC, NI, 24 * LANES), BF16), pltpu.SemaphoreType.DMA],
        compiler_params=room(51),
        cost_estimate=pl.CostEstimate(flops=0, bytes_accessed=5_000_000, transcendentals=0),
    )(pair_count, pair_blocks.T, ints_cabs)
    sent, factors = pl.pallas_call(
        partial_t,
        out_shape=[shape_of((NA, SROWS, LANES), F32), shape_of((SROWS, LANES), F32)],
        in_specs=vmem(3) + [ANY],
        out_specs=vmem(2),
        scratch_shapes=[
            pltpu.VMEM((TJ, 5 * LANES), BF16),
            pltpu.VMEM((2 * TJ + 16, 3 * LANES), BF16),
            pltpu.VMEM((CROWS, LANES), F32),
            pltpu.VMEM((NI * NF, 24 * LANES), BF16),
            pltpu.SemaphoreType.DMA((3,)),
        ],
        compiler_params=room(49),
    )(amps, weight, cabs, jnp.transpose(ints_fit, (1, 0, 2)).reshape(NI * NF, 24 * LANES))
    shares = exchange((sent * factors[None]).astype(F16), "aux", FROM_AUX)

    sent = pl.pallas_call(
        sum_aux,
        out_shape=shape_of((TROWS + 8, LANES), F32),
        in_specs=vmem(2),
        out_specs=vmem(1)[0],
        compiler_params=PARAMS,
    )(slots, shares[:, : TROWS + 8].astype(F32))
    sent = jnp.broadcast_to(sent.astype(F16)[None], (NP, TROWS + 8, LANES))
    got = exchange(sent, "pair", FROM_PAIR).astype(F32)

    sent = pl.pallas_call(
        all_blocks,
        out_shape=shape_of((NO, 40, LANES), BF16),
        in_specs=[SMEM] + vmem(2),
        out_specs=vmem(1)[0],
        scratch_shapes=[
            pltpu.VMEM((8 * NP, LANES), jnp.int32),
            pltpu.SMEM((8 * NP, LANES), jnp.int32),
            pltpu.VMEM((NP * TJ, 6 * LANES), F32),
            pltpu.VMEM((3, 8 * LANES, LANES), F32),
            pltpu.VMEM((NO * 40, LANES), F32),
            pltpu.SemaphoreType.DMA,
        ],
        compiler_params=PARAMS,
    )(shell_len, got, shares[:, TROWS:].astype(F32))
    got = exchange(sent, "occ", FROM_ROOT)

    sent = pl.pallas_call(
        sum_occ,
        out_shape=shape_of((NP * NA, 16, LANES), F32),
        in_specs=vmem(1),
        out_specs=vmem(1)[0],
        scratch_shapes=[pltpu.VMEM((40, LANES), F32)],
        compiler_params=PARAMS,
    )(got)
    got = exchange(sent.astype(F16), ("pair", "aux"), FROM_BOTH).astype(F32)

    return pl.pallas_call(
        unpack,
        out_shape=shape_of((40, 8, LANES), F32),
        in_specs=vmem(1),
        out_specs=vmem(1)[0],
        scratch_shapes=[pltpu.VMEM((5, NA, 8, LANES), F32)],
        compiler_params=PARAMS,
    )(got)


def solution(mesh):
    placed = (
        P("aux", None, "occ"),
        P("aux", None, "occ"),
        P("occ", None),
        P("occ"),
        P("aux", "occ", None),
        P("aux", "occ", None),
        P(),
        P("pair", None),
        P("pair"),
    )
    return jax.shard_map(
        on_device, mesh=mesh, in_specs=placed, out_specs=P("pair", "occ", None), check_vma=False
    )
```
